32 devices in a mesh: seq: 16 (over z, y, x), tp: 2 (over core).
Axes of the slice: x: 2, y: 2, z: 4, core: 2. Of those that a mesh axis runs over, the one named last changes fastest.
Arguments:
- tokens: bfloat16 [2048, 1152], P('seq'), may hold values from -6 to 6
- norm_gain: float32 [1152], replicated, may hold values from 0.5 to 1.5
- in_conv_weight: bfloat16 [1152, 2304], P(None, 'tp'), may hold values from -0.1875 to 0.1875
- in_gate_weight: bfloat16 [1152, 2304], P(None, 'tp'), may hold values from -0.1875 to 0.1875
- conv_weight: float32 [4, 2304], P(None, 'tp'), may hold values from -3 to 3
- conv_bias: float32 [2304], P('tp'), may hold values from -3 to 3
- scan_proj_weight: bfloat16 [2304, 104], P('tp'), may hold values from -0.125 to 0.125
- step_proj_weight: bfloat16 [72, 2304], P(None, 'tp'), may hold values from -0.75 to 0.75
- step_bias: float32 [2304], P('tp'), may hold values from -9 to -2
- decay_log: float32 [16, 2304], P(None, 'tp'), may hold values from -3 to 1
- skip_gain: float32 [2304], P('tp'), may hold values from -4 to 4
- out_weight: bfloat16 [2304, 1152], P('tp'), may hold values from -0.125 to 0.125
- segment_ids: int32 [2048], replicated, may hold values from 0 to 4, as said below
- cotangent: bfloat16 [2048, 1152], P('seq'), may hold values from -6 to 6
Outputs:
- mixed: bfloat16 [2048, 1152], P('seq')
- input_grad: float32 [2048, 1152], P('seq')
- gain_grad: float32 [1152], replicated
- in_conv_grad: float32 [1152, 2304], P('seq', 'tp')
- in_gate_grad: float32 [1152, 2304], P('seq', 'tp')
- conv_weight_grad: float32 [4, 2304], P(None, 'tp')
- conv_bias_grad: float32 [2304], P('tp')
- scan_proj_grad: float32 [2304, 104], P('tp')
- step_proj_grad: float32 [72, 2304], P(None, 'tp')
- step_bias_grad: float32 [2304], P('tp')
- decay_log_grad: float32 [16, 2304], P(None, 'tp')
- skip_grad: float32 [2304], P('tp')
- out_grad: float32 [2304, 1152], P('tp', 'seq')
The draws below stay inside these ranges and needn't reach their ends.
Inputs may be any that keep to these rules, and one draw needn't show every extreme that they name: `segment_ids`: segment ids never fall along the tokens and rise by one at each new segment; one segment begins among the first 128 tokens and ends among the last 128.
All inputs are finite; a program needn't handle non-finite values.
Results may differ from the reference program's by a relative error of at most 0.0055.
The reference program's roundings to bfloat16 on the way count: a program that leaves them out, or rounds other values in their place, can miss the bound.
Values may be sent and summed in bfloat16 or wider, within the bound.
No kernel may reach another device: no remote copies, remote signals or barrier semaphores. Data moves between devices by JAX's collectives and lax.ppermute only.
A program may use at most 192 MiB of HBM per device.

```python
import jax
import jax.numpy as jnp
from jax import lax

D = 1152
DI = 2304
STATE = 16
RANK = 72
CONVW = 4
TOK_DEV = 128
TOKENS = 2048


def draw_segment_ids(key, part):
    key = jax.random.fold_in(key, 11)
    subkeys = jax.random.split(key, 2)
    pieces = max(2, TOK_DEV // 64)
    short_end = max(pieces + 1, TOK_DEV // 4 + 1)
    head_len = jax.random.randint(subkeys[0], (), pieces, short_end)
    tail_len = jax.random.randint(subkeys[1], (), pieces, short_end)
    places = jnp.arange(TOKENS, dtype=jnp.int32)
    tail_start = TOKENS - tail_len
    head_ids = places * pieces // head_len
    tail_ids = pieces + 1 + (places - tail_start) * pieces // tail_len
    segment = jnp.where(places < head_len, head_ids, jnp.where(places < tail_start, pieces, tail_ids))
    return segment.astype(jnp.int32)


def levels(key, dims, cuts, smallest, largest):
    level, own = 1.0, jax.random.fold_in(key, 6)
    for position, parts in cuts:
        draws = jnp.exp(jax.random.uniform(jax.random.fold_in(own, position), (parts,), jnp.float32, smallest / len(cuts), largest / len(cuts)))
        level = level * jnp.repeat(draws, dims[position] // parts).reshape([-1 if axis == position else 1 for axis in range(len(dims))])
    return level


def scatter_about(rng, extent, width, bound, cuts=(), held_as=jnp.bfloat16):
    values = jax.random.normal(rng, extent, jnp.float32) * width
    if len(cuts) > 0:
        values = levels(rng, extent, cuts, -0.22, 0.18) * values
    return jnp.clip(values, min=-bound, max=bound).astype(held_as)


def setup_inputs(seed: int = 0) -> dict:
    streams_of = jax.random.split(jax.random.key(seed), 15)
    return {
        "tokens": scatter_about(streams_of[0], (TOKENS, D), 1.0, 6.0, ((0, 16),)),
        "norm_gain": jnp.clip(1.0 + 0.1 * jax.random.normal(streams_of[1], (D,), jnp.float32), 0.5, 1.5),
        "in_conv_weight": scatter_about(streams_of[2], (D, DI), D ** -0.5, 0.1875, ((1, 2),)),
        "in_gate_weight": scatter_about(streams_of[3], (D, DI), D ** -0.5, 0.1875, ((1, 2),)),
        "conv_weight": scatter_about(streams_of[4], (CONVW, DI), CONVW ** -0.5, 3.0, ((1, 2),), jnp.float32),
        "conv_bias": scatter_about(streams_of[5], (DI,), 0.5, 3.0, ((0, 2),), jnp.float32),
        "scan_proj_weight": scatter_about(streams_of[6], (DI, RANK + 2 * STATE), DI ** -0.5, 0.125, ((0, 2),)),
        "step_proj_weight": scatter_about(streams_of[7], (RANK, DI), RANK ** -0.5, 0.75, ((1, 2),)),
        "step_bias": jnp.clip(-9.0 + 7.0 * jax.random.uniform(streams_of[8], (DI,), jnp.float32) ** levels(streams_of[8], (DI,), ((0, 2),), -0.2, 0.2), -9.0, -2.0),
        "decay_log": jnp.clip(-3.0 + 4.0 * jax.random.uniform(streams_of[9], (STATE, DI), jnp.float32) ** levels(streams_of[9], (STATE, DI), ((1, 2),), -0.2, 0.2), -3.0, 1.0),
        "skip_gain": scatter_about(streams_of[10], (DI,), 1.0, 4.0, ((0, 2),), jnp.float32),
        "out_weight": scatter_about(streams_of[11], (DI, D), DI ** -0.5, 0.125, ((0, 2),)),
        "segment_ids": draw_segment_ids(jax.random.fold_in(streams_of[14], 71), 0),
        "cotangent": scatter_about(streams_of[13], (TOKENS, D), 1.0, 6.0, ((0, 16),)),
    }


NORM_EPS = 1e-05

@jax.custom_vjp
def low(v):
    return lax.optimization_barrier(v.astype(jnp.bfloat16)).astype(jnp.float32)

@jax.custom_vjp
def low_back(v):
    return v

def low_keep(v):
    return (low(v), None)

def low_pass(kept, grad):
    return (grad,)

def back_keep(v):
    return (v, None)

def back_low(kept, grad):
    return (low(grad),)
low.defvjp(low_keep, low_pass)
low_back.defvjp(back_keep, back_low)

def scan_tokens(step_size, in_coef, out_coef, conv_out, rate, same_prev):
    count_all = step_size.shape[0]
    blocks = count_all // TOK_DEV

    def block_fn(state, pieces):

        def token_step(hidden, row):
            step_row, in_row, out_row, conv_row, same_row = row
            hidden = jnp.exp(step_row[None, :] * rate) * same_row * hidden + in_row[:, None] * (step_row * conv_row)[None, :]
            return (hidden, lax.optimization_barrier(jnp.sum(hidden * out_row[:, None], axis=0)))
        return lax.scan(token_step, state, pieces)

    def shaped(array):
        return array.reshape((blocks, TOK_DEV) + array.shape[1:])
    start_state = jnp.zeros(rate.shape, jnp.float32)
    _, outputs = lax.scan(jax.checkpoint(block_fn), start_state, (shaped(step_size), shaped(in_coef), shaped(out_coef), shaped(conv_out), shaped(same_prev)))
    return outputs.reshape(count_all, rate.shape[1])

def reference(tokens, norm_gain, in_conv_weight, in_gate_weight, conv_weight, conv_bias, scan_proj_weight, step_proj_weight, step_bias, decay_log, skip_gain, out_weight, segment_ids, cotangent):
    kernel = conv_weight.shape[0]
    length = segment_ids.shape[0]
    rank_width = step_proj_weight.shape[0]
    states = decay_log.shape[0]
    padded_ids = jnp.concatenate([jnp.full((kernel,), -1, jnp.int32), segment_ids.astype(jnp.int32)])
    conv_masks = [(segment_ids == padded_ids[offset + 1:offset + 1 + length]).astype(jnp.float32)[:, None] for offset in range(kernel)]
    same_prev = (segment_ids == padded_ids[kernel - 1:kernel - 1 + length]).astype(jnp.float32)

    def forward(tok, gain, w_conv, w_gate, taps, tap_bias, w_scan, w_step, bias_step, log_decay, skip, w_out):
        inv_rms = lax.rsqrt(lax.optimization_barrier(jnp.mean(tok * tok, axis=1, keepdims=True)) + NORM_EPS)
        normed = low(tok * inv_rms * gain)
        conv_in = low(low_back(jnp.dot(normed, w_conv, precision=lax.Precision.HIGHEST)))
        gate_in = low_back(jnp.dot(normed, w_gate, precision=lax.Precision.HIGHEST))
        conv_ext = jnp.concatenate([jnp.zeros((kernel - 1, conv_in.shape[1]), jnp.float32), conv_in], axis=0)
        conv_pre = tap_bias + sum((taps[offset] * conv_ext[offset:offset + length] * conv_masks[offset] for offset in range(kernel)))
        conv_out = low(jax.nn.silu(conv_pre))
        projected = low_back(jnp.dot(conv_out, w_scan, precision=lax.Precision.HIGHEST))
        step_low = low(projected[:, :rank_width])
        in_coef = projected[:, rank_width:rank_width + states]
        out_coef = projected[:, rank_width + states:]
        step_size = jax.nn.softplus(low_back(jnp.dot(step_low, w_step, precision=lax.Precision.HIGHEST)) + bias_step)
        rate = -jnp.exp(log_decay)
        scan_out = scan_tokens(step_size, in_coef, out_coef, conv_out, rate, same_prev) + skip * conv_out
        gated = low(scan_out * jax.nn.silu(gate_in))
        branch = low_back(jnp.dot(gated, w_out, precision=lax.Precision.HIGHEST))
        return tok + branch
    inputs = (tokens.astype(jnp.float32), norm_gain, in_conv_weight.astype(jnp.float32), in_gate_weight.astype(jnp.float32), conv_weight, conv_bias, scan_proj_weight.astype(jnp.float32), step_proj_weight.astype(jnp.float32), step_bias, decay_log, skip_gain, out_weight.astype(jnp.float32))
    result, pull = jax.vjp(forward, *inputs)
    gradients = pull(cotangent.astype(jnp.float32))
    return (result.astype(jnp.bfloat16), gradients[0], gradients[1], gradients[2], gradients[3], gradients[4], gradients[5], gradients[6], gradients[7], gradients[8], gradients[9], gradients[10], gradients[11])
```

```python
import functools

import jax
import jax.numpy as jnp
from jax import lax
from jax.experimental import pallas as pl
from jax.experimental.pallas import tpu as pltpu
from jax.sharding import PartitionSpec as P

NORM_EPS = 1e-05
LANES = 128
CHUNKS = 8
LOG2E = 1.4426950408889634
LN2 = 0.6931471805599453
FAR = 1e30
VMEM = 48 * 1024 * 1024


def sigmoid(value):
    return 1.0 / (1.0 + jnp.exp(-value))


def silu_grad(value):
    sigma = sigmoid(value)
    return sigma * (1.0 + value * (1.0 - sigma))


def softplus(value):
    small = jnp.exp(-jnp.abs(value))
    series = small * (1.0 - small * (0.5 - small * (1.0 / 3.0 - small * 0.25)))
    return jnp.maximum(value, 0.0) + jnp.where(small < 0.01, series, jnp.log(1.0 + small))


def dot(first, second, contract):
    return lax.dot_general(
        first, second, (contract, ((), ())), preferred_element_type=jnp.float32
    )


def strided(number, length):
    return pl.ds(number, CHUNKS, stride=length // CHUNKS)


def spread(proj_ref, first, table_ref, states, length):
    for place in range(length // CHUNKS):
        rows = proj_ref[strided(place, length), :]
        for state in range(states):
            column = rows[:, first + state : first + state + 1]
            start = (place * states + state) * CHUNKS
            table_ref[start : start + CHUNKS, :] = jnp.broadcast_to(column, (CHUNKS, LANES))


def tile(ref, place, state, states):
    start = (place * states + state) * CHUNKS
    return ref[start : start + CHUNKS, :]


def ends_kernel(
    rank, states,
    own_ref, peer_ref, weight_ref, bias_ref, decay_ref, conv_ref, gg_ref, gate_ref, same_ref,
    step_ref, ends_ref, seeds_ref, totals_ref,
    proj_ref, in_ref, out_ref, long_ref, drive_ref, source_ref,
):
    length = conv_ref.shape[0]
    places = length // CHUNKS

    @pl.when(pl.program_id(0) == 0)
    def _():
        proj_ref[...] = own_ref[...] + peer_ref[...]
        spread(proj_ref, rank, in_ref, states, length)
        spread(proj_ref, rank + states, out_ref, states, length)

    low = proj_ref[:, :rank].astype(jnp.bfloat16)
    step_pre = dot(low, weight_ref[...], ((1,), (0,))) + bias_ref[...]
    step_ref[...] = step_pre
    step = softplus(step_pre)
    long_ref[...] = jnp.where(same_ref[...] > 0.0, step, FAR)
    drive_ref[...] = step * conv_ref[...].astype(jnp.float32)
    gate = gate_ref[...]
    source_ref[...] = gg_ref[...] * gate * sigmoid(gate)
    rate2 = -jnp.exp(decay_ref[...]) * LOG2E
    rates = [jnp.broadcast_to(rate2[n : n + 1, :], (CHUNKS, LANES)) for n in range(states)]
    hidden = [None] * states
    sums = None
    for place in range(places):
        long = long_ref[strided(place, length), :]
        drive = drive_ref[strided(place, length), :]
        sums = long if place == 0 else sums + long
        for n in range(states):
            term = tile(in_ref, place, n, states) * drive
            hidden[n] = term if place == 0 else jnp.exp2(long * rates[n]) * hidden[n] + term
    for n in range(states):
        ends_ref[n * CHUNKS : (n + 1) * CHUNKS, :] = hidden[n]
    back = [None] * states
    for place in reversed(range(places)):
        long = long_ref[strided(place, length), :]
        source = source_ref[strided(place, length), :]
        for n in range(states):
            term = tile(out_ref, place, n, states) * source
            term = term if place == places - 1 else back[n] + term
            back[n] = jnp.exp2(long * rates[n]) * term
    for n in range(states):
        seeds_ref[n * CHUNKS : (n + 1) * CHUNKS, :] = back[n]
    decays = [jnp.exp2(rate2 * sums[c : c + 1, :]) for c in range(CHUNKS)]
    end = jnp.zeros((states, LANES), jnp.float32)
    seed = jnp.zeros((states, LANES), jnp.float32)
    for c in range(CHUNKS):
        end = decays[c] * end + ends_ref[pl.ds(c, states, stride=CHUNKS), :]
    for c in reversed(range(CHUNKS)):
        seed = decays[c] * seed + seeds_ref[pl.ds(c, states, stride=CHUNKS), :]
    totals_ref[:states, :] = end
    totals_ref[states : 2 * states, :] = seed
    total = jnp.sum(sums, axis=0, keepdims=True)
    totals_ref[2 * states :, :] = jnp.broadcast_to(total, (8, LANES))


def scan_kernel(
    rank, states, groups,
    own_ref, peer_ref, weight_ref, decay_ref, skip_ref, conv_ref, gg_ref, gate_ref, same_ref,
    step_ref, ends_ref, seeds_ref, carry_ref, incoming_ref,
    pack_ref, gconv_ref, gproj_ref,
    proj_ref, in_ref, out_ref, long_ref, true_ref, drive_ref, source_ref,
    start_ref, last_ref, hidden_ref, in_acc, out_acc, low_acc, scan_ref, gstep_ref, mix_ref,
):
    length = conv_ref.shape[0]
    places = length // CHUNKS
    index = pl.program_id(0)

    @pl.when(index == 0)
    def _():
        proj_ref[...] = own_ref[...] + peer_ref[...]
        spread(proj_ref, rank, in_ref, states, length)
        spread(proj_ref, rank + states, out_ref, states, length)
        in_acc[...] = jnp.zeros_like(in_acc)
        out_acc[...] = jnp.zeros_like(out_acc)
        low_acc[...] = jnp.zeros_like(low_acc)

    step_pre = step_ref[...]
    step = softplus(step_pre)
    conv = conv_ref[...].astype(jnp.float32)
    gate = gate_ref[...]
    gg = gg_ref[...]
    sigma = sigmoid(gate)
    act = gate * sigma
    source_all = gg * act
    true_ref[...] = step
    long_ref[...] = jnp.where(same_ref[...] > 0.0, step, FAR)
    drive_ref[...] = step * conv
    source_ref[...] = source_all
    rate = -jnp.exp(decay_ref[...])
    rate2 = rate * LOG2E
    rates = [jnp.broadcast_to(rate2[n : n + 1, :], (CHUNKS, LANES)) for n in range(states)]
    sums = long_ref[strided(0, length), :]
    for place in range(1, places):
        sums = sums + long_ref[strided(place, length), :]
    decays = [jnp.exp2(rate2 * sums[c : c + 1, :]) for c in range(CHUNKS)]
    state = carry_ref[...]
    for c in range(CHUNKS):
        start_ref[pl.ds(c, states, stride=CHUNKS), :] = state
        state = decays[c] * state + ends_ref[pl.ds(c, states, stride=CHUNKS), :]
    state = incoming_ref[...]
    for c in reversed(range(CHUNKS)):
        last_ref[pl.ds(c, states, stride=CHUNKS), :] = state
        state = decays[c] * state + seeds_ref[pl.ds(c, states, stride=CHUNKS), :]

    hidden = [start_ref[n * CHUNKS : (n + 1) * CHUNKS, :] for n in range(states)]
    for place in range(places):
        long = long_ref[strided(place, length), :]
        drive = drive_ref[strided(place, length), :]
        source = source_ref[strided(place, length), :]
        rows = slice(place * CHUNKS, (place + 1) * CHUNKS)
        scan = None
        for n in range(states):
            lanes = slice(n * LANES, (n + 1) * LANES)
            value = jnp.exp2(long * rates[n]) * hidden[n] + tile(in_ref, place, n, states) * drive
            hidden[n] = value
            if place < places - 1:
                hidden_ref[(place * states + n) * CHUNKS : (place * states + n + 1) * CHUNKS, :] = value
            part = tile(out_ref, place, n, states) * value
            scan = part if n == 0 else scan + part
            out_acc[rows, lanes] += source * value
        scan_ref[strided(place, length), :] = scan

    back = [last_ref[n * CHUNKS : (n + 1) * CHUNKS, :] for n in range(states)]
    logs = [None] * states
    for place in reversed(range(places)):
        long = long_ref[strided(place, length), :]
        true = true_ref[strided(place, length), :]
        drive = drive_ref[strided(place, length), :]
        source = source_ref[strided(place, length), :]
        rows = slice(place * CHUNKS, (place + 1) * CHUNKS)
        gstep = None
        mixed = None
        for n in range(states):
            lanes = slice(n * LANES, (n + 1) * LANES)
            grad = back[n] + tile(out_ref, place, n, states) * source
            previous = (
                start_ref[n * CHUNKS : (n + 1) * CHUNKS, :] if place == 0
                else tile(hidden_ref, place - 1, n, states)
            )
            back[n] = jnp.exp2(long * rates[n]) * grad
            log = back[n] * previous
            part = log * true
            logs[n] = part if logs[n] is None else logs[n] + part
            part = log * rates[n]
            gstep = part if n == 0 else gstep + part
            part = grad * tile(in_ref, place, n, states)
            mixed = part if n == 0 else mixed + part
            in_acc[rows, lanes] += grad * drive
        gstep_ref[strided(place, length), :] = gstep
        mix_ref[strided(place, length), :] = mixed

    scan_out = scan_ref[...] + skip_ref[...] * conv
    gated = scan_out * act
    ggate = gg * scan_out * sigma * (1.0 + gate * (1.0 - sigma))
    mix = mix_ref[...]
    gconv_ref[...] = source_all * skip_ref[...] + mix * step
    gpre = (gstep_ref[...] * LN2 + mix * conv) * sigmoid(step_pre)
    gpre_low = gpre.astype(jnp.bfloat16)
    low_acc[:, :rank] += dot(gpre_low, weight_ref[...], ((1,), (1,)))
    low = proj_ref[...].astype(jnp.bfloat16)
    step_part = dot(gpre_low, low, ((0,), (0,)))
    row_number = lax.broadcasted_iota(jnp.int32, (LANES, LANES), 0)
    table = jnp.where(row_number == rank + states, jnp.sum(gpre, axis=0, keepdims=True), 0.0)
    table = jnp.where(
        row_number == rank + states + 1, jnp.sum(source_all * conv, axis=0, keepdims=True), table
    )
    for n in range(states):
        value = jnp.sum(logs[n], axis=0, keepdims=True) * rate[n : n + 1, :]
        table = jnp.where(row_number == rank + n, value, table)
    lane_number = lax.broadcasted_iota(jnp.int32, (LANES, LANES), 1)
    small = jnp.where(lane_number < rank, step_part, table.T)
    pack_ref[:, :LANES] = gated.T.astype(jnp.bfloat16)
    pack_ref[:, LANES : 2 * LANES] = ggate.T.astype(jnp.bfloat16)
    pack_ref[:, 2 * LANES :] = small.astype(jnp.bfloat16)

    @pl.when(index == groups - 1)
    def _():
        wide = states * LANES
        source_state = lax.broadcasted_iota(jnp.int32, (wide, LANES), 0) // LANES
        column = lax.broadcasted_iota(jnp.int32, (wide, LANES), 1)
        total = jnp.zeros((length, LANES), jnp.float32)
        for acc, first in ((in_acc, rank), (out_acc, rank + states)):
            pick = jnp.where(source_state + first == column, 1.0, 0.0).astype(jnp.bfloat16)
            value = acc[...]
            high = value.astype(jnp.bfloat16)
            rest = (value - high.astype(jnp.float32)).astype(jnp.bfloat16)
            total = total + dot(high, pick, ((1,), (0,))) + dot(rest, pick, ((1,), (0,)))
        scan_ref[...] = total
        for place in range(places):
            mix_ref[strided(place, length), :] = scan_ref[place * CHUNKS : (place + 1) * CHUNKS, :]
        gproj_ref[...] = mix_ref[...] + low_acc[...]


def column_block(rows, width=LANES):
    return pl.BlockSpec((rows, width), lambda g: (0, g))


def row_block(width):
    return pl.BlockSpec((LANES, width), lambda g: (g, 0))


def whole(*shape):
    return pl.BlockSpec(shape, lambda g: (0,) * len(shape))


def run_ends(own, peer, weight, bias, decay_log, conv, gg, gate, same):
    length, width = conv.shape
    rank, states = weight.shape[0], decay_log.shape[0]
    tall = length // CHUNKS * states * CHUNKS
    f32 = jnp.float32
    return pl.pallas_call(
        functools.partial(ends_kernel, rank, states),
        grid=(width // LANES,),
        in_specs=[
            whole(length, LANES), whole(length, LANES), column_block(rank), column_block(1),
            column_block(states), column_block(length), column_block(length), column_block(length),
            whole(length, 1),
        ],
        out_specs=[
            column_block(length), column_block(states * CHUNKS), column_block(states * CHUNKS),
            column_block(2 * states + 8),
        ],
        out_shape=[
            jax.ShapeDtypeStruct((length, width), f32),
            jax.ShapeDtypeStruct((states * CHUNKS, width), f32),
            jax.ShapeDtypeStruct((states * CHUNKS, width), f32),
            jax.ShapeDtypeStruct((2 * states + 8, width), f32),
        ],
        scratch_shapes=[
            pltpu.VMEM((length, LANES), f32), pltpu.VMEM((tall, LANES), f32),
            pltpu.VMEM((tall, LANES), f32), pltpu.VMEM((length, LANES), f32),
            pltpu.VMEM((length, LANES), f32), pltpu.VMEM((length, LANES), f32),
        ],
        compiler_params=pltpu.CompilerParams(vmem_limit_bytes=VMEM),
        name="ends",
    )(own, peer, weight, bias, decay_log, conv, gg, gate, same)


def run_scan(own, peer, weight, decay_log, skip, conv, gg, gate, same, step, ends, seeds, carry, incoming):
    length, width = conv.shape
    rank, states = weight.shape[0], decay_log.shape[0]
    places = length // CHUNKS
    tall = places * states * CHUNKS
    f32 = jnp.float32
    block = pltpu.VMEM((length, LANES), f32)
    return pl.pallas_call(
        functools.partial(scan_kernel, rank, states, width // LANES),
        grid=(width // LANES,),
        in_specs=[
            whole(length, LANES), whole(length, LANES), column_block(rank), column_block(states),
            column_block(1), column_block(length), column_block(length), column_block(length),
            whole(length, 1), column_block(length), column_block(states * CHUNKS),
            column_block(states * CHUNKS), column_block(states), column_block(states),
        ],
        out_specs=[row_block(3 * LANES), column_block(length), whole(length, LANES)],
        out_shape=[
            jax.ShapeDtypeStruct((width, 3 * LANES), jnp.bfloat16),
            jax.ShapeDtypeStruct((length, width), f32),
            jax.ShapeDtypeStruct((length, LANES), f32),
        ],
        scratch_shapes=[
            block, pltpu.VMEM((tall, LANES), f32), pltpu.VMEM((tall, LANES), f32),
            block, block, block, block,
            pltpu.VMEM((states * CHUNKS, LANES), f32), pltpu.VMEM((states * CHUNKS, LANES), f32),
            pltpu.VMEM((tall, LANES), f32),
            pltpu.VMEM((length, states * LANES), f32), pltpu.VMEM((length, states * LANES), f32),
            block, block, block, block,
        ],
        compiler_params=pltpu.CompilerParams(vmem_limit_bytes=VMEM),
        name="scan",
    )(own, peer, weight, decay_log, skip, conv, gg, gate, same, step, ends, seeds, carry, incoming)


def from_behind(block, axis, distance):
    devices = range(lax.axis_size(axis))
    route = [(i - distance, i) for i in devices if i - distance in devices]
    return lax.ppermute(block, axis, route)


def swap(block):
    return lax.ppermute(block, "tp", [(0, 1), (1, 0)])


def levels(members):
    found, stride = [], 1
    while stride < members:
        left = members // stride
        radix = 4 if left % 4 == 0 else 2 if left % 2 == 0 else left
        found.append((stride, radix))
        stride *= radix
    return found


def exchange(totals, rate2, states):
    members = lax.axis_size("seq")
    device = lax.axis_index("seq")
    end, seed, sums = totals[:states], totals[states : 2 * states], totals[2 * states : 2 * states + 1]
    carry = jnp.zeros_like(end)
    incoming = jnp.zeros_like(end)
    before = jnp.zeros_like(sums)
    behind = jnp.zeros_like(sums)
    for stride, radix in levels(members):
        digit = device // stride % radix
        payload = jnp.concatenate([end, seed, sums], axis=0)
        got = [payload]
        for hop in range(1, radix):
            route = []
            for i in range(members):
                own = i // stride % radix
                to = own ^ hop if radix in (2, 4) else (own + hop) % radix
                route.append((i, i + (to - own) * stride))
            got.append(lax.ppermute(payload, "seq", route))
        parts = []
        for number in range(radix):
            hop = (digit ^ number) if radix in (2, 4) else (digit - number) % radix
            value = got[0]
            for other in range(1, radix):
                value = jnp.where(hop == other, got[other], value)
            parts.append((value[:states], value[states : 2 * states], value[2 * states :]))
        near_carry, near_before = jnp.zeros_like(end), jnp.zeros_like(sums)
        end, sums_all = jnp.zeros_like(end), jnp.zeros_like(sums)
        for number in range(radix):
            part_end, _, part_sum = parts[number]
            decay = jnp.exp2(rate2 * part_sum)
            end = decay * end + part_end
            near_carry = jnp.where(number < digit, decay * near_carry + part_end, near_carry)
            near_before = jnp.where(number < digit, near_before + part_sum, near_before)
            sums_all = sums_all + part_sum
        near_incoming, near_behind, seed = jnp.zeros_like(seed), jnp.zeros_like(sums), jnp.zeros_like(seed)
        for number in reversed(range(radix)):
            _, part_seed, part_sum = parts[number]
            decay = jnp.exp2(rate2 * part_sum)
            seed = decay * seed + part_seed
            near_incoming = jnp.where(number > digit, decay * near_incoming + part_seed, near_incoming)
            near_behind = jnp.where(number > digit, near_behind + part_sum, near_behind)
        carry = carry + jnp.exp2(rate2 * before) * near_carry
        incoming = incoming + jnp.exp2(rate2 * behind) * near_incoming
        before, behind, sums = before + near_before, behind + near_behind, sums_all
    return carry, incoming


def shards(
    tokens, norm_gain, in_conv_weight, in_gate_weight, conv_weight, conv_bias, scan_proj_weight,
    step_proj_weight, step_bias, decay_log, skip_gain, out_weight, segment_ids, cotangent,
):
    f32, bf16 = jnp.float32, jnp.bfloat16
    length, model = tokens.shape
    rank = step_proj_weight.shape[0]
    states = decay_log.shape[0]
    kernel = conv_weight.shape[0]
    width = conv_weight.shape[1]
    members = lax.axis_size("seq")
    device = lax.axis_index("seq")
    core = lax.axis_index("tp")
    rows = width // members
    half = model // 2
    padded_ids = jnp.concatenate([jnp.full((kernel,), -1, jnp.int32), segment_ids])
    near_ids = lax.dynamic_slice_in_dim(padded_ids, device * length, length + kernel)
    own_ids = near_ids[kernel:]
    conv_masks = [
        (own_ids == near_ids[offset + 1 : offset + 1 + length]).astype(f32)[:, None]
        for offset in range(kernel)
    ]
    same_prev = conv_masks[kernel - 2]

    tok_float = tokens.astype(f32)
    inv_rms = lax.rsqrt(jnp.mean(tok_float * tok_float, axis=1, keepdims=True) + NORM_EPS)
    normed = (tok_float * inv_rms * norm_gain).astype(bf16)
    factor = jnp.where(
        core == 0,
        jnp.concatenate([normed[:, :half], cotangent[:, :half]], axis=1),
        jnp.concatenate([normed[:, half:], cotangent[:, half:]], axis=1),
    )
    factors = lax.all_gather(factor, "seq", axis=0, tiled=True)
    conv_in = dot(normed, in_conv_weight, ((1,), (0,))).astype(bf16)
    left_rim = from_behind(conv_in[length - (kernel - 1) :], "seq", 1)
    gate_in = dot(normed, in_gate_weight, ((1,), (0,)))
    grad_gated = dot(cotangent, out_weight, ((1,), (1,)))
    conv_ext = jnp.concatenate([left_rim, conv_in], axis=0).astype(f32)
    conv_pre = conv_bias + sum(
        conv_weight[offset] * conv_ext[offset : offset + length] * conv_masks[offset]
        for offset in range(kernel)
    )
    conv_out = (conv_pre * sigmoid(conv_pre)).astype(bf16)
    own = jnp.pad(
        dot(conv_out, scan_proj_weight, ((1,), (0,))), ((0, 0), (0, LANES - rank - 2 * states))
    )
    peer = swap(own)
    step_pre, ends, seeds, totals = run_ends(
        own, peer, step_proj_weight, step_bias[None], decay_log, conv_out, grad_gated, gate_in, same_prev
    )
    rate2 = -jnp.exp(decay_log) * LOG2E
    carry, incoming = exchange(totals, rate2, states)
    pack, grad_conv, low_own = run_scan(
        own, peer, step_proj_weight, decay_log, skip_gain[None], conv_out, grad_gated, gate_in,
        same_prev, step_pre, ends, seeds, carry, incoming,
    )
    first_got = lax.all_to_all(pack.reshape(members, rows, 3 * LANES), "seq", 0, 0, tiled=True)
    low_peer = swap(low_own)
    gated_t, ggate_t = pack[:, :LANES], pack[:, LANES : 2 * LANES]
    branch_own = dot(gated_t, out_weight, ((0,), (0,)))
    branch = branch_own + swap(branch_own)
    mixed_out = (tok_float + branch).astype(bf16)

    grad_proj = (low_own + low_peer).astype(bf16)[:, : rank + 2 * states]
    scan_proj_part = dot(conv_out, grad_proj, ((0,), (0,)))
    grad_conv = grad_conv + dot(grad_proj, scan_proj_weight, ((1,), (1,)))
    grad_cpre = grad_conv * silu_grad(conv_pre)
    conv_bias_part = jnp.sum(grad_cpre, axis=0)
    conv_weight_part = [
        jnp.sum(grad_cpre * conv_ext[offset : offset + length] * conv_masks[offset], axis=0)
        for offset in range(kernel)
    ]
    grad_ext = sum(
        jnp.pad(
            grad_cpre * conv_weight[offset] * conv_masks[offset],
            ((offset, kernel - 1 - offset), (0, 0)),
        )
        for offset in range(kernel)
    )
    rim_back = from_behind(grad_ext[: kernel - 1], "seq", -1)
    grad_conv_in = grad_ext[kernel - 1 :] + jnp.concatenate(
        [jnp.zeros((length - (kernel - 1), width), f32), rim_back], axis=0
    )
    grad_conv_low = grad_conv_in.astype(bf16)
    normed_own = dot(grad_conv_low, in_conv_weight, ((1,), (1,))) + dot(
        ggate_t, in_gate_weight, ((0,), (1,))
    )
    gain_part = jnp.sum(normed_own * tok_float * inv_rms, axis=0)
    small = jnp.concatenate(
        [scan_proj_part, jnp.stack(conv_weight_part + [conv_bias_part, gain_part], axis=1)], axis=1
    )
    small = jnp.pad(small, ((0, 0), (0, LANES - small.shape[1]))).astype(bf16)
    second = jnp.concatenate([grad_conv_low.T, small], axis=1)
    second_got = lax.all_to_all(second.reshape(members, rows, 2 * LANES), "seq", 0, 0, tiled=True)

    grad_normed = normed_own + swap(normed_own)
    scaled_grad = grad_normed * norm_gain
    input_grad = (
        cotangent.astype(f32)
        + inv_rms * scaled_grad
        - tok_float * inv_rms * inv_rms * inv_rms
        * jnp.mean(scaled_grad * tok_float, axis=1, keepdims=True)
    )

    late = jnp.stack([first_got[:, :, :LANES], first_got[:, :, LANES : 2 * LANES], second_got[:, :, :LANES]])
    late_peer = swap(late)
    normed_all = factors[:, :half].reshape(members, length, half)
    cot_all = factors[:, half:].reshape(members, length, half)

    def product(values, factor_all):
        return lax.dot_general(
            values, factor_all, (((0, 2), (0, 1)), ((), ())), preferred_element_type=f32
        )

    def products(values):
        return jnp.stack(
            [product(values[0], cot_all), product(values[1], normed_all), product(values[2], normed_all)]
        )

    kept = products(late)
    given = swap(products(late_peer))
    full = jnp.where(
        core == 0, jnp.concatenate([kept, given], axis=2), jnp.concatenate([given, kept], axis=2)
    )
    sums_first = jnp.sum(first_got[:, :, 2 * LANES :].astype(f32), axis=0)
    sums_second = jnp.sum(second_got[:, :, LANES:].astype(f32), axis=0)
    cols = model // members
    out_blocks = full.reshape(3, rows, members, cols).transpose(2, 1, 0, 3).reshape(members, rows, 3 * cols)
    final = lax.all_to_all(out_blocks, "seq", 0, 0, tiled=True).reshape(width, 3, cols)
    sums = jnp.concatenate([sums_first, sums_second], axis=1).astype(bf16)
    sums = lax.all_to_all(
        jnp.broadcast_to(sums[None], (members, rows, 2 * LANES)), "seq", 0, 0, tiled=True
    ).reshape(width, 2 * LANES).astype(f32)
    out_grad = final[:, 0]
    in_gate_grad = final[:, 1].T
    in_conv_grad = final[:, 2].T
    step_proj_grad = sums[:, :rank].T
    decay_log_grad = sums[:, rank : rank + states].T
    step_bias_grad = sums[:, rank + states]
    skip_grad = sums[:, rank + states + 1]
    base = LANES
    scan_width = rank + 2 * states
    scan_proj_grad = sums[:, base : base + scan_width]
    conv_weight_grad = sums[:, base + scan_width : base + scan_width + kernel].T
    conv_bias_grad = sums[:, base + scan_width + kernel]
    gain_grad = sums[:, base + scan_width + kernel + 1]
    gain_grad = gain_grad + swap(gain_grad)
    return (
        mixed_out, input_grad, gain_grad, in_conv_grad, in_gate_grad, conv_weight_grad,
        conv_bias_grad, scan_proj_grad, step_proj_grad, step_bias_grad, decay_log_grad, skip_grad,
        out_grad,
    )


def solution(mesh):
    in_specs = (
        P("seq", None), P(), P(None, "tp"), P(None, "tp"), P(None, "tp"), P("tp"), P("tp", None),
        P(None, "tp"), P("tp"), P(None, "tp"), P("tp"), P("tp", None), P(), P("seq", None),
    )
    out_specs = (
        P("seq", None), P("seq", None), P(), P("seq", "tp"), P("seq", "tp"), P(None, "tp"), P("tp"),
        P("tp", None), P(None, "tp"), P("tp"), P(None, "tp"), P("tp"), P("tp", "seq"),
    )
    return jax.shard_map(shards, mesh=mesh, in_specs=in_specs, out_specs=out_specs, check_vma=False)
```

```python
import functools

import jax
import jax.numpy as jnp
from jax import lax
from jax.experimental import pallas as pl
from jax.experimental.pallas import tpu as pltpu
from jax.sharding import PartitionSpec as P

NORM_EPS = 1e-05
LANES = 128
PLANE = 4
CHUNKS = 8
LOG2E = 1.4426950408889634
LN2 = 0.6931471805599453
FAR = 1e30
MIB = 1024 * 1024
TAP_BIAS, STEP_BIAS, SKIP, GAIN = 0, 1, 2, 3


def sigmoid(value):
    return 1.0 / (1.0 + jnp.exp(-value))


def silu_grad(value):
    sigma = sigmoid(value)
    return sigma * (1.0 + value * (1.0 - sigma))


def softplus(value):
    small = jnp.exp(-jnp.abs(value))
    series = small * (1.0 - small * (0.5 - small * (1.0 / 3.0 - small * 0.25)))
    return jnp.maximum(value, 0.0) + jnp.where(small < 0.01, series, jnp.log(1.0 + small))


def dot(first, second, contract):
    return lax.dot_general(
        first, second, (contract, ((), ())), preferred_element_type=jnp.float32
    )


def strided(number, length):
    return pl.ds(number, CHUNKS, stride=length // CHUNKS)


def spread(proj_ref, first, table_ref, states, length):
    for place in range(length // CHUNKS):
        rows = proj_ref[strided(place, length), :]
        for state in range(states):
            column = rows[:, first + state : first + state + 1]
            start = (place * states + state) * CHUNKS
            table_ref[start : start + CHUNKS, :] = jnp.broadcast_to(column, (CHUNKS, LANES))


def tile(ref, place, state, states):
    start = (place * states + state) * CHUNKS
    return ref[start : start + CHUNKS, :]


def row(ref, number):
    return ref[number : number + 1, :]


def inverse_rms(tokens):
    return lax.rsqrt(jnp.mean(tokens * tokens, axis=1, keepdims=True) + NORM_EPS)


def columns(masks_ref, tap):
    return jnp.broadcast_to(row(masks_ref, tap), (LANES, masks_ref.shape[1])).T


def two_rows(line):
    high = line.astype(jnp.bfloat16).astype(jnp.float32)
    number = lax.broadcasted_iota(jnp.int32, (2 * CHUNKS, line.shape[1]), 0)
    return jnp.where(number == 0, high, jnp.where(number == 1, line - high, 0.0)).astype(jnp.bfloat16)


def group_at(group):
    return pl.ds(pl.multiple_of(group * LANES, LANES), LANES)


def params():
    return pltpu.CompilerParams(vmem_limit_bytes=64 * MIB)


def cost(us):
    return pl.CostEstimate(flops=0, bytes_accessed=int(us * 3e6), transcendentals=0)


def shifted(block, rim, back):
    if back == 0:
        return block
    moved = pltpu.roll(block, back, 0)
    near = lax.broadcasted_iota(jnp.int32, (CHUNKS, block.shape[1]), 0)
    top = jnp.where(near < back, pltpu.roll(rim, back, 0), moved[:CHUNKS])
    return jnp.concatenate([top, moved[CHUNKS:]], axis=0)


def enter_kernel(
    kernel, scan_width,
    tokens_ref, rim_tokens_ref, cot_ref, tap_bias_ref, step_bias_ref, skip_ref, gain_ref, masks_ref,
    conv_w_ref, gate_w_ref, out_w_ref, taps_ref, weight_ref,
    conv_ref, rim_ref, out_ref, gate_ref, gg_ref, normed_ref, proj_ref, stacked_ref,
    both_ref, mask_ref, bias_ref,
):
    length = tokens_ref.shape[0]
    block = conv_w_ref.shape[1]

    @pl.when(pl.program_id(0) == 0)
    def _():
        for number, ref in enumerate((tap_bias_ref, step_bias_ref, skip_ref, gain_ref)):
            stacked_ref[number : number + 1, :] = ref[...].reshape(1, ref.shape[0])
        for tap in range(kernel):
            mask_ref[tap] = columns(masks_ref, tap)
        gain = row(stacked_ref, GAIN)
        tokens = tokens_ref[...].astype(jnp.float32)
        normed = (tokens * inverse_rms(tokens) * gain).astype(jnp.bfloat16)
        rim = rim_tokens_ref[...].astype(jnp.float32)
        rim = (rim * inverse_rms(rim) * gain).astype(jnp.bfloat16)
        normed_ref[...] = normed
        both_ref[:length, :] = normed
        both_ref[length:, :] = jnp.concatenate([rim, rim], axis=0)
        proj_ref[...] = jnp.zeros_like(proj_ref)

    normed = both_ref[...]
    conv_in = dot(normed, conv_w_ref[...], ((1,), (0,))).astype(jnp.bfloat16)
    conv_ref[...] = conv_in[:length]
    wide = conv_in[:length].astype(jnp.float32)
    rim = conv_in[length : length + CHUNKS].astype(jnp.float32)
    rim_ref[...] = rim
    at = pl.ds(pl.multiple_of(pl.program_id(0) * block, LANES), block)
    total = jnp.broadcast_to(stacked_ref[TAP_BIAS : TAP_BIAS + 1, at], (length, block))
    for tap in range(kernel):
        mask = jnp.concatenate([mask_ref[tap]] * (block // LANES), axis=1)
        total = total + row(taps_ref, tap) * shifted(wide, rim, kernel - 1 - tap) * mask
    out = (total * sigmoid(total)).astype(jnp.bfloat16)
    out_ref[...] = out
    proj_ref[:, :scan_width] += dot(out, weight_ref[...], ((1,), (1,)))
    gate_ref[...] = dot(normed[:length], gate_w_ref[...], ((1,), (0,)))
    gg_ref[...] = dot(cot_ref[...], out_w_ref[...], ((1,), (1,)))


def run_enter(tokens, rim, cot, vectors, masks, conv_w, gate_w, out_w, taps, weight):
    length, model = tokens.shape
    width = conv_w.shape[1]
    block = 3 * LANES
    f32, bf16 = jnp.float32, jnp.bfloat16
    flat = pl.BlockSpec(memory_space=pltpu.VMEM)
    return pl.pallas_call(
        functools.partial(enter_kernel, taps.shape[0], weight.shape[0]),
        grid=(width // block,),
        in_specs=[whole(length, model), whole(CHUNKS, model), whole(length, model)] + [flat] * 4 + [
            whole(*masks.shape), column_block(model, block), column_block(model, block),
            pl.BlockSpec((block, model), lambda g: (g, 0)), column_block(taps.shape[0], block),
            column_block(weight.shape[0], block),
        ],
        out_specs=[
            column_block(length, block), column_block(CHUNKS, block), column_block(length, block),
            column_block(length, block), column_block(length, block), whole(length, model),
            whole(length, LANES), whole(len(vectors), width),
        ],
        out_shape=[
            jax.ShapeDtypeStruct((length, width), bf16), jax.ShapeDtypeStruct((CHUNKS, width), f32),
            jax.ShapeDtypeStruct((length, width), bf16), jax.ShapeDtypeStruct((length, width), f32),
            jax.ShapeDtypeStruct((length, width), f32), jax.ShapeDtypeStruct((length, model), bf16),
            jax.ShapeDtypeStruct((length, LANES), f32),
            jax.ShapeDtypeStruct((len(vectors), width), f32),
        ],
        scratch_shapes=[
            pltpu.VMEM((length + 2 * CHUNKS, model), bf16),
            pltpu.VMEM((taps.shape[0], length, LANES), f32), pltpu.VMEM((8, LANES), f32),
        ],
        compiler_params=params(), cost_estimate=cost(6), name="enter",
    )(tokens, rim, cot, *vectors, masks, conv_w, gate_w, out_w, taps, weight)


def early_kernel(members, where_ref, normed_ref, cot_ref, *rest):
    early_refs, turned_ref = rest[:PLANE], rest[PLANE]
    model = normed_ref.shape[1]
    for group in range(model // LANES):
        at = slice(group * LANES, (group + 1) * LANES)
        turned_ref[at, :] = normed_ref[:, at].astype(jnp.float32).T
        turned_ref[model + group * LANES : model + (group + 1) * LANES, :] = (
            cot_ref[:, at].astype(jnp.float32).T
        )
    rows, lines = model // members, members // PLANE
    for mask, early_ref in enumerate(early_refs):
        place = jnp.bitwise_xor(where_ref[0] % PLANE, mask)
        for source in range(2):
            pieces = []
            for line in range(lines):
                first = source * model + (line * PLANE + place) * rows
                if rows % 8 == 0:
                    first = pl.multiple_of(first, 8)
                pieces.append(turned_ref[pl.ds(first, rows), :])
            at = slice(source * lines * rows, (source + 1) * lines * rows)
            early_ref[at, :] = jnp.concatenate(pieces, axis=0).astype(jnp.bfloat16)


def run_early(where, normed, cot):
    length, model = normed.shape
    members = lax.axis_size("seq")
    vmem = pl.BlockSpec(memory_space=pltpu.VMEM)
    early = jax.ShapeDtypeStruct((2 * model // PLANE, length), jnp.bfloat16)
    return pl.pallas_call(
        functools.partial(early_kernel, members),
        in_specs=[pl.BlockSpec(memory_space=pltpu.SMEM), vmem, vmem],
        out_specs=[vmem] * PLANE, out_shape=[early] * PLANE,
        scratch_shapes=[pltpu.VMEM((2 * model, length), jnp.float32)],
        compiler_params=params(), cost_estimate=cost(3), name="early",
    )(where, normed, cot)


def ends_kernel(
    rank, states,
    own_ref, peer_ref, weight_ref, bias_ref, decay_ref, conv_ref, gg_ref, gate_ref, masks_ref,
    ends_ref, seeds_ref, totals_ref,
    proj_ref, in_ref, out_ref, same_ref, *scratch,
):
    length, width = conv_ref.shape
    proj_ref[...] = own_ref[...] + peer_ref[...]
    spread(proj_ref, rank, in_ref, states, length)
    spread(proj_ref, rank + states, out_ref, states, length)
    same_ref[...] = columns(masks_ref, masks_ref.shape[0] - 2)

    @pl.loop(0, width // LANES)
    def _(group):
        at = group_at(group)
        views = [ref.at[:, at] for ref in (weight_ref, bias_ref, decay_ref, conv_ref, gg_ref, gate_ref)]
        outs = [ref.at[:, at] for ref in (ends_ref, seeds_ref, totals_ref)]
        ends_group(rank, states, *views, *outs, proj_ref, in_ref, out_ref, same_ref, *scratch)


def ends_group(
    rank, states,
    weight_ref, bias_ref, decay_ref, conv_ref, gg_ref, gate_ref,
    ends_ref, seeds_ref, totals_ref,
    proj_ref, in_ref, out_ref, same_ref, long_ref, drive_ref, source_ref, end_ref, seed_ref,
):
    length = conv_ref.shape[0]
    places = length // CHUNKS
    low = proj_ref[:, :rank].astype(jnp.bfloat16)
    step_pre = dot(low, weight_ref[...], ((1,), (0,))) + row(bias_ref, STEP_BIAS)
    step = softplus(step_pre)
    long_ref[...] = jnp.where(same_ref[...] > 0.0, step, FAR)
    drive_ref[...] = step * conv_ref[...].astype(jnp.float32)
    gate = gate_ref[...]
    source_ref[...] = gg_ref[...] * gate * sigmoid(gate)
    rate2 = -jnp.exp(decay_ref[...]) * LOG2E
    rates = [jnp.broadcast_to(rate2[n : n + 1, :], (CHUNKS, LANES)) for n in range(states)]
    hidden = [None] * states
    sums = None
    for place in range(places):
        long = long_ref[strided(place, length), :]
        drive = drive_ref[strided(place, length), :]
        sums = long if place == 0 else sums + long
        for n in range(states):
            term = tile(in_ref, place, n, states) * drive
            hidden[n] = term if place == 0 else jnp.exp2(long * rates[n]) * hidden[n] + term
    for n in range(states):
        end_ref[n * CHUNKS : (n + 1) * CHUNKS, :] = hidden[n]
    back = [None] * states
    for place in reversed(range(places)):
        long = long_ref[strided(place, length), :]
        source = source_ref[strided(place, length), :]
        for n in range(states):
            term = tile(out_ref, place, n, states) * source
            term = term if place == places - 1 else back[n] + term
            back[n] = jnp.exp2(long * rates[n]) * term
    for n in range(states):
        seed_ref[n * CHUNKS : (n + 1) * CHUNKS, :] = back[n]
    ends_ref[...] = end_ref[...]
    seeds_ref[...] = seed_ref[...]
    decays = [jnp.exp2(rate2 * sums[c : c + 1, :]) for c in range(CHUNKS)]
    end = jnp.zeros((states, LANES), jnp.float32)
    seed = jnp.zeros((states, LANES), jnp.float32)
    for c in range(CHUNKS):
        end = decays[c] * end + end_ref[pl.ds(c, states, stride=CHUNKS), :]
    for c in reversed(range(CHUNKS)):
        seed = decays[c] * seed + seed_ref[pl.ds(c, states, stride=CHUNKS), :]
    totals_ref[:states, :] = end.astype(jnp.bfloat16)
    totals_ref[states : 2 * states, :] = seed.astype(jnp.bfloat16)
    totals_ref[2 * states :, :] = two_rows(jnp.sum(sums, axis=0, keepdims=True))


def scan_kernel(
    rank, states, members,
    where_ref, own_ref, peer_ref, weight_ref, bias_ref, decay_ref, conv_ref, gg_ref, gate_ref, masks_ref,
    ends_ref, seeds_ref, near_ref, *rest,
):
    stride, radix = levels(members)[-1]
    far_refs = rest[: radix - 1]
    both_ref, small_ref, gconv_ref, gproj_ref = rest[-22:-18]
    scratch = rest[-18:]
    (
        proj_ref, in_ref, out_ref, long_ref, true_ref, drive_ref, source_ref, same_ref,
        start_ref, last_ref, hidden_ref, in_acc, out_acc, scan_ref, gstep_ref, mix_ref, end_ref, seed_ref,
    ) = scratch
    length, width = conv_ref.shape
    places = length // CHUNKS
    proj_ref[...] = own_ref[...] + peer_ref[...]
    spread(proj_ref, rank, in_ref, states, length)
    spread(proj_ref, rank + states, out_ref, states, length)
    same_ref[...] = columns(masks_ref, masks_ref.shape[0] - 2)
    in_acc[...] = jnp.zeros_like(in_acc)
    out_acc[...] = jnp.zeros_like(out_acc)
    gproj_ref[...] = jnp.zeros_like(gproj_ref)
    digit = where_ref[0] // stride % radix

    @pl.loop(0, width // LANES)
    def _(group):
        at = group_at(group)
        sliced = (
            weight_ref, bias_ref, decay_ref, conv_ref, gg_ref, gate_ref, ends_ref, seeds_ref, near_ref,
            both_ref, gconv_ref,
        )
        views = [ref.at[:, at] for ref in sliced]
        scan_group(
            rank, states, digit, [ref.at[:, at] for ref in far_refs], *views, small_ref.at[at, :],
            gproj_ref, *scratch,
        )

    wide = states * LANES
    source_state = lax.broadcasted_iota(jnp.int32, (wide, LANES), 0) // LANES
    column = lax.broadcasted_iota(jnp.int32, (wide, LANES), 1)
    total = jnp.zeros((length, LANES), jnp.float32)
    for acc, first in ((in_acc, rank), (out_acc, rank + states)):
        pick = jnp.where(source_state + first == column, 1.0, 0.0).astype(jnp.bfloat16)
        value = acc[...]
        high = value.astype(jnp.bfloat16)
        rest = (value - high.astype(jnp.float32)).astype(jnp.bfloat16)
        total = total + dot(high, pick, ((1,), (0,))) + dot(rest, pick, ((1,), (0,)))
    scan_ref[...] = total
    for place in range(places):
        mix_ref[strided(place, length), :] = scan_ref[place * CHUNKS : (place + 1) * CHUNKS, :]
    gproj_ref[...] += mix_ref[...]


def scan_group(
    rank, states, digit, far_refs,
    weight_ref, bias_ref, decay_ref, conv_ref, gg_ref, gate_ref, ends_ref, seeds_ref, near_ref,
    both_ref, gconv_ref, small_ref, gproj_ref,
    proj_ref, in_ref, out_ref, long_ref, true_ref, drive_ref, source_ref, same_ref,
    start_ref, last_ref, hidden_ref, in_acc, out_acc, scan_ref, gstep_ref, mix_ref, end_ref, seed_ref,
):
    length = conv_ref.shape[0]
    places = length // CHUNKS
    low = proj_ref[:, :rank].astype(jnp.bfloat16)
    step_pre = dot(low, weight_ref[...], ((1,), (0,))) + row(bias_ref, STEP_BIAS)
    step = softplus(step_pre)
    conv = conv_ref[...].astype(jnp.float32)
    gate = gate_ref[...]
    gg = gg_ref[...]
    sigma = sigmoid(gate)
    act = gate * sigma
    source_all = gg * act
    true_ref[...] = step
    long_ref[...] = jnp.where(same_ref[...] > 0.0, step, FAR)
    drive_ref[...] = step * conv
    source_ref[...] = source_all
    rate = -jnp.exp(decay_ref[...])
    rate2 = rate * LOG2E
    rates = [jnp.broadcast_to(rate2[n : n + 1, :], (CHUNKS, LANES)) for n in range(states)]
    sums = long_ref[strided(0, length), :]
    for place in range(1, places):
        sums = sums + long_ref[strided(place, length), :]
    decays = [jnp.exp2(rate2 * sums[c : c + 1, :]) for c in range(CHUNKS)]
    carry, incoming = arrive(digit, rate2, near_ref, far_refs, states)
    end_ref[...] = ends_ref[...]
    seed_ref[...] = seeds_ref[...]
    state = carry
    for c in range(CHUNKS):
        start_ref[pl.ds(c, states, stride=CHUNKS), :] = state
        state = decays[c] * state + end_ref[pl.ds(c, states, stride=CHUNKS), :]
    state = incoming
    for c in reversed(range(CHUNKS)):
        last_ref[pl.ds(c, states, stride=CHUNKS), :] = state
        state = decays[c] * state + seed_ref[pl.ds(c, states, stride=CHUNKS), :]

    hidden = [start_ref[n * CHUNKS : (n + 1) * CHUNKS, :] for n in range(states)]
    for place in range(places):
        long = long_ref[strided(place, length), :]
        drive = drive_ref[strided(place, length), :]
        source = source_ref[strided(place, length), :]
        rows = slice(place * CHUNKS, (place + 1) * CHUNKS)
        scan = None
        for n in range(states):
            lanes = slice(n * LANES, (n + 1) * LANES)
            value = jnp.exp2(long * rates[n]) * hidden[n] + tile(in_ref, place, n, states) * drive
            hidden[n] = value
            if place < places - 1:
                hidden_ref[(place * states + n) * CHUNKS : (place * states + n + 1) * CHUNKS, :] = value
            part = tile(out_ref, place, n, states) * value
            scan = part if n == 0 else scan + part
            out_acc[rows, lanes] += source * value
        scan_ref[strided(place, length), :] = scan

    back = [last_ref[n * CHUNKS : (n + 1) * CHUNKS, :] for n in range(states)]
    logs = [None] * states
    for place in reversed(range(places)):
        long = long_ref[strided(place, length), :]
        true = true_ref[strided(place, length), :]
        drive = drive_ref[strided(place, length), :]
        source = source_ref[strided(place, length), :]
        rows = slice(place * CHUNKS, (place + 1) * CHUNKS)
        gstep = None
        mixed = None
        for n in range(states):
            lanes = slice(n * LANES, (n + 1) * LANES)
            grad = back[n] + tile(out_ref, place, n, states) * source
            previous = (
                start_ref[n * CHUNKS : (n + 1) * CHUNKS, :] if place == 0
                else tile(hidden_ref, place - 1, n, states)
            )
            back[n] = jnp.exp2(long * rates[n]) * grad
            log = back[n] * previous
            part = log * true
            logs[n] = part if logs[n] is None else logs[n] + part
            part = log * rates[n]
            gstep = part if n == 0 else gstep + part
            part = grad * tile(in_ref, place, n, states)
            mixed = part if n == 0 else mixed + part
            in_acc[rows, lanes] += grad * drive
        gstep_ref[strided(place, length), :] = gstep
        mix_ref[strided(place, length), :] = mixed

    scan_out = scan_ref[...] + row(bias_ref, SKIP) * conv
    gated = scan_out * act
    ggate = gg * scan_out * sigma * (1.0 + gate * (1.0 - sigma))
    mix = mix_ref[...]
    gconv_ref[...] = source_all * row(bias_ref, SKIP) + mix * step
    gpre = (gstep_ref[...] * LN2 + mix * conv) * sigmoid(step_pre)
    gpre_low = gpre.astype(jnp.bfloat16)
    gproj_ref[:, :rank] += dot(gpre_low, weight_ref[...], ((1,), (1,)))
    step_part = dot(gpre_low, proj_ref[...].astype(jnp.bfloat16), ((0,), (0,)))
    row_number = lax.broadcasted_iota(jnp.int32, (LANES, LANES), 0)
    table = jnp.where(row_number == rank + states, jnp.sum(gpre, axis=0, keepdims=True), 0.0)
    table = jnp.where(
        row_number == rank + states + 1, jnp.sum(source_all * conv, axis=0, keepdims=True), table
    )
    for n in range(states):
        value = jnp.sum(logs[n], axis=0, keepdims=True) * rate[n : n + 1, :]
        table = jnp.where(row_number == rank + n, value, table)
    lane_number = lax.broadcasted_iota(jnp.int32, (LANES, LANES), 1)
    small = jnp.where(lane_number < rank, step_part, table.T)
    both_ref[:length, :] = gated.astype(jnp.bfloat16)
    both_ref[length:, :] = ggate.astype(jnp.bfloat16)
    small_ref[...] = small.astype(jnp.bfloat16)


def column_block(rows, width=LANES):
    return pl.BlockSpec((rows, width), lambda g: (0, g))


def whole(*shape):
    return pl.BlockSpec(shape, lambda g: (0,) * len(shape))


def run_ends(own, peer, weight, stacked, decay_log, conv, gg, gate, masks):
    length, width = conv.shape
    rank, states = weight.shape[0], decay_log.shape[0]
    tall = length // CHUNKS * states * CHUNKS
    f32 = jnp.float32
    block = pltpu.VMEM((length, LANES), f32)
    vmem = pl.BlockSpec(memory_space=pltpu.VMEM)
    return pl.pallas_call(
        functools.partial(ends_kernel, rank, states),
        in_specs=[vmem] * 9, out_specs=[vmem] * 3,
        out_shape=[
            jax.ShapeDtypeStruct((states * CHUNKS, width), f32),
            jax.ShapeDtypeStruct((states * CHUNKS, width), f32),
            jax.ShapeDtypeStruct((2 * states + 2 * CHUNKS, width), jnp.bfloat16),
        ],
        scratch_shapes=[
            block, pltpu.VMEM((tall, LANES), f32), pltpu.VMEM((tall, LANES), f32),
            block, block, block, block,
            pltpu.VMEM((states * CHUNKS, LANES), f32), pltpu.VMEM((states * CHUNKS, LANES), f32),
        ],
        compiler_params=params(), cost_estimate=cost(8), name="ends",
    )(own, peer, weight, stacked, decay_log, conv, gg, gate, masks)


def run_scan(where, own, peer, weight, stacked, decay_log, conv, gg, gate, masks, ends, seeds, near, far, deps):
    length, width = conv.shape
    members = lax.axis_size("seq")
    rank, states = weight.shape[0], decay_log.shape[0]
    places = length // CHUNKS
    tall = places * states * CHUNKS
    f32, bf16 = jnp.float32, jnp.bfloat16
    block = pltpu.VMEM((length, LANES), f32)
    table = pltpu.VMEM((tall, LANES), f32)
    vmem = pl.BlockSpec(memory_space=pltpu.VMEM)
    return pl.pallas_call(
        functools.partial(scan_kernel, rank, states, members),
        in_specs=[pl.BlockSpec(memory_space=pltpu.SMEM)] + [vmem] * (12 + len(far))
        + [pl.BlockSpec(memory_space=pl.ANY) for _ in deps],
        out_specs=[vmem] * 4,
        out_shape=[
            jax.ShapeDtypeStruct((2 * length, width), bf16),
            jax.ShapeDtypeStruct((width, LANES), bf16),
            jax.ShapeDtypeStruct((length, width), f32),
            jax.ShapeDtypeStruct((length, LANES), f32),
        ],
        scratch_shapes=[
            block, table, table, block, block, block, block, block,
            pltpu.VMEM((states * CHUNKS, LANES), f32), pltpu.VMEM((states * CHUNKS, LANES), f32),
            table, pltpu.VMEM((length, states * LANES), f32),
            pltpu.VMEM((length, states * LANES), f32), block, block, block,
            pltpu.VMEM((states * CHUNKS, LANES), f32), pltpu.VMEM((states * CHUNKS, LANES), f32),
        ],
        compiler_params=params(), cost_estimate=cost(15), name="scan",
    )(where, own, peer, weight, stacked, decay_log, conv, gg, gate, masks, ends, seeds, near, *far, *deps)


def levels(members):
    found, stride = [], 1
    while stride < members:
        radix = 4 if members // stride % 4 == 0 else 2
        found.append((stride, radix))
        stride *= radix
    return found


def chosen(refs, own, hop):
    value = own
    for mask, ref in enumerate(refs, 1):
        value = jnp.where(hop == mask, ref[...].astype(jnp.float32), value)
    return value


def arrive(digit, rate2, near_ref, far_refs, states):
    near = near_ref[...]
    radix = len(far_refs) + 1
    carry = jnp.zeros_like(rate2)
    incoming = jnp.zeros_like(rate2)
    blank = jnp.zeros(far_refs[0].shape, jnp.float32)
    for number in range(radix):
        value = chosen(far_refs, blank, digit ^ number)
        decay = jnp.exp2(rate2 * (value[states : states + 1] + value[states + 1 : states + 2]))
        carry = jnp.where(number < digit, decay * carry + value[:states], carry)
    for number in reversed(range(radix)):
        value = chosen(far_refs, blank, digit ^ number)
        decay = jnp.exp2(rate2 * (value[states : states + 1] + value[states + 1 : states + 2]))
        incoming = jnp.where(number > digit, decay * incoming + value[:states], incoming)
    before, behind = near[2 * states : 2 * states + 1], near[2 * states + 1 : 2 * states + 2]
    carry = near[:states] + jnp.exp2(rate2 * before) * carry
    incoming = near[states : 2 * states] + jnp.exp2(rate2 * behind) * incoming
    return carry, incoming


def fold_kernel(states, level, members, start, where_ref, decay_ref, *refs):
    stride, radix = levels(members)[level]
    next_stride, next_radix = levels(members)[level + 1]
    last = level + 2 == len(levels(members))
    digit = where_ref[0] // stride % radix
    if not start:
        old = refs[0][...]
        refs = refs[1:]
    own = refs[0][...]
    got = refs[1:radix]
    near_ref, outs = refs[radix], refs[radix + 1 :]
    rate2 = -jnp.exp(decay_ref[...]) * LOG2E
    own = own.astype(jnp.float32)
    values = [chosen(got, own, digit ^ number) for number in range(radix)]
    first = 2 * states
    sums = [value[first : first + 1] + value[first + 1 : first + 2] for value in values]
    decays = [jnp.exp2(rate2 * one) for one in sums]
    zero, line = jnp.zeros_like(rate2), jnp.zeros_like(sums[0])
    end, seed, carry, incoming, before, behind, total = zero, zero, zero, zero, line, line, line
    for number in range(radix):
        part = values[number][:states]
        end = decays[number] * end + part
        carry = jnp.where(number < digit, decays[number] * carry + part, carry)
        before = jnp.where(number < digit, before + sums[number], before)
        total = total + sums[number]
    for number in reversed(range(radix)):
        part = values[number][states : 2 * states]
        seed = decays[number] * seed + part
        incoming = jnp.where(number > digit, decays[number] * incoming + part, incoming)
        behind = jnp.where(number > digit, behind + sums[number], behind)
    if not start:
        old_before, old_behind = old[2 * states : 2 * states + 1], old[2 * states + 1 : 2 * states + 2]
        carry = old[:states] + jnp.exp2(rate2 * old_before) * carry
        incoming = old[states : 2 * states] + jnp.exp2(rate2 * old_behind) * incoming
        before, behind = before + old_before, behind + old_behind
    pad = jnp.zeros((6, line.shape[1]), jnp.float32)
    near_ref[...] = jnp.concatenate([carry, incoming, before, behind, pad], axis=0)
    tail = two_rows(total)
    if last:
        next_digit = where_ref[0] // next_stride % next_radix
        for mask, out in enumerate(outs, 1):
            value = jnp.where(next_digit < (next_digit ^ mask), end, seed)
            out[:states, :] = value.astype(jnp.bfloat16)
            out[states:, :] = tail
    else:
        outs[0][: 2 * states, :] = jnp.concatenate([end, seed], axis=0).astype(jnp.bfloat16)
        outs[0][2 * states :, :] = tail


def run_fold(level, where, decay_log, near, parts):
    states, width = decay_log.shape
    members = lax.axis_size("seq")
    f32, bf16 = jnp.float32, jnp.bfloat16
    vmem = pl.BlockSpec(memory_space=pltpu.VMEM)
    tall = jax.ShapeDtypeStruct((2 * states + 8, width), f32)
    if level + 2 == len(levels(members)):
        sent = [jax.ShapeDtypeStruct((states + 2 * CHUNKS, width), bf16)] * (levels(members)[-1][1] - 1)
    else:
        sent = [jax.ShapeDtypeStruct((2 * states + 2 * CHUNKS, width), bf16)]
    extra = [] if near is None else [near]
    return pl.pallas_call(
        functools.partial(fold_kernel, states, level, members, near is None),
        in_specs=[pl.BlockSpec(memory_space=pltpu.SMEM)] + [vmem] * (1 + len(extra) + len(parts)),
        out_specs=[vmem] * (1 + len(sent)),
        out_shape=[tall] + sent,
        compiler_params=params(), cost_estimate=cost(2), name="fold",
    )(where, decay_log, *extra, *parts)


def exchange(where, totals, decay_log):
    members = lax.axis_size("seq")
    found = levels(members)
    near = None
    for level, (stride, radix) in enumerate(found[:-1]):
        parts = [totals] + [hop(totals, mask * stride) for mask in range(1, radix)]
        near, *sent = run_fold(level, where, decay_log, near, parts)
        totals = sent[0]
    stride, radix = found[-1]
    return near, [hop(one, mask * stride) for mask, one in enumerate(sent, 1)]


def taps_kernel(
    kernel, ndeps,
    own_ref, peer_ref, conv_ref, in_ref, ext_ref, weight_ref, gconv_ref, taps_ref, params_ref, masks_ref,
    first_small_ref, *rest,
):
    main_ref, rim_ref, small_ref = rest[ndeps:]
    length, total_width = conv_ref.shape
    width = weight_ref.shape[0]
    grad_proj = (own_ref[...] + peer_ref[...]).astype(jnp.bfloat16)
    masks = [columns(masks_ref, tap) for tap in range(kernel)]
    row_number = lax.broadcasted_iota(jnp.int32, (LANES, LANES), 0)
    lane_number = lax.broadcasted_iota(jnp.int32, (LANES, LANES), 1)
    near_row = lax.broadcasted_iota(jnp.int32, (CHUNKS, LANES), 0)
    token = lax.broadcasted_iota(jnp.int32, (length, LANES), 0)
    for group in range(total_width // LANES):
        at = slice(group * LANES, (group + 1) * LANES)
        taps = [taps_ref[tap : tap + 1, at] for tap in range(kernel)]
        conv_in = in_ref[:, at].astype(jnp.float32)
        ext = ext_ref[:, at]
        seen = [shifted(conv_in, ext, kernel - 1 - tap) * masks[tap] for tap in range(kernel)]
        pre = jnp.broadcast_to(params_ref[TAP_BIAS : TAP_BIAS + 1, at], (length, LANES))
        for tap in range(kernel):
            pre = pre + taps[tap] * seen[tap]
        scan_part = dot(conv_ref[:, at], grad_proj, ((0,), (0,)))
        grad = gconv_ref[:, at] + dot(grad_proj[:, :width], weight_ref[:, at], ((1,), (0,)))
        grad = grad * silu_grad(pre)
        table = jnp.where(row_number == width + kernel, jnp.sum(grad, axis=0, keepdims=True), 0.0)
        main = jnp.zeros((length, LANES), jnp.float32)
        rim = jnp.zeros((CHUNKS, LANES), jnp.float32)
        for tap in range(kernel):
            back = kernel - 1 - tap
            part = jnp.sum(grad * seen[tap], axis=0, keepdims=True)
            table = jnp.where(row_number == width + tap, part, table)
            masked = grad * masks[tap] * taps[tap]
            if back == 0:
                main = main + masked
            else:
                moved = pltpu.roll(masked, length - back, 0)
                main = main + jnp.where(token < length - back, moved, 0.0)
                rim = rim + jnp.where(
                    near_row >= CHUNKS - back, pltpu.roll(masked[:CHUNKS], CHUNKS - back, 0), 0.0
                )
        main_ref[:, at] = main
        rim_ref[:, at] = rim
        small_ref[at, :LANES] = first_small_ref[at, :]
        small_ref[at, LANES:] = jnp.where(lane_number < width, scan_part, table.T).astype(jnp.bfloat16)


def run_taps(own, peer, conv, conv_in, ext, weight, gconv, taps, stacked, masks, small, deps):
    length, width = conv.shape
    kernel = taps.shape[0]
    f32 = jnp.float32
    vmem = pl.BlockSpec(memory_space=pltpu.VMEM)
    return pl.pallas_call(
        functools.partial(taps_kernel, kernel, len(deps)),
        in_specs=[vmem] * 11 + [pl.BlockSpec(memory_space=pl.ANY) for _ in deps],
        out_specs=[vmem] * 3,
        out_shape=[
            jax.ShapeDtypeStruct((length, width), f32),
            jax.ShapeDtypeStruct((CHUNKS, width), f32),
            jax.ShapeDtypeStruct((width, 2 * LANES), jnp.bfloat16),
        ],
        compiler_params=params(), cost_estimate=cost(4), name="taps",
    )(own, peer, conv, conv_in, ext, weight, gconv, taps, stacked, masks, small, *deps)


def inputs_kernel(
    ndeps, main_ref, rim_ref, weight_ref, gate_part_ref, tokens_ref, *rest,
):
    low_ref, normed_ref = rest[ndeps:]
    length, width = main_ref.shape
    main = main_ref[...]
    low = jnp.concatenate(
        [main[: length - CHUNKS], main[length - CHUNKS :] + rim_ref[...]], axis=0
    ).astype(jnp.bfloat16)
    normed = dot(low, weight_ref[...], ((1,), (1,))) + gate_part_ref[...]
    normed_ref[...] = normed
    tokens = tokens_ref[...].astype(jnp.float32)
    gain = jnp.sum(normed * tokens * inverse_rms(tokens), axis=0, keepdims=True)
    low_ref[:length, :] = low
    low_ref[length:, :] = two_rows(gain)


def run_inputs(main, rim, weight, gate_part, tokens, deps):
    length, width = main.shape
    return pl.pallas_call(
        functools.partial(inputs_kernel, len(deps)),
        in_specs=[pl.BlockSpec(memory_space=pltpu.VMEM)] * 5
        + [pl.BlockSpec(memory_space=pl.ANY) for _ in deps],
        out_shape=[
            jax.ShapeDtypeStruct((length + 2 * CHUNKS, width), jnp.bfloat16),
            jax.ShapeDtypeStruct((length, weight.shape[0]), jnp.float32),
        ],
        compiler_params=params(), cost_estimate=cost(3), name="inputs",
    )(main, rim, weight, gate_part, tokens, *deps)


def pick(rows, lanes, shift):
    row = lax.broadcasted_iota(jnp.int32, (rows, lanes), 0)
    lane = lax.broadcasted_iota(jnp.int32, (rows, lanes), 1)
    return jnp.where(lane == row + shift, 1.0, 0.0).astype(jnp.bfloat16)


def products_kernel(
    halves, members, gain, ndeps,
    where_ref, e0_ref, e1_ref, e2_ref, e3_ref, here_ref, x_ref, y_ref, first_ref, second_ref,
    *rest,
):
    kept_ref, *sent_refs, total_ref = rest[ndeps:]
    f32, bf16 = jnp.float32, jnp.bfloat16
    lines = members // PLANE
    tall, width = here_ref.shape
    length = e0_ref.shape[1]
    share = e0_ref.shape[0] // 2
    rows = share // lines
    early = (e0_ref, e1_ref, e2_ref, e3_ref)
    cut = tall // 2
    for number, half in enumerate(halves):
        at = slice(number * length, (number + 1) * length)
        total = None
        for mask in range(PLANE):
            if mask < 3:
                late = (here_ref, x_ref, y_ref)[mask][at, :]
            else:
                late = jnp.concatenate([first_ref[...], second_ref[...]], axis=0)[at]
            part = dot(early[mask][half * share : (half + 1) * share, :], late, ((1,), (0,)))
            total = part if total is None else total + part
        for line in range(lines):
            total_ref[line, number * rows : (number + 1) * rows, :] = total[line * rows : (line + 1) * rows]
    if gain:
        last = slice(tall - 2 * CHUNKS, tall)
        line = jnp.zeros((1, width), f32)
        for ref in (here_ref, x_ref, y_ref):
            line = line + jnp.sum(ref[last, :].astype(f32), axis=0, keepdims=True)
        tail = second_ref[second_ref.shape[0] - 2 * CHUNKS :, :]
        line = line + jnp.sum(tail.astype(f32), axis=0, keepdims=True)
        for number in range(lines):
            total_ref[number, len(halves) * rows :, :] = jnp.broadcast_to(
                line, (total_ref.shape[1] - len(halves) * rows, width)
            )
    send(where_ref[0], levels(members)[1:], 0, total_ref, kept_ref, sent_refs, gain)


def split_gain(value, gain):
    if not gain:
        return value.astype(jnp.bfloat16)
    number = value.shape[0] - 2 * CHUNKS
    return jnp.concatenate(
        [value[:number].astype(jnp.bfloat16), two_rows(value[number : number + 1])], axis=0
    )


def send(device, found, level, total_ref, kept_ref, sent_refs, gain):
    stride, radix = found[len(found) - 1 - level]
    digit = device // stride % radix
    size = total_ref.shape[0] // radix
    for mask in range(radix):
        for block in range(size):
            value = total_ref[jnp.bitwise_xor(digit, mask) * size + block]
            if mask == 0:
                kept_ref[block] = value
            else:
                sent_refs[mask - 1][block] = split_gain(value, gain)


def gather_kernel(members, level, gain, where_ref, kept_ref, *refs):
    found = levels(members)[1:]
    radix = found[len(found) - 1 - level][1]
    got, outs = refs[: radix - 1], refs[radix - 1 :]
    total = kept_ref[...]
    number = total.shape[1] - (2 * CHUNKS if gain else 0)
    pieces = total[:, :number, :]
    line = total[:, number : number + 1, :] if gain else None
    for ref in got:
        value = ref[...].astype(jnp.float32)
        pieces = pieces + value[:, :number, :]
        if gain:
            line = line + value[:, number : number + 1, :] + value[:, number + 1 : number + 2, :]
    if level + 1 == len(found):
        if gain:
            outs[0][...] = pieces[0]
            outs[1][...] = line[0]
        else:
            rows = outs[0].shape[0]
            for index, out in enumerate(outs):
                out[...] = pieces[0, index * rows : (index + 1) * rows, :]
        return
    total_ref = refs[-1]
    total_ref[:, :number, :] = pieces
    if gain:
        total_ref[:, number:, :] = jnp.broadcast_to(line, (total.shape[0], 2 * CHUNKS, total.shape[2]))
    send(where_ref[0], found, level + 1, total_ref, outs[0], outs[1:-1], gain)


def gather_plane(late):
    cut = late.shape[0] // 2
    x, y = hop(late, 1), hop(late, 2)
    return late, x, y, hop(x[:cut], 2), hop(y[cut:], 1)


def multiply(halves, where, early, late, gain, deps):
    f32, bf16 = jnp.float32, jnp.bfloat16
    members = lax.axis_size("seq")
    lines = members // PLANE
    width = late[0].shape[1]
    rows = early[0].shape[0] // 2 // lines
    block = len(halves) * rows + (2 * CHUNKS if gain else 0)
    vmem = pl.BlockSpec(memory_space=pltpu.VMEM)
    out_shape = level_shapes(0, lines, block, width)
    return pl.pallas_call(
        functools.partial(products_kernel, halves, members, gain, len(deps)),
        in_specs=[pl.BlockSpec(memory_space=pltpu.SMEM)] + [vmem] * 9
        + [pl.BlockSpec(memory_space=pl.ANY) for _ in deps],
        out_specs=[vmem] * len(out_shape), out_shape=out_shape,
        scratch_shapes=[pltpu.VMEM((lines, block, width), f32)],
        compiler_params=params(), cost_estimate=cost(4), name="products",
    )(where, *early, *late, *deps)


def level_shapes(level, left, block, width):
    found = levels(lax.axis_size("seq"))[1:]
    radix = found[len(found) - 1 - level][1]
    kept = (left // radix, block, width)
    return [jax.ShapeDtypeStruct(kept, jnp.float32)] + [
        jax.ShapeDtypeStruct(kept, jnp.bfloat16)
    ] * (radix - 1)


def add_lines(where, kept, sent, count, gain):
    f32 = jnp.float32
    members = lax.axis_size("seq")
    found = levels(members)[1:]
    vmem = pl.BlockSpec(memory_space=pltpu.VMEM)
    for level in range(len(found)):
        stride, radix = found[len(found) - 1 - level]
        got = [hop(one, mask * stride) for mask, one in enumerate(sent, 1)]
        left, block, width = kept.shape
        scratch = []
        if level + 1 == len(found):
            rows = (block - (2 * CHUNKS if gain else 0)) // count
            out_shape = [jax.ShapeDtypeStruct((rows, width), f32)] * count
            if gain:
                out_shape = out_shape + [jax.ShapeDtypeStruct((1, width), f32)]
        else:
            out_shape = level_shapes(level + 1, left, block, width)
            scratch = [pltpu.VMEM((left, block, width), f32)]
        kept, *sent = pl.pallas_call(
            functools.partial(gather_kernel, members, level, gain),
            in_specs=[pl.BlockSpec(memory_space=pltpu.SMEM)] + [vmem] * (1 + len(got)),
            out_specs=[vmem] * len(out_shape), out_shape=out_shape, scratch_shapes=scratch,
            compiler_params=params(), cost_estimate=cost(2), name="gather",
        )(where, kept, *got)
    return kept, *sent


def place_kernel(counts, got_ref, *refs):
    members, rows, wide = got_ref.shape
    width = members * rows
    table_ref = refs[-1]
    table_ref[...] = jnp.zeros_like(table_ref)
    for source in range(members):
        start = rows * source // LANES * LANES
        at = slice(start, start + 2 * LANES)
        place = pick(rows, 2 * LANES, rows * source - start)
        table_ref[:, at] += dot(got_ref[source], place, ((0,), (0,)))
    for out, (first, count) in zip(refs[:-1], counts, strict=True):
        out[...] = table_ref[first : first + count, :width]


def run_place(got, counts):
    members, rows, wide = got.shape
    width = members * rows
    f32 = jnp.float32
    padded = rows * (members - 1) // LANES * LANES + 2 * LANES
    return pl.pallas_call(
        functools.partial(place_kernel, counts),
        out_shape=[jax.ShapeDtypeStruct((count, width), f32) for _, count in counts],
        scratch_shapes=[pltpu.VMEM((wide, padded), f32)],
        compiler_params=params(), cost_estimate=cost(3), name="place",
    )(got)


def spread_kernel(got_ref, out_ref):
    members = got_ref.shape[0]
    total = got_ref[0].astype(jnp.float32)
    for member in range(1, members):
        total = total + got_ref[member].astype(jnp.float32)
    total = total.astype(out_ref.dtype)
    for member in range(members):
        out_ref[member] = total


def run_spread(got):
    return pl.pallas_call(
        spread_kernel, out_shape=jax.ShapeDtypeStruct(got.shape, got.dtype),
        compiler_params=params(), cost_estimate=cost(2), name="spread",
    )(got)


def from_behind(block, axis, distance):
    devices = range(lax.axis_size(axis))
    route = [(i - distance, i) for i in devices if i - distance in devices]
    return lax.ppermute(block, axis, route)


def swap(block):
    return lax.ppermute(block, "tp", [(0, 1), (1, 0)])


def hop(block, mask):
    members = lax.axis_size("seq")
    return lax.ppermute(block, "seq", [(i, i ^ mask) for i in range(members)])


def shards(
    tokens, norm_gain, in_conv_weight, in_gate_weight, conv_weight, conv_bias, scan_proj_weight,
    step_proj_weight, step_bias, decay_log, skip_gain, out_weight, segment_ids, cotangent,
):
    f32 = jnp.float32
    length, model = tokens.shape
    rank = step_proj_weight.shape[0]
    states = decay_log.shape[0]
    kernel = conv_weight.shape[0]
    width = conv_weight.shape[1]
    members = lax.axis_size("seq")
    device = lax.axis_index("seq")
    where = jnp.stack([device, lax.axis_index("tp")]).astype(jnp.int32)
    rows = width // members
    scan_width = rank + 2 * states
    rim_tokens = from_behind(tokens[length - CHUNKS :], "seq", 1)
    padded_ids = jnp.concatenate([jnp.full((kernel,), -1, jnp.int32), segment_ids])
    near_ids = lax.dynamic_slice_in_dim(padded_ids, device * length, length + kernel)
    masks = jnp.stack(
        [near_ids[kernel:] == near_ids[tap + 1 : tap + 1 + length] for tap in range(kernel)]
    ).astype(f32)
    scan_weight = scan_proj_weight.T

    conv_in, ext, conv_out, gate_in, grad_gated, normed, own, stacked = run_enter(
        tokens, rim_tokens, cotangent, (conv_bias, step_bias, skip_gain, norm_gain), masks,
        in_conv_weight, in_gate_weight, out_weight, conv_weight, scan_weight,
    )
    kept_early, *sent_early = run_early(where, normed, cotangent)
    early = [kept_early] + [hop(one, mask) for mask, one in enumerate(sent_early, 1)]
    peer = swap(own)
    ends, seeds, totals = run_ends(
        own, peer, step_proj_weight, stacked, decay_log, conv_out, grad_gated, gate_in, masks
    )
    near, far = exchange(where, totals, decay_log)
    both, first_small, grad_conv, low_own = run_scan(
        where, own, peer, step_proj_weight, stacked, decay_log, conv_out, grad_gated, gate_in, masks,
        ends, seeds, near, far, early[1:],
    )
    low_peer = swap(low_own)
    main, rim, small = run_taps(
        low_own, low_peer, conv_out, conv_in, ext, scan_weight, grad_conv, conv_weight, stacked, masks,
        first_small, (),
    )
    small = lax.all_to_all(small.reshape(members, rows, 2 * LANES), "seq", 0, 0, tiled=True)
    rim = from_behind(rim, "seq", -1)
    gated, ggate = both[:length], both[length:]
    first_late = gather_plane(both)
    gate_part = dot(ggate, in_gate_weight, ((1,), (1,)))
    low, normed_own = run_inputs(main, rim, in_conv_weight, gate_part, tokens, first_late[1:3])

    tok_float = tokens.astype(f32)
    inv_rms = inverse_rms(tok_float)
    branch_own = dot(gated, out_weight, ((1,), (0,)))
    branch = branch_own + swap(branch_own)
    mixed_out = (tok_float + branch).astype(jnp.bfloat16)
    grad_normed = normed_own + swap(normed_own)
    scaled_grad = grad_normed * norm_gain
    input_grad = (
        cotangent.astype(f32)
        + inv_rms * scaled_grad
        - tok_float * inv_rms * inv_rms * inv_rms
        * jnp.mean(scaled_grad * tok_float, axis=1, keepdims=True)
    )

    first_kept, *first_sent = multiply((1, 0), where, early, first_late, False, ())
    second_kept, *second_sent = multiply((0,), where, early, gather_plane(low), True, (first_kept,))
    out_grad, in_gate_grad = add_lines(where, first_kept, first_sent, 2, False)
    in_conv_grad, gain_grad = add_lines(where, second_kept, second_sent, 1, True)
    small = lax.all_to_all(run_spread(small), "seq", 0, 0, tiled=True)
    step_proj_grad, decay_log_grad, vectors, scan_proj_grad, conv_weight_grad, conv_bias_grad = run_place(
        small,
        (
            (0, rank), (rank, states), (rank + states, 2), (LANES, scan_width),
            (LANES + scan_width, kernel), (LANES + scan_width + kernel, 1),
        ),
    )
    gain_grad = gain_grad + swap(gain_grad)
    return (
        mixed_out, input_grad, gain_grad[0], in_conv_grad, in_gate_grad, conv_weight_grad,
        conv_bias_grad[0], scan_proj_grad.T, step_proj_grad, vectors[0], decay_log_grad, vectors[1],
        out_grad.T,
    )


def solution(mesh):
    in_specs = (
        P("seq", None), P(), P(None, "tp"), P(None, "tp"), P(None, "tp"), P("tp"), P("tp", None),
        P(None, "tp"), P("tp"), P(None, "tp"), P("tp"), P("tp", None), P(), P("seq", None),
    )
    out_specs = (
        P("seq", None), P("seq", None), P(), P("seq", "tp"), P("seq", "tp"), P(None, "tp"), P("tp"),
        P("tp", None), P(None, "tp"), P("tp"), P(None, "tp"), P("tp"), P("tp", "seq"),
    )
    return jax.shard_map(shards, mesh=mesh, in_specs=in_specs, out_specs=out_specs, check_vma=False)
```

```python
import functools

import jax
import jax.numpy as jnp
from jax import lax
from jax.experimental import pallas as pl
from jax.experimental.pallas import tpu as pltpu
from jax.sharding import PartitionSpec as P

NORM_EPS = 1e-05
LANES = 128
PLANE = 4
CHUNKS = 8
LOG2E = 1.4426950408889634
LN2 = 0.6931471805599453
FAR = 1e30
MIB = 1024 * 1024
TAP_BIAS, STEP_BIAS, SKIP, GAIN = 0, 1, 2, 3


def sigmoid(value):
    return 1.0 / (1.0 + jnp.exp(-value))


def silu_grad(value):
    sigma = sigmoid(value)
    return sigma * (1.0 + value * (1.0 - sigma))


def softplus(value):
    small = jnp.exp(-jnp.abs(value))
    series = small * (1.0 - small * (0.5 - small * (1.0 / 3.0 - small * 0.25)))
    return jnp.maximum(value, 0.0) + jnp.where(small < 0.01, series, jnp.log(1.0 + small))


def dot(first, second, contract):
    return lax.dot_general(
        first, second, (contract, ((), ())), preferred_element_type=jnp.float32
    )


def strided(number, length):
    return pl.ds(number, CHUNKS, stride=length // CHUNKS)


def spread(proj_ref, first, table_ref, states, length):
    for place in range(length // CHUNKS):
        rows = proj_ref[strided(place, length), :]
        for state in range(states):
            column = rows[:, first + state : first + state + 1]
            start = (place * states + state) * CHUNKS
            table_ref[start : start + CHUNKS, :] = jnp.broadcast_to(column, (CHUNKS, LANES))


def tile(ref, place, state, states):
    start = (place * states + state) * CHUNKS
    return ref[start : start + CHUNKS, :]


def padded(number, unit):
    return -(-number // unit) * unit


def row(ref, number):
    return ref[number : number + 1, :]


def inverse_rms(tokens):
    return lax.rsqrt(jnp.mean(tokens * tokens, axis=1, keepdims=True) + NORM_EPS)


def columns(masks_ref, tap):
    return jnp.broadcast_to(row(masks_ref, tap), (LANES, masks_ref.shape[1])).T


def two_rows(line):
    high = line.astype(jnp.bfloat16).astype(jnp.float32)
    number = lax.broadcasted_iota(jnp.int32, (2 * CHUNKS, line.shape[1]), 0)
    return jnp.where(number == 0, high, jnp.where(number == 1, line - high, 0.0)).astype(jnp.bfloat16)


def group_at(group):
    return pl.ds(pl.multiple_of(group * LANES, LANES), LANES)


def params():
    return pltpu.CompilerParams(vmem_limit_bytes=64 * MIB)


def cost(us):
    return pl.CostEstimate(flops=0, bytes_accessed=int(us * 3e6), transcendentals=0)


def shifted(block, rim, back):
    if back == 0:
        return block
    moved = pltpu.roll(block, back, 0)
    near = lax.broadcasted_iota(jnp.int32, (CHUNKS, block.shape[1]), 0)
    top = jnp.where(near < back, pltpu.roll(rim, back, 0), moved[:CHUNKS])
    return jnp.concatenate([top, moved[CHUNKS:]], axis=0)


def enter_kernel(
    kernel, scan_width,
    normed_ref, rim_tokens_ref, cot_ref, tap_bias_ref, step_bias_ref, skip_ref, gain_ref, masks_ref,
    conv_w_ref, gate_w_ref, out_w_ref, taps_ref, weight_ref,
    conv_ref, rim_ref, out_ref, gate_ref, gg_ref, proj_ref, stacked_ref,
    both_ref, mask_ref,
):
    length = normed_ref.shape[0]
    block = conv_w_ref.shape[1]

    @pl.when(pl.program_id(0) == 0)
    def _():
        for number, ref in enumerate((tap_bias_ref, step_bias_ref, skip_ref, gain_ref)):
            stacked_ref[number : number + 1, :] = ref[...].reshape(1, ref.shape[0])
        for tap in range(kernel):
            mask_ref[tap] = columns(masks_ref, tap)
        gain = row(stacked_ref, GAIN)
        rim = rim_tokens_ref[...].astype(jnp.float32)
        rim = (rim * inverse_rms(rim) * gain).astype(jnp.bfloat16)
        both_ref[:length, :] = normed_ref[...]
        both_ref[length:, :] = jnp.concatenate([rim, rim], axis=0)
        proj_ref[...] = jnp.zeros_like(proj_ref)

    normed = both_ref[...]
    conv_in = dot(normed, conv_w_ref[...], ((1,), (0,))).astype(jnp.bfloat16)
    conv_ref[...] = conv_in[:length]
    wide = conv_in[:length].astype(jnp.float32)
    rim = conv_in[length : length + CHUNKS].astype(jnp.float32)
    rim_ref[...] = rim
    at = pl.ds(pl.multiple_of(pl.program_id(0) * block, LANES), block)
    total = jnp.broadcast_to(stacked_ref[TAP_BIAS : TAP_BIAS + 1, at], (length, block))
    for tap in range(kernel):
        mask = jnp.concatenate([mask_ref[tap]] * (block // LANES), axis=1)
        total = total + row(taps_ref, tap) * shifted(wide, rim, kernel - 1 - tap) * mask
    out = (total * sigmoid(total)).astype(jnp.bfloat16)
    out_ref[...] = out
    proj_ref[:, :scan_width] += dot(out, weight_ref[...], ((1,), (1,)))
    gate_ref[...] = dot(normed[:length], gate_w_ref[...], ((1,), (0,)))
    gg_ref[...] = dot(cot_ref[...], out_w_ref[...], ((1,), (1,)))


def run_enter(normed, rim, cot, vectors, masks, conv_w, gate_w, out_w, taps, weight):
    length, model = normed.shape
    width = conv_w.shape[1]
    block = 3 * LANES
    f32, bf16 = jnp.float32, jnp.bfloat16
    flat = pl.BlockSpec(memory_space=pltpu.VMEM)
    return pl.pallas_call(
        functools.partial(enter_kernel, taps.shape[0], weight.shape[0]),
        grid=(width // block,),
        in_specs=[whole(length, model), whole(CHUNKS, model), whole(length, model)] + [flat] * 4 + [
            whole(*masks.shape), column_block(model, block), column_block(model, block),
            pl.BlockSpec((block, model), lambda g: (g, 0)), column_block(taps.shape[0], block),
            column_block(weight.shape[0], block),
        ],
        out_specs=[
            column_block(length, block), column_block(CHUNKS, block), column_block(length, block),
            column_block(length, block), column_block(length, block), whole(length, LANES),
            whole(len(vectors), width),
        ],
        out_shape=[
            jax.ShapeDtypeStruct((length, width), bf16), jax.ShapeDtypeStruct((CHUNKS, width), f32),
            jax.ShapeDtypeStruct((length, width), bf16), jax.ShapeDtypeStruct((length, width), f32),
            jax.ShapeDtypeStruct((length, width), f32), jax.ShapeDtypeStruct((length, LANES), f32),
            jax.ShapeDtypeStruct((len(vectors), width), f32),
        ],
        scratch_shapes=[
            pltpu.VMEM((length + 2 * CHUNKS, model), bf16),
            pltpu.VMEM((taps.shape[0], length, LANES), f32),
        ],
        compiler_params=params(), cost_estimate=cost(6), name="enter",
    )(normed, rim, cot, *vectors, masks, conv_w, gate_w, out_w, taps, weight)


def early_kernel(members, where_ref, tokens_ref, cot_ref, gain_ref, normed_ref, *rest):
    rim_ref, *early_refs, turned_ref = rest
    length, model = tokens_ref.shape
    rim_ref[...] = tokens_ref[length - CHUNKS :, :]
    tokens = tokens_ref[...].astype(jnp.float32)
    gain = gain_ref[...].reshape(1, model)
    normed_ref[...] = (tokens * inverse_rms(tokens) * gain).astype(jnp.bfloat16)
    for group in range(model // LANES):
        at = slice(group * LANES, (group + 1) * LANES)
        turned_ref[at, :] = normed_ref[:, at].astype(jnp.float32).T
        turned_ref[model + group * LANES : model + (group + 1) * LANES, :] = (
            cot_ref[:, at].astype(jnp.float32).T
        )
    rows, lines = model // members, members // PLANE
    for mask, early_ref in enumerate(early_refs):
        place = jnp.bitwise_xor(where_ref[0] % PLANE, mask)
        for source in range(2):
            pieces = []
            for line in range(lines):
                first = source * model + (line * PLANE + place) * rows
                if rows % 8 == 0:
                    first = pl.multiple_of(first, 8)
                pieces.append(turned_ref[pl.ds(first, rows), :])
            at = slice(source * lines * rows, (source + 1) * lines * rows)
            early_ref[at, :] = jnp.concatenate(pieces, axis=0).astype(jnp.bfloat16)


def run_early(where, tokens, cot, gain):
    length, model = tokens.shape
    members = lax.axis_size("seq")
    vmem = pl.BlockSpec(memory_space=pltpu.VMEM)
    early = jax.ShapeDtypeStruct((2 * model // PLANE, length), jnp.bfloat16)
    return pl.pallas_call(
        functools.partial(early_kernel, members),
        in_specs=[pl.BlockSpec(memory_space=pltpu.SMEM), vmem, vmem, vmem],
        out_specs=[vmem] * (2 + PLANE),
        out_shape=[
            jax.ShapeDtypeStruct(tokens.shape, jnp.bfloat16),
            jax.ShapeDtypeStruct((CHUNKS, model), jnp.bfloat16),
        ] + [early] * PLANE,
        scratch_shapes=[pltpu.VMEM((2 * model, length), jnp.float32)],
        compiler_params=params(), cost_estimate=cost(3), name="early",
    )(where, tokens, cot, gain)


def every(width):
    return [(group, slice(group * LANES, (group + 1) * LANES)) for group in range(width // LANES)]


def chunk_sums(long_ref, group, length):
    sums = long_ref[group, strided(0, length), :]
    for place in range(1, length // CHUNKS):
        sums = sums + long_ref[group, strided(place, length), :]
    return sums


def prepare(
    rank, states, own_ref, peer_ref, weight_ref, bias_ref, conv_ref, gg_ref, gate_ref, masks_ref,
    proj_ref, in_ref, out_ref, long_ref, drive_ref, source_ref, true_ref=None,
):
    length, width = conv_ref.shape
    proj_ref[...] = own_ref[...] + peer_ref[...]
    low = proj_ref[:, :rank].astype(jnp.bfloat16)
    step_pre = dot(low, weight_ref[...], ((1,), (0,))) + row(bias_ref, STEP_BIAS)
    spread(proj_ref, rank, in_ref, states, length)
    spread(proj_ref, rank + states, out_ref, states, length)
    same = columns(masks_ref, masks_ref.shape[0] - 2)
    for group, at in every(width):
        step = softplus(step_pre[:, at])
        if true_ref is not None:
            true_ref[group] = step
        long_ref[group] = jnp.where(same > 0.0, step, FAR)
        drive_ref[group] = step * conv_ref[:, at].astype(jnp.float32)
        gate = gate_ref[:, at]
        source_ref[group] = gg_ref[:, at] * gate * sigmoid(gate)
    return step_pre


def ends_kernel(
    rank, states, ndeps,
    own_ref, peer_ref, weight_ref, bias_ref, decay_ref, conv_ref, gg_ref, gate_ref, masks_ref, *rest,
):
    (
        ends_ref, seeds_ref, totals_ref,
        proj_ref, in_ref, out_ref, long_ref, drive_ref, source_ref, end_ref, seed_ref, dec_ref,
    ) = rest[ndeps:]
    length, width = conv_ref.shape
    places = length // CHUNKS
    prepare(
        rank, states, own_ref, peer_ref, weight_ref, bias_ref, conv_ref, gg_ref, gate_ref, masks_ref,
        proj_ref, in_ref, out_ref, long_ref, drive_ref, source_ref,
    )

    @pl.loop(0, width // LANES)
    def _(group):
        rate2 = -jnp.exp(decay_ref[:, group_at(group)]) * LOG2E
        rates = [jnp.broadcast_to(rate2[n : n + 1, :], (CHUNKS, LANES)) for n in range(states)]
        hidden = [None] * states
        for place in range(places):
            long = long_ref[group, strided(place, length), :]
            drive = drive_ref[group, strided(place, length), :]
            for n in range(states):
                term = tile(in_ref, place, n, states) * drive
                decay = jnp.exp2(long * rates[n])
                dec_ref[(place * states + n) * CHUNKS : (place * states + n + 1) * CHUNKS, :] = decay
                hidden[n] = term if place == 0 else decay * hidden[n] + term
        for n in range(states):
            end_ref[group, n * CHUNKS : (n + 1) * CHUNKS, :] = hidden[n]
        back = [None] * states
        for place in reversed(range(places)):
            long = long_ref[group, strided(place, length), :]
            source = source_ref[group, strided(place, length), :]
            for n in range(states):
                term = tile(out_ref, place, n, states) * source
                term = term if place == places - 1 else back[n] + term
                back[n] = tile(dec_ref, place, n, states) * term
        for n in range(states):
            seed_ref[group, n * CHUNKS : (n + 1) * CHUNKS, :] = back[n]

    for group, at in every(width):
        ends_ref[:, at] = end_ref[group]
        seeds_ref[:, at] = seed_ref[group]
        rate2 = -jnp.exp(decay_ref[:, at]) * LOG2E
        sums = chunk_sums(long_ref, group, length)
        decays = [jnp.exp2(rate2 * sums[c : c + 1, :]) for c in range(CHUNKS)]
        end = jnp.zeros((states, LANES), jnp.float32)
        seed = jnp.zeros((states, LANES), jnp.float32)
        for c in range(CHUNKS):
            end = decays[c] * end + end_ref[group, pl.ds(c, states, stride=CHUNKS), :]
        for c in reversed(range(CHUNKS)):
            seed = decays[c] * seed + seed_ref[group, pl.ds(c, states, stride=CHUNKS), :]
        totals_ref[:states, at] = end.astype(jnp.bfloat16)
        totals_ref[states : 2 * states, at] = seed.astype(jnp.bfloat16)
        totals_ref[2 * states :, at] = two_rows(jnp.sum(sums, axis=0, keepdims=True))


def scan_kernel(
    rank, states, members,
    where_ref, own_ref, peer_ref, weight_ref, bias_ref, decay_ref, conv_ref, gg_ref, gate_ref, masks_ref,
    ends_ref, seeds_ref, near_ref, *rest,
):
    stride, radix = levels(members)[-1]
    far_refs = rest[: radix - 1]
    gated_ref, ggate_ref, small_ref, gconv_ref, gproj_ref = rest[-22:-17]
    (
        proj_ref, in_ref, out_ref, long_ref, true_ref, drive_ref, source_ref,
        start_ref, last_ref, hidden_ref, in_acc, out_acc, scan_ref, gstep_ref, mix_ref, log_ref, dec_ref,
    ) = rest[-17:]
    length, width = conv_ref.shape
    places = length // CHUNKS
    step_pre = prepare(
        rank, states, own_ref, peer_ref, weight_ref, bias_ref, conv_ref, gg_ref, gate_ref, masks_ref,
        proj_ref, in_ref, out_ref, long_ref, drive_ref, source_ref, true_ref,
    )
    in_acc[...] = jnp.zeros_like(in_acc)
    out_acc[...] = jnp.zeros_like(out_acc)
    digit = where_ref[0] // stride % radix
    for group, at in every(width):
        start_ref[group] = ends_ref[:, at]
        last_ref[group] = seeds_ref[:, at]
        rate2 = -jnp.exp(decay_ref[:, at]) * LOG2E
        sums = chunk_sums(long_ref, group, length)
        decays = [jnp.exp2(rate2 * sums[c : c + 1, :]) for c in range(CHUNKS)]
        forward, backward = arrive(
            digit, rate2, near_ref[:, at], [ref[:, at] for ref in far_refs], states
        )
        for c in range(CHUNKS):
            rows = pl.ds(c, states, stride=CHUNKS)
            own = start_ref[group, rows, :]
            start_ref[group, rows, :] = forward
            forward = decays[c] * forward + own
        for c in reversed(range(CHUNKS)):
            rows = pl.ds(c, states, stride=CHUNKS)
            own = last_ref[group, rows, :]
            last_ref[group, rows, :] = backward
            backward = decays[c] * backward + own

    @pl.loop(0, width // LANES)
    def _(group):
        rate2 = -jnp.exp(decay_ref[:, group_at(group)]) * LOG2E
        rates = [jnp.broadcast_to(rate2[n : n + 1, :], (CHUNKS, LANES)) for n in range(states)]
        hidden = [start_ref[group, n * CHUNKS : (n + 1) * CHUNKS, :] for n in range(states)]
        for place in range(places):
            long = long_ref[group, strided(place, length), :]
            drive = drive_ref[group, strided(place, length), :]
            source = source_ref[group, strided(place, length), :]
            rows = slice(place * CHUNKS, (place + 1) * CHUNKS)
            scan = None
            for n in range(states):
                lanes = slice(n * LANES, (n + 1) * LANES)
                decay = jnp.exp2(long * rates[n])
                dec_ref[(place * states + n) * CHUNKS : (place * states + n + 1) * CHUNKS, :] = decay
                value = decay * hidden[n] + tile(in_ref, place, n, states) * drive
                hidden[n] = value
                if place < places - 1:
                    first = (place * states + n) * CHUNKS
                    hidden_ref[first : first + CHUNKS, :] = value
                part = tile(out_ref, place, n, states) * value
                scan = part if n == 0 else scan + part
                out_acc[rows, lanes] += source * value
            scan_ref[group, strided(place, length), :] = scan

        back = [last_ref[group, n * CHUNKS : (n + 1) * CHUNKS, :] for n in range(states)]
        logs = [None] * states
        for place in reversed(range(places)):
            long = long_ref[group, strided(place, length), :]
            true = true_ref[group, strided(place, length), :]
            drive = drive_ref[group, strided(place, length), :]
            source = source_ref[group, strided(place, length), :]
            rows = slice(place * CHUNKS, (place + 1) * CHUNKS)
            gstep = None
            mixed = None
            for n in range(states):
                lanes = slice(n * LANES, (n + 1) * LANES)
                grad = back[n] + tile(out_ref, place, n, states) * source
                previous = (
                    start_ref[group, n * CHUNKS : (n + 1) * CHUNKS, :] if place == 0
                    else tile(hidden_ref, place - 1, n, states)
                )
                back[n] = tile(dec_ref, place, n, states) * grad
                log = back[n] * previous
                part = log * true
                logs[n] = part if logs[n] is None else logs[n] + part
                part = log * rates[n]
                gstep = part if n == 0 else gstep + part
                part = grad * tile(in_ref, place, n, states)
                mixed = part if n == 0 else mixed + part
                in_acc[rows, lanes] += grad * drive
            gstep_ref[group, strided(place, length), :] = gstep
            mix_ref[group, strided(place, length), :] = mixed
        for n in range(states):
            log_ref[group, n * CHUNKS : (n + 1) * CHUNKS, :] = logs[n]

    low = proj_ref[...].astype(jnp.bfloat16)
    small_ref[rank + states + 2 :, :] = jnp.zeros((small_ref.shape[0] - rank - states - 2, width), jnp.float32)
    grad_low = jnp.zeros((length, rank), jnp.float32)
    for group, at in every(width):
        conv = conv_ref[:, at].astype(jnp.float32)
        gate, gg = gate_ref[:, at], gg_ref[:, at]
        source, step, mix = source_ref[group], true_ref[group], mix_ref[group]
        sigma = sigmoid(gate)
        skip = bias_ref[SKIP : SKIP + 1, at]
        scan_out = scan_ref[group] + skip * conv
        gated_ref[:, at] = (scan_out * gate * sigma).astype(jnp.bfloat16)
        ggate = gg * scan_out * sigma * (1.0 + gate * (1.0 - sigma))
        ggate_ref[:, at] = ggate.astype(jnp.bfloat16)
        gconv_ref[:, at] = source * skip + mix * step
        gpre = (gstep_ref[group] * LN2 + mix * conv) * sigmoid(step_pre[:, at])
        gpre_low = gpre.astype(jnp.bfloat16)
        grad_low = grad_low + dot(gpre_low, weight_ref[:, at], ((1,), (1,)))
        small_ref[:rank, at] = dot(low, gpre_low, ((0,), (0,)))[:rank]
        decay = -jnp.exp(decay_ref[:, at])
        logs = log_ref[group, pl.ds(0, states, stride=CHUNKS), :]
        for c in range(1, CHUNKS):
            logs = logs + log_ref[group, pl.ds(c, states, stride=CHUNKS), :]
        first = rank + states
        small_ref[rank:first, at] = logs * decay
        small_ref[first : first + 1, at] = jnp.sum(gpre, axis=0, keepdims=True)
        small_ref[first + 1 : first + 2, at] = jnp.sum(source * conv, axis=0, keepdims=True)

    wide = states * LANES
    source_state = lax.broadcasted_iota(jnp.int32, (wide, LANES), 0) // LANES
    column = lax.broadcasted_iota(jnp.int32, (wide, LANES), 1)
    total = jnp.zeros((length, LANES), jnp.float32)
    for acc, first in ((in_acc, rank), (out_acc, rank + states)):
        pick = jnp.where(source_state + first == column, 1.0, 0.0).astype(jnp.bfloat16)
        value = acc[...]
        high = value.astype(jnp.bfloat16)
        rest = (value - high.astype(jnp.float32)).astype(jnp.bfloat16)
        total = total + dot(high, pick, ((1,), (0,))) + dot(rest, pick, ((1,), (0,)))
    scan_ref[0] = total
    for place in range(places):
        mix_ref[0, strided(place, length), :] = scan_ref[0, place * CHUNKS : (place + 1) * CHUNKS, :]
    gproj_ref[...] = mix_ref[0]
    gproj_ref[:, :rank] += grad_low


def column_block(rows, width=LANES):
    return pl.BlockSpec((rows, width), lambda g: (0, g))


def whole(*shape):
    return pl.BlockSpec(shape, lambda g: (0,) * len(shape))


def run_ends(own, peer, weight, stacked, decay_log, conv, gg, gate, masks, deps=()):
    length, width = conv.shape
    rank, states = weight.shape[0], decay_log.shape[0]
    tall = length // CHUNKS * states * CHUNKS
    f32 = jnp.float32
    vmem = pl.BlockSpec(memory_space=pltpu.VMEM)
    return pl.pallas_call(
        functools.partial(ends_kernel, rank, states, len(deps)),
        in_specs=[vmem] * 9 + [pl.BlockSpec(memory_space=pl.ANY) for _ in deps], out_specs=[vmem] * 3,
        out_shape=[
            jax.ShapeDtypeStruct((states * CHUNKS, width), f32),
            jax.ShapeDtypeStruct((states * CHUNKS, width), f32),
            jax.ShapeDtypeStruct((2 * states + 2 * CHUNKS, width), jnp.bfloat16),
        ],
        scratch_shapes=[pltpu.VMEM((length, LANES), f32)]
        + [pltpu.VMEM((tall, LANES), f32)] * 2 + [pltpu.VMEM((width // LANES, length, LANES), f32)] * 3
        + [pltpu.VMEM((width // LANES, states * CHUNKS, LANES), f32)] * 2
        + [pltpu.VMEM((tall, LANES), f32)],
        compiler_params=params(), cost_estimate=cost(8), name="ends",
    )(own, peer, weight, stacked, decay_log, conv, gg, gate, masks, *deps)


def run_scan(where, own, peer, weight, stacked, decay_log, conv, gg, gate, masks, ends, seeds, near, far, deps):
    length, width = conv.shape
    members = lax.axis_size("seq")
    rank, states = weight.shape[0], decay_log.shape[0]
    places = length // CHUNKS
    tall = places * states * CHUNKS
    f32, bf16 = jnp.float32, jnp.bfloat16
    groups = pltpu.VMEM((width // LANES, length, LANES), f32)
    chunks = pltpu.VMEM((width // LANES, states * CHUNKS, LANES), f32)
    table = pltpu.VMEM((tall, LANES), f32)
    vmem = pl.BlockSpec(memory_space=pltpu.VMEM)
    return pl.pallas_call(
        functools.partial(scan_kernel, rank, states, members),
        in_specs=[pl.BlockSpec(memory_space=pltpu.SMEM)] + [vmem] * (12 + len(far))
        + [pl.BlockSpec(memory_space=pl.ANY) for _ in deps],
        out_specs=[vmem] * 5,
        out_shape=[
            jax.ShapeDtypeStruct((length, width), bf16), jax.ShapeDtypeStruct((length, width), bf16),
            jax.ShapeDtypeStruct((padded(rank + states + 2, 8), width), f32),
            jax.ShapeDtypeStruct((length, width), f32),
            jax.ShapeDtypeStruct((length, LANES), f32),
        ],
        scratch_shapes=[pltpu.VMEM((length, LANES), f32), table, table] + [groups] * 4 + [chunks] * 2
        + [table] + [pltpu.VMEM((length, states * LANES), f32)] * 2 + [groups] * 3 + [chunks, table],
        compiler_params=params(), cost_estimate=cost(15), name="scan",
    )(where, own, peer, weight, stacked, decay_log, conv, gg, gate, masks, ends, seeds, near, *far, *deps)


def levels(members):
    found, stride = [], 1
    while stride < members:
        radix = 4 if members // stride % 4 == 0 else 2
        found.append((stride, radix))
        stride *= radix
    return found


def chosen(refs, own, hop):
    value = own
    for mask, ref in enumerate(refs, 1):
        value = jnp.where(hop == mask, ref.astype(jnp.float32), value)
    return value


def arrive(digit, rate2, near, far, states):
    radix = len(far) + 1
    carry = jnp.zeros_like(rate2)
    incoming = jnp.zeros_like(rate2)
    blank = jnp.zeros(far[0].shape, jnp.float32)
    for number in range(radix):
        value = chosen(far, blank, digit ^ number)
        decay = jnp.exp2(rate2 * (value[states : states + 1] + value[states + 1 : states + 2]))
        carry = jnp.where(number < digit, decay * carry + value[:states], carry)
    for number in reversed(range(radix)):
        value = chosen(far, blank, digit ^ number)
        decay = jnp.exp2(rate2 * (value[states : states + 1] + value[states + 1 : states + 2]))
        incoming = jnp.where(number > digit, decay * incoming + value[:states], incoming)
    before, behind = near[2 * states : 2 * states + 1], near[2 * states + 1 : 2 * states + 2]
    carry = near[:states] + jnp.exp2(rate2 * before) * carry
    incoming = near[states : 2 * states] + jnp.exp2(rate2 * behind) * incoming
    return carry, incoming


def fold_kernel(states, level, members, start, where_ref, decay_ref, *refs):
    stride, radix = levels(members)[level]
    next_stride, next_radix = levels(members)[level + 1]
    last = level + 2 == len(levels(members))
    digit = where_ref[0] // stride % radix
    if not start:
        old = refs[0][...]
        refs = refs[1:]
    own = refs[0][...]
    got = [ref[...] for ref in refs[1:radix]]
    near_ref, outs = refs[radix], refs[radix + 1 :]
    rate2 = -jnp.exp(decay_ref[...]) * LOG2E
    own = own.astype(jnp.float32)
    values = [chosen(got, own, digit ^ number) for number in range(radix)]
    first = 2 * states
    sums = [value[first : first + 1] + value[first + 1 : first + 2] for value in values]
    decays = [jnp.exp2(rate2 * one) for one in sums]
    zero, line = jnp.zeros_like(rate2), jnp.zeros_like(sums[0])
    end, seed, carry, incoming, before, behind, total = zero, zero, zero, zero, line, line, line
    for number in range(radix):
        part = values[number][:states]
        end = decays[number] * end + part
        carry = jnp.where(number < digit, decays[number] * carry + part, carry)
        before = jnp.where(number < digit, before + sums[number], before)
        total = total + sums[number]
    for number in reversed(range(radix)):
        part = values[number][states : 2 * states]
        seed = decays[number] * seed + part
        incoming = jnp.where(number > digit, decays[number] * incoming + part, incoming)
        behind = jnp.where(number > digit, behind + sums[number], behind)
    if not start:
        old_before, old_behind = old[2 * states : 2 * states + 1], old[2 * states + 1 : 2 * states + 2]
        carry = old[:states] + jnp.exp2(rate2 * old_before) * carry
        incoming = old[states : 2 * states] + jnp.exp2(rate2 * old_behind) * incoming
        before, behind = before + old_before, behind + old_behind
    pad = jnp.zeros((6, line.shape[1]), jnp.float32)
    near_ref[...] = jnp.concatenate([carry, incoming, before, behind, pad], axis=0)
    tail = two_rows(total)
    if last:
        next_digit = where_ref[0] // next_stride % next_radix
        for mask, out in enumerate(outs, 1):
            value = jnp.where(next_digit < (next_digit ^ mask), end, seed)
            out[:states, :] = value.astype(jnp.bfloat16)
            out[states:, :] = tail
    else:
        outs[0][: 2 * states, :] = jnp.concatenate([end, seed], axis=0).astype(jnp.bfloat16)
        outs[0][2 * states :, :] = tail


def run_fold(level, where, decay_log, near, parts):
    states, width = decay_log.shape
    members = lax.axis_size("seq")
    f32, bf16 = jnp.float32, jnp.bfloat16
    vmem = pl.BlockSpec(memory_space=pltpu.VMEM)
    tall = jax.ShapeDtypeStruct((2 * states + 8, width), f32)
    if level + 2 == len(levels(members)):
        sent = [jax.ShapeDtypeStruct((states + 2 * CHUNKS, width), bf16)] * (levels(members)[-1][1] - 1)
    else:
        sent = [jax.ShapeDtypeStruct((2 * states + 2 * CHUNKS, width), bf16)]
    extra = [] if near is None else [near]
    return pl.pallas_call(
        functools.partial(fold_kernel, states, level, members, near is None),
        in_specs=[pl.BlockSpec(memory_space=pltpu.SMEM)] + [vmem] * (1 + len(extra) + len(parts)),
        out_specs=[vmem] * (1 + len(sent)),
        out_shape=[tall] + sent,
        compiler_params=params(), cost_estimate=cost(2), name="fold",
    )(where, decay_log, *extra, *parts)


def exchange(where, totals, decay_log):
    members = lax.axis_size("seq")
    found = levels(members)
    near = None
    for level, (stride, radix) in enumerate(found[:-1]):
        parts = [totals] + [hop(totals, mask * stride) for mask in range(1, radix)]
        near, *sent = run_fold(level, where, decay_log, near, parts)
        totals = sent[0]
    stride, radix = found[-1]
    return near, [hop(one, mask * stride) for mask, one in enumerate(sent, 1)]


def taps_kernel(
    kernel, ndeps,
    own_ref, peer_ref, conv_ref, in_ref, ext_ref, weight_ref, gconv_ref, taps_ref, params_ref, masks_ref,
    *rest,
):
    main_ref, rim_ref, small_ref = rest[ndeps:]
    length, total_width = conv_ref.shape
    width = weight_ref.shape[0]
    grad_proj = (own_ref[...] + peer_ref[...]).astype(jnp.bfloat16)
    masks = [columns(masks_ref, tap) for tap in range(kernel)]
    near_row = lax.broadcasted_iota(jnp.int32, (CHUNKS, LANES), 0)
    token = lax.broadcasted_iota(jnp.int32, (length, LANES), 0)
    for group in range(total_width // LANES):
        at = slice(group * LANES, (group + 1) * LANES)
        taps = [taps_ref[tap : tap + 1, at] for tap in range(kernel)]
        conv_in = in_ref[:, at].astype(jnp.float32)
        ext = ext_ref[:, at]
        seen = [shifted(conv_in, ext, kernel - 1 - tap) * masks[tap] for tap in range(kernel)]
        pre = jnp.broadcast_to(params_ref[TAP_BIAS : TAP_BIAS + 1, at], (length, LANES))
        for tap in range(kernel):
            pre = pre + taps[tap] * seen[tap]
        small_ref[:width, at] = dot(grad_proj, conv_ref[:, at], ((0,), (0,)))[:width]
        grad = gconv_ref[:, at] + dot(grad_proj[:, :width], weight_ref[:, at], ((1,), (0,)))
        grad = grad * silu_grad(pre)
        lines = []
        main = jnp.zeros((length, LANES), jnp.float32)
        rim = jnp.zeros((CHUNKS, LANES), jnp.float32)
        for tap in range(kernel):
            back = kernel - 1 - tap
            lines.append(jnp.sum(grad * seen[tap], axis=0, keepdims=True))
            masked = grad * masks[tap] * taps[tap]
            if back == 0:
                main = main + masked
            else:
                moved = pltpu.roll(masked, length - back, 0)
                main = main + jnp.where(token < length - back, moved, 0.0)
                rim = rim + jnp.where(
                    near_row >= CHUNKS - back, pltpu.roll(masked[:CHUNKS], CHUNKS - back, 0), 0.0
                )
        main_ref[:, at] = main
        rim_ref[:, at] = rim
        lines.append(jnp.sum(grad, axis=0, keepdims=True))
        lines.append(jnp.zeros((small_ref.shape[0] - width - kernel - 1, LANES), jnp.float32))
        small_ref[width:, at] = jnp.concatenate(lines, axis=0)


def run_taps(own, peer, conv, conv_in, ext, weight, gconv, taps, stacked, masks, deps):
    length, width = conv.shape
    kernel = taps.shape[0]
    f32 = jnp.float32
    vmem = pl.BlockSpec(memory_space=pltpu.VMEM)
    return pl.pallas_call(
        functools.partial(taps_kernel, kernel, len(deps)),
        in_specs=[vmem] * 10 + [pl.BlockSpec(memory_space=pl.ANY) for _ in deps],
        out_specs=[vmem] * 3,
        out_shape=[
            jax.ShapeDtypeStruct((length, width), f32),
            jax.ShapeDtypeStruct((CHUNKS, width), f32),
            jax.ShapeDtypeStruct((padded(weight.shape[0] + kernel + 2, 8), width), f32),
        ],
        compiler_params=params(), cost_estimate=cost(4), name="taps",
    )(own, peer, conv, conv_in, ext, weight, gconv, taps, stacked, masks, *deps)


def inputs_kernel(
    gain_row, ndeps, where_ref, main_ref, rim_ref, weight_ref, gate_part_ref, tokens_ref,
    first_small_ref, second_small_ref, *rest,
):
    x_first_ref, x_second_ref, y_first_ref, y_second_ref, own_ref, normed_ref, small_ref = rest[ndeps:]
    bf16 = jnp.bfloat16
    length, width = main_ref.shape
    half = length // 2
    main = main_ref[...]
    low = jnp.concatenate(
        [main[: length - CHUNKS], main[length - CHUNKS :] + rim_ref[...]], axis=0
    ).astype(bf16)
    normed = dot(low, weight_ref[...], ((1,), (1,))) + gate_part_ref[...]
    normed_ref[...] = normed
    tokens = tokens_ref[...].astype(jnp.float32)
    gain = jnp.sum(normed * tokens * inverse_rms(tokens), axis=0, keepdims=True)
    second = second_small_ref[...]
    number = lax.broadcasted_iota(jnp.int32, second.shape, 0)
    second = jnp.where(number == gain_row, gain, second)
    small = jnp.concatenate([first_small_ref[...], second], axis=0)
    count = small_ref.shape[1]
    blank = jnp.zeros((PLANE * count - small.shape[0], width), jnp.float32)
    small = jnp.concatenate([small, blank], axis=0)
    for quarter in range(PLANE):
        small_ref[quarter] = small[quarter * count : (quarter + 1) * count]
    place = where_ref[0] % PLANE
    own_ref[...] = small_ref[place]
    across = small_ref[jnp.bitwise_xor(place, 3)].astype(bf16)
    x_first_ref[...] = jnp.concatenate([low[:half], across], axis=0)
    x_second_ref[...] = jnp.concatenate([low[half:], small_ref[jnp.bitwise_xor(place, 1)].astype(bf16)], axis=0)
    y_first_ref[...] = jnp.concatenate([low[:half], small_ref[jnp.bitwise_xor(place, 2)].astype(bf16)], axis=0)
    y_second_ref[...] = low[half:]


def run_inputs(gain_row, where, main, rim, weight, gate_part, tokens, first_small, second_small, deps):
    length, width = main.shape
    f32, bf16 = jnp.float32, jnp.bfloat16
    vmem = pl.BlockSpec(memory_space=pltpu.VMEM)
    count = padded(first_small.shape[0] + second_small.shape[0], 8 * PLANE) // PLANE
    tall = jax.ShapeDtypeStruct((length // 2 + count, width), bf16)
    return pl.pallas_call(
        functools.partial(inputs_kernel, gain_row, len(deps)),
        in_specs=[pl.BlockSpec(memory_space=pltpu.SMEM)] + [vmem] * 7
        + [pl.BlockSpec(memory_space=pl.ANY) for _ in deps],
        out_specs=[vmem] * 6,
        out_shape=[
            tall, tall, tall, jax.ShapeDtypeStruct((length // 2, width), bf16),
            jax.ShapeDtypeStruct((count, width), f32),
            jax.ShapeDtypeStruct((length, weight.shape[0]), f32),
        ],
        scratch_shapes=[pltpu.VMEM((PLANE, count, width), f32)],
        compiler_params=params(), cost_estimate=cost(3), name="inputs",
    )(where, main, rim, weight, gate_part, tokens, first_small, second_small, *deps)


def products_kernel(halves, members, ndeps, where_ref, *rest):
    early = rest[:PLANE]
    late = rest[PLANE : 3 * PLANE]
    small = len(halves) == 1
    if small:
        own_ref = rest[3 * PLANE]
        rest = rest[1:]
    kept_ref, *small_refs, sent_ref, total_ref = rest[3 * PLANE + ndeps :]
    lines = members // PLANE
    share, length = early[0].shape[0] // 2, early[0].shape[1]
    rows = share // lines
    for number, half in enumerate(halves):
        total = None
        for mask in range(PLANE):
            if small:
                tops = [late[2 * mask + part][: length // 2, :] for part in range(2)]
                block = jnp.concatenate(tops, axis=0)
            else:
                block = late[2 * mask + number][...]
            part = dot(early[mask][half * share : (half + 1) * share, :], block, ((1,), (0,)))
            total = part if total is None else total + part
        for line in range(lines):
            total_ref[line, number * rows : (number + 1) * rows, :] = total[line * rows : (line + 1) * rows]
    line = None
    if small:
        line = own_ref[...]
        for ref in (late[3], late[4], late[6]):
            line = line + ref[length // 2 :, :].astype(jnp.float32)
    send(where_ref[0], 0, total_ref, line, kept_ref, small_refs, sent_ref)


def send(device, level, total_ref, line, kept_ref, small_refs, sent_ref):
    digit = device // (PLANE << level) % 2
    pieces = []
    if line is not None:
        small_refs[0][...] = line
        pieces.append(line)
    for block in range(total_ref.shape[0] // 2):
        kept_ref[block] = total_ref[2 * block + digit]
        pieces.append(total_ref[2 * block + 1 - digit])
    sent_ref[...] = jnp.concatenate(pieces, axis=0).astype(jnp.bfloat16)


def gather_kernel(level, count, small, ndeps, where_ref, kept_ref, *refs):
    total = kept_ref[...]
    line = None
    first = 0
    if small:
        first = refs[0].shape[0]
        line = refs[0][...] + refs[1][:first, :].astype(jnp.float32)
        refs = refs[1:]
    got = refs[0][first:, :].astype(jnp.float32)
    refs = refs[1 + ndeps :]
    left, rows, width = total.shape
    pieces = [total[index] + got[index * rows : (index + 1) * rows] for index in range(left)]
    if left > 1:
        total_ref = refs[-1]
        for index, piece in enumerate(pieces):
            total_ref[index] = piece
        send(where_ref[0], level + 1, total_ref, line, refs[0], refs[1:-2], refs[-2])
        return
    for index in range(count):
        refs[index][...] = pieces[0][index * (rows // count) : (index + 1) * (rows // count)]
    if small:
        refs[count][...] = line.astype(jnp.bfloat16)


def gather_plane(first, second, x_first, x_second, y_first, y_second):
    near = [first, second, hop(x_first, 1), hop(x_second, 1), hop(y_first, 2), hop(y_second, 2)]
    return near + [hop(near[2], 2), hop(near[5], 1)]


def multiply(halves, where, early, late, small, deps):
    members = lax.axis_size("seq")
    lines = members // PLANE
    width = late[0].shape[1]
    rows = len(halves) * (early[0].shape[0] // 2 // lines)
    vmem = pl.BlockSpec(memory_space=pltpu.VMEM)
    out_shape = level_shapes(lines, rows, width, small)
    extra = [] if small is None else [small]
    return pl.pallas_call(
        functools.partial(products_kernel, halves, members, len(deps)),
        in_specs=[pl.BlockSpec(memory_space=pltpu.SMEM)] + [vmem] * (3 * PLANE + len(extra))
        + [pl.BlockSpec(memory_space=pl.ANY) for _ in deps],
        out_specs=[vmem] * len(out_shape), out_shape=out_shape,
        scratch_shapes=[pltpu.VMEM((lines, rows, width), jnp.float32)],
        compiler_params=params(), cost_estimate=cost(4), name="products",
    )(where, *early, *late, *extra, *deps)


def level_shapes(left, rows, width, small):
    kept = jax.ShapeDtypeStruct((left // 2, rows, width), jnp.float32)
    if small is None:
        return [kept, jax.ShapeDtypeStruct((left // 2 * rows, width), jnp.bfloat16)]
    sent = jax.ShapeDtypeStruct((small.shape[0] + left // 2 * rows, width), jnp.bfloat16)
    return [kept, jax.ShapeDtypeStruct(small.shape, jnp.float32), sent]


def add_line(level, where, parts, count, deps=()):
    f32, bf16 = jnp.float32, jnp.bfloat16
    kept, *small, sent = parts
    vmem = pl.BlockSpec(memory_space=pltpu.VMEM)
    got = hop(sent, PLANE << level)
    left, rows, width = kept.shape
    scratch = []
    if left > 1:
        out_shape = level_shapes(left, rows, width, small[0] if small else None)
        scratch = [pltpu.VMEM((left, rows, width), f32)]
    else:
        out_shape = [jax.ShapeDtypeStruct((rows // count, width), f32)] * count
        out_shape = out_shape + [jax.ShapeDtypeStruct(one.shape, bf16) for one in small]
    return pl.pallas_call(
        functools.partial(gather_kernel, level, count, bool(small), len(deps)),
        in_specs=[pl.BlockSpec(memory_space=pltpu.SMEM)] + [vmem] * (2 + len(small))
        + [pl.BlockSpec(memory_space=pl.ANY) for _ in deps],
        out_specs=[vmem] * len(out_shape), out_shape=out_shape, scratch_shapes=scratch,
        compiler_params=params(), cost_estimate=cost(2), name="gather",
    )(where, kept, *small, got, *deps)


def project_kernel(gated_ref, ggate_ref, out_w_ref, gate_w_ref, branch_ref, part_ref):
    branch_ref[...] = dot(gated_ref[...], out_w_ref[...], ((1,), (0,)))
    part_ref[...] = dot(ggate_ref[...], gate_w_ref[...], ((1,), (1,)))


def run_project(gated, ggate, out_w, gate_w):
    length = gated.shape[0]
    width, model = out_w.shape
    out = jax.ShapeDtypeStruct((length, model), jnp.float32)
    vmem = pl.BlockSpec(memory_space=pltpu.VMEM)
    return pl.pallas_call(
        project_kernel, in_specs=[vmem] * 4, out_specs=[vmem] * 2, out_shape=[out, out],
        compiler_params=params(), cost_estimate=cost(5), name="project",
    )(gated, ggate, out_w, gate_w)


def place_kernel(counts, where_ref, *refs):
    quarters, outs, (table_ref,) = refs[:PLANE], refs[PLANE:-1], refs[-1:]
    place = where_ref[0] % PLANE
    for mask, ref in enumerate(quarters):
        table_ref[jnp.bitwise_xor(place, mask)] = ref[...].astype(jnp.float32)
    table = jnp.concatenate([table_ref[quarter] for quarter in range(PLANE)], axis=0)
    for out, (first, count) in zip(outs, counts, strict=True):
        value = table[first : first + count]
        out[...] = value.reshape(value.shape[1]) if count == 1 else value


def run_place(where, own, counts):
    count, width = own.shape
    f32 = jnp.float32
    x, y = hop(own, 1), hop(own, 2)
    vmem = pl.BlockSpec(memory_space=pltpu.VMEM)
    shapes = [(width,) if number == 1 else (number, width) for _, number in counts]
    return pl.pallas_call(
        functools.partial(place_kernel, counts),
        in_specs=[pl.BlockSpec(memory_space=pltpu.SMEM)] + [vmem] * PLANE,
        out_specs=[vmem] * len(shapes),
        out_shape=[jax.ShapeDtypeStruct(shape, f32) for shape in shapes],
        scratch_shapes=[pltpu.VMEM((PLANE, count, width), f32)],
        compiler_params=params(), cost_estimate=cost(3), name="place",
    )(where, own, x, y, hop(x, 2))


def leave_kernel(tokens_ref, cot_ref, params_ref, branch_ref, branch_peer_ref, own_ref, peer_ref, mixed_ref, grad_ref):
    tokens = tokens_ref[...].astype(jnp.float32)
    mixed_ref[...] = (tokens + (branch_ref[...] + branch_peer_ref[...])).astype(jnp.bfloat16)
    scale = inverse_rms(tokens)
    scaled = (own_ref[...] + peer_ref[...]) * row(params_ref, GAIN)
    mean = jnp.mean(scaled * tokens, axis=1, keepdims=True)
    grad = cot_ref[...].astype(jnp.float32) + scale * scaled
    grad_ref[...] = grad - tokens * (scale * scale * scale * mean)


def run_leave(tokens, cot, stacked, branch, branch_peer, own, peer):
    vmem = pl.BlockSpec(memory_space=pltpu.VMEM)
    return pl.pallas_call(
        leave_kernel, in_specs=[vmem] * 7, out_specs=[vmem] * 2,
        out_shape=[
            jax.ShapeDtypeStruct(tokens.shape, jnp.bfloat16),
            jax.ShapeDtypeStruct(tokens.shape, jnp.float32),
        ],
        compiler_params=params(), cost_estimate=cost(3), name="leave",
    )(tokens, cot, stacked, branch, branch_peer, own, peer)


def from_behind(block, axis, distance):
    devices = range(lax.axis_size(axis))
    route = [(i - distance, i) for i in devices if i - distance in devices]
    return lax.ppermute(block, axis, route)


def swap(block):
    return lax.ppermute(block, "tp", [(0, 1), (1, 0)])


def hop(block, mask):
    members = lax.axis_size("seq")
    return lax.ppermute(block, "seq", [(i, i ^ mask) for i in range(members)])


def shards(
    tokens, norm_gain, in_conv_weight, in_gate_weight, conv_weight, conv_bias, scan_proj_weight,
    step_proj_weight, step_bias, decay_log, skip_gain, out_weight, segment_ids, cotangent,
):
    f32 = jnp.float32
    length, model = tokens.shape
    rank = step_proj_weight.shape[0]
    states = decay_log.shape[0]
    kernel = conv_weight.shape[0]
    width = conv_weight.shape[1]
    members = lax.axis_size("seq")
    device = lax.axis_index("seq")
    where = jnp.stack([device, lax.axis_index("tp")]).astype(jnp.int32)
    scan_width = rank + 2 * states
    padded_ids = jnp.concatenate([jnp.full((kernel,), -1, jnp.int32), segment_ids])
    near_ids = lax.dynamic_slice_in_dim(padded_ids, device * length, length + kernel)
    masks = jnp.stack(
        [near_ids[kernel:] == near_ids[tap + 1 : tap + 1 + length] for tap in range(kernel)]
    ).astype(f32)
    scan_weight = scan_proj_weight.T

    normed, rim_tokens, kept_early, *sent_early = run_early(where, tokens, cotangent, norm_gain)
    rim_tokens = from_behind(rim_tokens, "seq", 1)
    early = [kept_early] + [hop(one, mask) for mask, one in enumerate(sent_early, 1)]
    conv_in, ext, conv_out, gate_in, grad_gated, own, stacked = run_enter(
        normed, rim_tokens, cotangent, (conv_bias, step_bias, skip_gain, norm_gain), masks,
        in_conv_weight, in_gate_weight, out_weight, conv_weight, scan_weight,
    )
    peer = swap(own)
    ends, seeds, totals = run_ends(
        own, peer, step_proj_weight, stacked, decay_log, conv_out, grad_gated, gate_in, masks,
        early[1:],
    )
    near, far = exchange(where, totals, decay_log)
    gated, ggate, first_small, grad_conv, low_own = run_scan(
        where, own, peer, step_proj_weight, stacked, decay_log, conv_out, grad_gated, gate_in, masks,
        ends, seeds, near, far, (),
    )
    low_peer = swap(low_own)
    main, rim, second_small = run_taps(
        low_own, low_peer, conv_out, conv_in, ext, scan_weight, grad_conv, conv_weight, stacked, masks, (),
    )
    rim = from_behind(rim, "seq", -1)
    first_late = gather_plane(gated, ggate, gated, ggate, gated, ggate)
    branch_own, gate_part = run_project(gated, ggate, out_weight, in_gate_weight)
    *sent_late, small, normed_own = run_inputs(
        scan_width + kernel + 1, where, main, rim, in_conv_weight, gate_part, tokens, first_small,
        second_small, first_late[2:6],
    )
    second_late = gather_plane(*sent_late[:2], *sent_late)
    mixed_out, input_grad = run_leave(
        tokens, cotangent, stacked, branch_own, swap(branch_own), normed_own, swap(normed_own)
    )
    first = multiply((1, 0), where, early, first_late, None, (normed_own,))
    second = multiply((0,), where, early, second_late, small, first[:1])
    lines = members // PLANE
    for level in range(lines.bit_length() - 1):
        first = add_line(level, where, first, 2, () if level == 0 else ())
        second = add_line(level, where, second, 1, () if level == 0 else ())
    out_grad, in_gate_grad = first
    in_conv_grad, small = second
    first_row = first_small.shape[0]
    last_row = first_row + scan_width
    (
        step_proj_grad, decay_log_grad, step_bias_grad, skip_grad, scan_proj_grad, conv_weight_grad,
        conv_bias_grad, gain_grad,
    ) = run_place(
        where, small,
        (
            (0, rank), (rank, states), (rank + states, 1), (rank + states + 1, 1), (first_row, scan_width),
            (last_row, kernel), (last_row + kernel, 1), (last_row + kernel + 1, 1),
        ),
    )
    gain_grad = gain_grad + swap(gain_grad)
    return (
        mixed_out, input_grad, gain_grad, in_conv_grad, in_gate_grad, conv_weight_grad,
        conv_bias_grad, scan_proj_grad.T, step_proj_grad, step_bias_grad, decay_log_grad, skip_grad,
        out_grad.T,
    )


def solution(mesh):
    in_specs = (
        P("seq", None), P(), P(None, "tp"), P(None, "tp"), P(None, "tp"), P("tp"), P("tp", None),
        P(None, "tp"), P("tp"), P(None, "tp"), P("tp"), P("tp", None), P(), P("seq", None),
    )
    out_specs = (
        P("seq", None), P("seq", None), P(), P("seq", "tp"), P("seq", "tp"), P(None, "tp"), P("tp"),
        P("tp", None), P(None, "tp"), P("tp"), P(None, "tp"), P("tp"), P("tp", "seq"),
    )
    return jax.shard_map(shards, mesh=mesh, in_specs=in_specs, out_specs=out_specs, check_vma=False)
```

```python
import functools

import jax
import jax.numpy as jnp
from jax import lax
from jax.experimental import pallas as pl
from jax.experimental.pallas import tpu as pltpu
from jax.sharding import PartitionSpec as P

NORM_EPS = 1e-05
LANES = 128
PLANE = 4
CHUNKS = 8
LOG2E = 1.4426950408889634
LN2 = 0.6931471805599453
FAR = 1e30
MIB = 1024 * 1024
TAP_BIAS, STEP_BIAS, SKIP, GAIN = 0, 1, 2, 3


def sigmoid(value):
    return 1.0 / (1.0 + jnp.exp(-value))


def silu_grad(value):
    sigma = sigmoid(value)
    return sigma * (1.0 + value * (1.0 - sigma))


def softplus(value):
    small = jnp.exp(-jnp.abs(value))
    series = small * (1.0 - small * (0.5 - small * (1.0 / 3.0 - small * 0.25)))
    return jnp.maximum(value, 0.0) + jnp.where(small < 0.01, series, jnp.log(1.0 + small))


def dot(first, second, contract):
    return lax.dot_general(
        first, second, (contract, ((), ())), preferred_element_type=jnp.float32
    )


def strided(number, length):
    return pl.ds(number, CHUNKS, stride=length // CHUNKS)


def spread(proj_ref, first, table_ref, states, length):
    for place in range(length // CHUNKS):
        rows = proj_ref[strided(place, length), :]
        for state in range(states):
            column = rows[:, first + state : first + state + 1]
            start = (place * states + state) * CHUNKS
            table_ref[start : start + CHUNKS, :] = jnp.broadcast_to(column, (CHUNKS, LANES))


def tile(ref, place, state, states):
    start = (place * states + state) * CHUNKS
    return ref[start : start + CHUNKS, :]


def padded(number, unit):
    return -(-number // unit) * unit


def row(ref, number):
    return ref[number : number + 1, :]


def inverse_rms(tokens):
    return lax.rsqrt(jnp.mean(tokens * tokens, axis=1, keepdims=True) + NORM_EPS)


def columns(masks_ref, tap):
    return jnp.broadcast_to(row(masks_ref, tap), (LANES, masks_ref.shape[1])).T


def two_rows(line):
    high = line.astype(jnp.bfloat16).astype(jnp.float32)
    number = lax.broadcasted_iota(jnp.int32, (2 * CHUNKS, line.shape[1]), 0)
    return jnp.where(number == 0, high, jnp.where(number == 1, line - high, 0.0)).astype(jnp.bfloat16)


def group_at(group):
    return pl.ds(pl.multiple_of(group * LANES, LANES), LANES)


def params():
    return pltpu.CompilerParams(vmem_limit_bytes=64 * MIB)


def cost(us):
    return pl.CostEstimate(flops=0, bytes_accessed=int(us * 3e6), transcendentals=0)


def shifted(block, rim, back):
    if back == 0:
        return block
    moved = pltpu.roll(block, back, 0)
    near = lax.broadcasted_iota(jnp.int32, (CHUNKS, block.shape[1]), 0)
    top = jnp.where(near < back, pltpu.roll(rim, back, 0), moved[:CHUNKS])
    return jnp.concatenate([top, moved[CHUNKS:]], axis=0)


def enter_kernel(
    kernel, scan_width,
    normed_ref, rim_tokens_ref, cot_ref, tap_bias_ref, step_bias_ref, skip_ref, gain_ref, masks_ref,
    conv_w_ref, gate_w_ref, out_w_ref, taps_ref, weight_ref,
    conv_ref, rim_ref, out_ref, gate_ref, gg_ref, proj_ref, stacked_ref,
    both_ref, mask_ref,
):
    length = normed_ref.shape[0]
    block = conv_w_ref.shape[1]

    @pl.when(pl.program_id(0) == 0)
    def _():
        for number, ref in enumerate((tap_bias_ref, step_bias_ref, skip_ref, gain_ref)):
            stacked_ref[number : number + 1, :] = ref[...].reshape(1, ref.shape[0])
        for tap in range(kernel):
            mask_ref[tap] = columns(masks_ref, tap)
        gain = row(stacked_ref, GAIN)
        rim = rim_tokens_ref[...].astype(jnp.float32)
        rim = (rim * inverse_rms(rim) * gain).astype(jnp.bfloat16)
        both_ref[:length, :] = normed_ref[...]
        both_ref[length:, :] = jnp.concatenate([rim, rim], axis=0)
        proj_ref[...] = jnp.zeros_like(proj_ref)

    normed = both_ref[...]
    conv_in = dot(normed, conv_w_ref[...], ((1,), (0,))).astype(jnp.bfloat16)
    conv_ref[...] = conv_in[:length]
    wide = conv_in[:length].astype(jnp.float32)
    rim = conv_in[length : length + CHUNKS].astype(jnp.float32)
    rim_ref[...] = rim
    at = pl.ds(pl.multiple_of(pl.program_id(0) * block, LANES), block)
    total = jnp.broadcast_to(stacked_ref[TAP_BIAS : TAP_BIAS + 1, at], (length, block))
    for tap in range(kernel):
        mask = jnp.concatenate([mask_ref[tap]] * (block // LANES), axis=1)
        total = total + row(taps_ref, tap) * shifted(wide, rim, kernel - 1 - tap) * mask
    out = (total * sigmoid(total)).astype(jnp.bfloat16)
    out_ref[...] = out
    proj_ref[:, :scan_width] += dot(out, weight_ref[...], ((1,), (1,)))
    gate_ref[...] = dot(normed[:length], gate_w_ref[...], ((1,), (0,)))
    gg_ref[...] = dot(cot_ref[...], out_w_ref[...], ((1,), (1,)))


def run_enter(normed, rim, cot, vectors, masks, conv_w, gate_w, out_w, taps, weight):
    length, model = normed.shape
    width = conv_w.shape[1]
    block = 3 * LANES
    f32, bf16 = jnp.float32, jnp.bfloat16
    flat = pl.BlockSpec(memory_space=pltpu.VMEM)
    return pl.pallas_call(
        functools.partial(enter_kernel, taps.shape[0], weight.shape[0]),
        grid=(width // block,),
        in_specs=[whole(length, model), whole(CHUNKS, model), whole(length, model)] + [flat] * 4 + [
            whole(*masks.shape), column_block(model, block), column_block(model, block),
            pl.BlockSpec((block, model), lambda g: (g, 0)), column_block(taps.shape[0], block),
            column_block(weight.shape[0], block),
        ],
        out_specs=[
            column_block(length, block), column_block(CHUNKS, block), column_block(length, block),
            column_block(length, block), column_block(length, block), whole(length, LANES),
            whole(len(vectors), width),
        ],
        out_shape=[
            jax.ShapeDtypeStruct((length, width), bf16), jax.ShapeDtypeStruct((CHUNKS, width), f32),
            jax.ShapeDtypeStruct((length, width), bf16), jax.ShapeDtypeStruct((length, width), f32),
            jax.ShapeDtypeStruct((length, width), f32), jax.ShapeDtypeStruct((length, LANES), f32),
            jax.ShapeDtypeStruct((len(vectors), width), f32),
        ],
        scratch_shapes=[
            pltpu.VMEM((length + 2 * CHUNKS, model), bf16),
            pltpu.VMEM((taps.shape[0], length, LANES), f32),
        ],
        compiler_params=params(), cost_estimate=cost(6), name="enter",
    )(normed, rim, cot, *vectors, masks, conv_w, gate_w, out_w, taps, weight)


def early_kernel(members, where_ref, tokens_ref, cot_ref, gain_ref, normed_ref, *rest):
    rim_ref, *early_refs, turned_ref = rest
    length, model = tokens_ref.shape
    rim_ref[...] = tokens_ref[length - CHUNKS :, :]
    tokens = tokens_ref[...].astype(jnp.float32)
    gain = gain_ref[...].reshape(1, model)
    normed_ref[...] = (tokens * inverse_rms(tokens) * gain).astype(jnp.bfloat16)
    for group in range(model // LANES):
        at = slice(group * LANES, (group + 1) * LANES)
        turned_ref[at, :] = normed_ref[:, at].astype(jnp.float32).T
        turned_ref[model + group * LANES : model + (group + 1) * LANES, :] = (
            cot_ref[:, at].astype(jnp.float32).T
        )
    rows, lines = model // members, members // PLANE
    for mask, early_ref in enumerate(early_refs):
        place = jnp.bitwise_xor(where_ref[0] % PLANE, mask)
        for source in range(2):
            pieces = []
            for line in range(lines):
                first = source * model + (line * PLANE + place) * rows
                if rows % 8 == 0:
                    first = pl.multiple_of(first, 8)
                pieces.append(turned_ref[pl.ds(first, rows), :])
            at = slice(source * lines * rows, (source + 1) * lines * rows)
            early_ref[at, :] = jnp.concatenate(pieces, axis=0).astype(jnp.bfloat16)


def run_early(where, tokens, cot, gain):
    length, model = tokens.shape
    members = lax.axis_size("seq")
    vmem = pl.BlockSpec(memory_space=pltpu.VMEM)
    early = jax.ShapeDtypeStruct((2 * model // PLANE, length), jnp.bfloat16)
    return pl.pallas_call(
        functools.partial(early_kernel, members),
        in_specs=[pl.BlockSpec(memory_space=pltpu.SMEM), vmem, vmem, vmem],
        out_specs=[vmem] * (2 + PLANE),
        out_shape=[
            jax.ShapeDtypeStruct(tokens.shape, jnp.bfloat16),
            jax.ShapeDtypeStruct((CHUNKS, model), jnp.bfloat16),
        ] + [early] * PLANE,
        scratch_shapes=[pltpu.VMEM((2 * model, length), jnp.float32)],
        compiler_params=params(), cost_estimate=cost(3), name="early",
    )(where, tokens, cot, gain)


def every(width):
    return [(group, slice(group * LANES, (group + 1) * LANES)) for group in range(width // LANES)]


def chunk_sums(long_ref, group, length):
    sums = long_ref[group, strided(0, length), :]
    for place in range(1, length // CHUNKS):
        sums = sums + long_ref[group, strided(place, length), :]
    return sums


def prepare(
    rank, states, own_ref, peer_ref, weight_ref, bias_ref, conv_ref, gg_ref, gate_ref, masks_ref,
    proj_ref, in_ref, out_ref, long_ref, drive_ref, source_ref, true_ref=None,
):
    length, width = conv_ref.shape
    proj_ref[...] = own_ref[...] + peer_ref[...]
    low = proj_ref[:, :rank].astype(jnp.bfloat16)
    step_pre = dot(low, weight_ref[...], ((1,), (0,))) + row(bias_ref, STEP_BIAS)
    spread(proj_ref, rank, in_ref, states, length)
    spread(proj_ref, rank + states, out_ref, states, length)
    same = columns(masks_ref, masks_ref.shape[0] - 2)
    for group, at in every(width):
        step = softplus(step_pre[:, at])
        if true_ref is not None:
            true_ref[group] = step
        long_ref[group] = jnp.where(same > 0.0, step, FAR)
        drive_ref[group] = step * conv_ref[:, at].astype(jnp.float32)
        gate = gate_ref[:, at]
        source_ref[group] = gg_ref[:, at] * gate * sigmoid(gate)
    return step_pre


def ends_kernel(
    rank, states, ndeps,
    own_ref, peer_ref, weight_ref, bias_ref, decay_ref, conv_ref, gg_ref, gate_ref, masks_ref, *rest,
):
    (
        ends_ref, seeds_ref, totals_ref,
        proj_ref, in_ref, out_ref, long_ref, drive_ref, source_ref, end_ref, seed_ref, dec_ref,
    ) = rest[ndeps:]
    length, width = conv_ref.shape
    places = length // CHUNKS
    prepare(
        rank, states, own_ref, peer_ref, weight_ref, bias_ref, conv_ref, gg_ref, gate_ref, masks_ref,
        proj_ref, in_ref, out_ref, long_ref, drive_ref, source_ref,
    )

    @pl.loop(0, width // LANES)
    def _(group):
        rate2 = -jnp.exp(decay_ref[:, group_at(group)]) * LOG2E
        rates = [jnp.broadcast_to(rate2[n : n + 1, :], (CHUNKS, LANES)) for n in range(states)]
        hidden = [None] * states
        for place in range(places):
            long = long_ref[group, strided(place, length), :]
            drive = drive_ref[group, strided(place, length), :]
            for n in range(states):
                term = tile(in_ref, place, n, states) * drive
                decay = jnp.exp2(long * rates[n])
                dec_ref[(place * states + n) * CHUNKS : (place * states + n + 1) * CHUNKS, :] = decay
                hidden[n] = term if place == 0 else decay * hidden[n] + term
        for n in range(states):
            end_ref[group, n * CHUNKS : (n + 1) * CHUNKS, :] = hidden[n]
        back = [None] * states
        for place in reversed(range(places)):
            long = long_ref[group, strided(place, length), :]
            source = source_ref[group, strided(place, length), :]
            for n in range(states):
                term = tile(out_ref, place, n, states) * source
                term = term if place == places - 1 else back[n] + term
                back[n] = tile(dec_ref, place, n, states) * term
        for n in range(states):
            seed_ref[group, n * CHUNKS : (n + 1) * CHUNKS, :] = back[n]

    for group, at in every(width):
        ends_ref[:, at] = end_ref[group]
        seeds_ref[:, at] = seed_ref[group]
        rate2 = -jnp.exp(decay_ref[:, at]) * LOG2E
        sums = chunk_sums(long_ref, group, length)
        decays = [jnp.exp2(rate2 * sums[c : c + 1, :]) for c in range(CHUNKS)]
        end = jnp.zeros((states, LANES), jnp.float32)
        seed = jnp.zeros((states, LANES), jnp.float32)
        for c in range(CHUNKS):
            end = decays[c] * end + end_ref[group, pl.ds(c, states, stride=CHUNKS), :]
        for c in reversed(range(CHUNKS)):
            seed = decays[c] * seed + seed_ref[group, pl.ds(c, states, stride=CHUNKS), :]
        totals_ref[:states, at] = end.astype(jnp.bfloat16)
        totals_ref[states : 2 * states, at] = seed.astype(jnp.bfloat16)
        totals_ref[2 * states :, at] = two_rows(jnp.sum(sums, axis=0, keepdims=True))


def scan_kernel(
    rank, states, members,
    where_ref, own_ref, peer_ref, weight_ref, bias_ref, decay_ref, conv_ref, gg_ref, gate_ref, masks_ref,
    ends_ref, seeds_ref, near_ref, *rest,
):
    stride, radix = levels(members)[-1]
    far_refs = rest[: radix - 1]
    both_ref, small_ref, gconv_ref, gproj_ref = rest[-21:-17]
    (
        proj_ref, in_ref, out_ref, long_ref, true_ref, drive_ref, source_ref,
        start_ref, last_ref, hidden_ref, in_acc, out_acc, scan_ref, gstep_ref, mix_ref, log_ref, dec_ref,
    ) = rest[-17:]
    length, width = conv_ref.shape
    places = length // CHUNKS
    step_pre = prepare(
        rank, states, own_ref, peer_ref, weight_ref, bias_ref, conv_ref, gg_ref, gate_ref, masks_ref,
        proj_ref, in_ref, out_ref, long_ref, drive_ref, source_ref, true_ref,
    )
    in_acc[...] = jnp.zeros_like(in_acc)
    out_acc[...] = jnp.zeros_like(out_acc)
    digit = where_ref[0] // stride % radix
    for group, at in every(width):
        start_ref[group] = ends_ref[:, at]
        last_ref[group] = seeds_ref[:, at]
        rate2 = -jnp.exp(decay_ref[:, at]) * LOG2E
        sums = chunk_sums(long_ref, group, length)
        decays = [jnp.exp2(rate2 * sums[c : c + 1, :]) for c in range(CHUNKS)]
        forward, backward = arrive(
            digit, rate2, near_ref[:, at], [ref[:, at] for ref in far_refs], states
        )
        for c in range(CHUNKS):
            rows = pl.ds(c, states, stride=CHUNKS)
            own = start_ref[group, rows, :]
            start_ref[group, rows, :] = forward
            forward = decays[c] * forward + own
        for c in reversed(range(CHUNKS)):
            rows = pl.ds(c, states, stride=CHUNKS)
            own = last_ref[group, rows, :]
            last_ref[group, rows, :] = backward
            backward = decays[c] * backward + own

    @pl.loop(0, width // LANES)
    def _(group):
        rate2 = -jnp.exp(decay_ref[:, group_at(group)]) * LOG2E
        rates = [jnp.broadcast_to(rate2[n : n + 1, :], (CHUNKS, LANES)) for n in range(states)]
        hidden = [start_ref[group, n * CHUNKS : (n + 1) * CHUNKS, :] for n in range(states)]
        for place in range(places):
            long = long_ref[group, strided(place, length), :]
            drive = drive_ref[group, strided(place, length), :]
            source = source_ref[group, strided(place, length), :]
            rows = slice(place * CHUNKS, (place + 1) * CHUNKS)
            scan = None
            for n in range(states):
                lanes = slice(n * LANES, (n + 1) * LANES)
                decay = jnp.exp2(long * rates[n])
                dec_ref[(place * states + n) * CHUNKS : (place * states + n + 1) * CHUNKS, :] = decay
                value = decay * hidden[n] + tile(in_ref, place, n, states) * drive
                hidden[n] = value
                if place < places - 1:
                    first = (place * states + n) * CHUNKS
                    hidden_ref[first : first + CHUNKS, :] = value
                part = tile(out_ref, place, n, states) * value
                scan = part if n == 0 else scan + part
                out_acc[rows, lanes] += source * value
            scan_ref[group, strided(place, length), :] = scan

        back = [last_ref[group, n * CHUNKS : (n + 1) * CHUNKS, :] for n in range(states)]
        logs = [None] * states
        for place in reversed(range(places)):
            long = long_ref[group, strided(place, length), :]
            true = true_ref[group, strided(place, length), :]
            drive = drive_ref[group, strided(place, length), :]
            source = source_ref[group, strided(place, length), :]
            rows = slice(place * CHUNKS, (place + 1) * CHUNKS)
            gstep = None
            mixed = None
            for n in range(states):
                lanes = slice(n * LANES, (n + 1) * LANES)
                grad = back[n] + tile(out_ref, place, n, states) * source
                previous = (
                    start_ref[group, n * CHUNKS : (n + 1) * CHUNKS, :] if place == 0
                    else tile(hidden_ref, place - 1, n, states)
                )
                back[n] = tile(dec_ref, place, n, states) * grad
                log = back[n] * previous
                part = log * true
                logs[n] = part if logs[n] is None else logs[n] + part
                part = log * rates[n]
                gstep = part if n == 0 else gstep + part
                part = grad * tile(in_ref, place, n, states)
                mixed = part if n == 0 else mixed + part
                in_acc[rows, lanes] += grad * drive
            gstep_ref[group, strided(place, length), :] = gstep
            mix_ref[group, strided(place, length), :] = mixed
        for n in range(states):
            log_ref[group, n * CHUNKS : (n + 1) * CHUNKS, :] = logs[n]

    low = proj_ref[...].astype(jnp.bfloat16)
    small_ref[rank + states + 2 :, :] = jnp.zeros((small_ref.shape[0] - rank - states - 2, width), jnp.float32)
    grad_low = jnp.zeros((length, rank), jnp.float32)
    for group, at in every(width):
        conv = conv_ref[:, at].astype(jnp.float32)
        gate, gg = gate_ref[:, at], gg_ref[:, at]
        source, step, mix = source_ref[group], true_ref[group], mix_ref[group]
        sigma = sigmoid(gate)
        skip = bias_ref[SKIP : SKIP + 1, at]
        scan_out = scan_ref[group] + skip * conv
        both_ref[:length, at] = (scan_out * gate * sigma).astype(jnp.bfloat16)
        ggate = gg * scan_out * sigma * (1.0 + gate * (1.0 - sigma))
        both_ref[length:, at] = ggate.astype(jnp.bfloat16)
        gconv_ref[:, at] = source * skip + mix * step
        gpre = (gstep_ref[group] * LN2 + mix * conv) * sigmoid(step_pre[:, at])
        gpre_low = gpre.astype(jnp.bfloat16)
        grad_low = grad_low + dot(gpre_low, weight_ref[:, at], ((1,), (1,)))
        small_ref[:rank, at] = dot(low, gpre_low, ((0,), (0,)))[:rank]
        decay = -jnp.exp(decay_ref[:, at])
        logs = log_ref[group, pl.ds(0, states, stride=CHUNKS), :]
        for c in range(1, CHUNKS):
            logs = logs + log_ref[group, pl.ds(c, states, stride=CHUNKS), :]
        first = rank + states
        small_ref[rank:first, at] = logs * decay
        small_ref[first : first + 1, at] = jnp.sum(gpre, axis=0, keepdims=True)
        small_ref[first + 1 : first + 2, at] = jnp.sum(source * conv, axis=0, keepdims=True)

    wide = states * LANES
    source_state = lax.broadcasted_iota(jnp.int32, (wide, LANES), 0) // LANES
    column = lax.broadcasted_iota(jnp.int32, (wide, LANES), 1)
    total = jnp.zeros((length, LANES), jnp.float32)
    for acc, first in ((in_acc, rank), (out_acc, rank + states)):
        pick = jnp.where(source_state + first == column, 1.0, 0.0).astype(jnp.bfloat16)
        value = acc[...]
        high = value.astype(jnp.bfloat16)
        rest = (value - high.astype(jnp.float32)).astype(jnp.bfloat16)
        total = total + dot(high, pick, ((1,), (0,))) + dot(rest, pick, ((1,), (0,)))
    scan_ref[0] = total
    for place in range(places):
        mix_ref[0, strided(place, length), :] = scan_ref[0, place * CHUNKS : (place + 1) * CHUNKS, :]
    gproj_ref[...] = mix_ref[0]
    gproj_ref[:, :rank] += grad_low


def column_block(rows, width=LANES):
    return pl.BlockSpec((rows, width), lambda g: (0, g))


def whole(*shape):
    return pl.BlockSpec(shape, lambda g: (0,) * len(shape))


def run_ends(own, peer, weight, stacked, decay_log, conv, gg, gate, masks, deps=()):
    length, width = conv.shape
    rank, states = weight.shape[0], decay_log.shape[0]
    tall = length // CHUNKS * states * CHUNKS
    f32 = jnp.float32
    vmem = pl.BlockSpec(memory_space=pltpu.VMEM)
    return pl.pallas_call(
        functools.partial(ends_kernel, rank, states, len(deps)),
        in_specs=[vmem] * 9 + [pl.BlockSpec(memory_space=pl.ANY) for _ in deps], out_specs=[vmem] * 3,
        out_shape=[
            jax.ShapeDtypeStruct((states * CHUNKS, width), f32),
            jax.ShapeDtypeStruct((states * CHUNKS, width), f32),
            jax.ShapeDtypeStruct((2 * states + 2 * CHUNKS, width), jnp.bfloat16),
        ],
        scratch_shapes=[pltpu.VMEM((length, LANES), f32)]
        + [pltpu.VMEM((tall, LANES), f32)] * 2 + [pltpu.VMEM((width // LANES, length, LANES), f32)] * 3
        + [pltpu.VMEM((width // LANES, states * CHUNKS, LANES), f32)] * 2
        + [pltpu.VMEM((tall, LANES), f32)],
        compiler_params=params(), cost_estimate=cost(8), name="ends",
    )(own, peer, weight, stacked, decay_log, conv, gg, gate, masks, *deps)


def run_scan(where, own, peer, weight, stacked, decay_log, conv, gg, gate, masks, ends, seeds, near, far, deps):
    length, width = conv.shape
    members = lax.axis_size("seq")
    rank, states = weight.shape[0], decay_log.shape[0]
    places = length // CHUNKS
    tall = places * states * CHUNKS
    f32, bf16 = jnp.float32, jnp.bfloat16
    groups = pltpu.VMEM((width // LANES, length, LANES), f32)
    chunks = pltpu.VMEM((width // LANES, states * CHUNKS, LANES), f32)
    table = pltpu.VMEM((tall, LANES), f32)
    vmem = pl.BlockSpec(memory_space=pltpu.VMEM)
    return pl.pallas_call(
        functools.partial(scan_kernel, rank, states, members),
        in_specs=[pl.BlockSpec(memory_space=pltpu.SMEM)] + [vmem] * (12 + len(far))
        + [pl.BlockSpec(memory_space=pl.ANY) for _ in deps],
        out_specs=[vmem] * 4,
        out_shape=[
            jax.ShapeDtypeStruct((2 * length, width), bf16),
            jax.ShapeDtypeStruct((padded(rank + states + 2, 8), width), f32),
            jax.ShapeDtypeStruct((length, width), f32),
            jax.ShapeDtypeStruct((length, LANES), f32),
        ],
        scratch_shapes=[pltpu.VMEM((length, LANES), f32), table, table] + [groups] * 4 + [chunks] * 2
        + [table] + [pltpu.VMEM((length, states * LANES), f32)] * 2 + [groups] * 3 + [chunks, table],
        compiler_params=params(), cost_estimate=cost(15), name="scan",
    )(where, own, peer, weight, stacked, decay_log, conv, gg, gate, masks, ends, seeds, near, *far, *deps)


def levels(members):
    found, stride = [], 1
    while stride < members:
        radix = 4 if members // stride % 4 == 0 else 2
        found.append((stride, radix))
        stride *= radix
    return found


def chosen(refs, own, hop):
    value = own
    for mask, ref in enumerate(refs, 1):
        value = jnp.where(hop == mask, ref.astype(jnp.float32), value)
    return value


def arrive(digit, rate2, near, far, states):
    radix = len(far) + 1
    carry = jnp.zeros_like(rate2)
    incoming = jnp.zeros_like(rate2)
    blank = jnp.zeros(far[0].shape, jnp.float32)
    for number in range(radix):
        value = chosen(far, blank, digit ^ number)
        decay = jnp.exp2(rate2 * (value[states : states + 1] + value[states + 1 : states + 2]))
        carry = jnp.where(number < digit, decay * carry + value[:states], carry)
    for number in reversed(range(radix)):
        value = chosen(far, blank, digit ^ number)
        decay = jnp.exp2(rate2 * (value[states : states + 1] + value[states + 1 : states + 2]))
        incoming = jnp.where(number > digit, decay * incoming + value[:states], incoming)
    before, behind = near[2 * states : 2 * states + 1], near[2 * states + 1 : 2 * states + 2]
    carry = near[:states] + jnp.exp2(rate2 * before) * carry
    incoming = near[states : 2 * states] + jnp.exp2(rate2 * behind) * incoming
    return carry, incoming


def fold_kernel(states, level, members, start, where_ref, decay_ref, *refs):
    stride, radix = levels(members)[level]
    next_stride, next_radix = levels(members)[level + 1]
    last = level + 2 == len(levels(members))
    digit = where_ref[0] // stride % radix
    if not start:
        old = refs[0][...]
        refs = refs[1:]
    own = refs[0][...]
    got = [ref[...] for ref in refs[1:radix]]
    near_ref, outs = refs[radix], refs[radix + 1 :]
    rate2 = -jnp.exp(decay_ref[...]) * LOG2E
    own = own.astype(jnp.float32)
    values = [chosen(got, own, digit ^ number) for number in range(radix)]
    first = 2 * states
    sums = [value[first : first + 1] + value[first + 1 : first + 2] for value in values]
    decays = [jnp.exp2(rate2 * one) for one in sums]
    zero, line = jnp.zeros_like(rate2), jnp.zeros_like(sums[0])
    end, seed, carry, incoming, before, behind, total = zero, zero, zero, zero, line, line, line
    for number in range(radix):
        part = values[number][:states]
        end = decays[number] * end + part
        carry = jnp.where(number < digit, decays[number] * carry + part, carry)
        before = jnp.where(number < digit, before + sums[number], before)
        total = total + sums[number]
    for number in reversed(range(radix)):
        part = values[number][states : 2 * states]
        seed = decays[number] * seed + part
        incoming = jnp.where(number > digit, decays[number] * incoming + part, incoming)
        behind = jnp.where(number > digit, behind + sums[number], behind)
    if not start:
        old_before, old_behind = old[2 * states : 2 * states + 1], old[2 * states + 1 : 2 * states + 2]
        carry = old[:states] + jnp.exp2(rate2 * old_before) * carry
        incoming = old[states : 2 * states] + jnp.exp2(rate2 * old_behind) * incoming
        before, behind = before + old_before, behind + old_behind
    pad = jnp.zeros((6, line.shape[1]), jnp.float32)
    near_ref[...] = jnp.concatenate([carry, incoming, before, behind, pad], axis=0)
    tail = two_rows(total)
    if last:
        next_digit = where_ref[0] // next_stride % next_radix
        for mask, out in enumerate(outs, 1):
            value = jnp.where(next_digit < (next_digit ^ mask), end, seed)
            out[:states, :] = value.astype(jnp.bfloat16)
            out[states:, :] = tail
    else:
        outs[0][: 2 * states, :] = jnp.concatenate([end, seed], axis=0).astype(jnp.bfloat16)
        outs[0][2 * states :, :] = tail


def run_fold(level, where, decay_log, near, parts):
    states, width = decay_log.shape
    members = lax.axis_size("seq")
    f32, bf16 = jnp.float32, jnp.bfloat16
    vmem = pl.BlockSpec(memory_space=pltpu.VMEM)
    tall = jax.ShapeDtypeStruct((2 * states + 8, width), f32)
    if level + 2 == len(levels(members)):
        sent = [jax.ShapeDtypeStruct((states + 2 * CHUNKS, width), bf16)] * (levels(members)[-1][1] - 1)
    else:
        sent = [jax.ShapeDtypeStruct((2 * states + 2 * CHUNKS, width), bf16)]
    extra = [] if near is None else [near]
    return pl.pallas_call(
        functools.partial(fold_kernel, states, level, members, near is None),
        in_specs=[pl.BlockSpec(memory_space=pltpu.SMEM)] + [vmem] * (1 + len(extra) + len(parts)),
        out_specs=[vmem] * (1 + len(sent)),
        out_shape=[tall] + sent,
        compiler_params=params(), cost_estimate=cost(2), name="fold",
    )(where, decay_log, *extra, *parts)


def exchange(where, totals, decay_log):
    members = lax.axis_size("seq")
    found = levels(members)
    near = None
    for level, (stride, radix) in enumerate(found[:-1]):
        parts = [totals] + [hop(totals, mask * stride) for mask in range(1, radix)]
        near, *sent = run_fold(level, where, decay_log, near, parts)
        totals = sent[0]
    stride, radix = found[-1]
    return near, [hop(one, mask * stride) for mask, one in enumerate(sent, 1)]


def taps_kernel(
    kernel,
    where_ref, own_ref, peer_ref, conv_ref, in_ref, ext_ref, weight_ref, gconv_ref, taps_ref, params_ref, masks_ref,
    first_small_ref, main_ref, rim_ref, kept_ref, *rest,
):
    *sent_refs, small_ref, quarter_ref = rest
    length, total_width = conv_ref.shape
    width = weight_ref.shape[0]
    grad_proj = (own_ref[...] + peer_ref[...]).astype(jnp.bfloat16)
    masks = [columns(masks_ref, tap) for tap in range(kernel)]
    near_row = lax.broadcasted_iota(jnp.int32, (CHUNKS, LANES), 0)
    token = lax.broadcasted_iota(jnp.int32, (length, LANES), 0)
    for group in range(total_width // LANES):
        at = slice(group * LANES, (group + 1) * LANES)
        taps = [taps_ref[tap : tap + 1, at] for tap in range(kernel)]
        conv_in = in_ref[:, at].astype(jnp.float32)
        ext = ext_ref[:, at]
        seen = [shifted(conv_in, ext, kernel - 1 - tap) * masks[tap] for tap in range(kernel)]
        pre = jnp.broadcast_to(params_ref[TAP_BIAS : TAP_BIAS + 1, at], (length, LANES))
        for tap in range(kernel):
            pre = pre + taps[tap] * seen[tap]
        small_ref[:width, at] = dot(grad_proj, conv_ref[:, at], ((0,), (0,)))[:width]
        grad = gconv_ref[:, at] + dot(grad_proj[:, :width], weight_ref[:, at], ((1,), (0,)))
        grad = grad * silu_grad(pre)
        lines = []
        main = jnp.zeros((length, LANES), jnp.float32)
        rim = jnp.zeros((CHUNKS, LANES), jnp.float32)
        for tap in range(kernel):
            back = kernel - 1 - tap
            lines.append(jnp.sum(grad * seen[tap], axis=0, keepdims=True))
            masked = grad * masks[tap] * taps[tap]
            if back == 0:
                main = main + masked
            else:
                moved = pltpu.roll(masked, length - back, 0)
                main = main + jnp.where(token < length - back, moved, 0.0)
                rim = rim + jnp.where(
                    near_row >= CHUNKS - back, pltpu.roll(masked[:CHUNKS], CHUNKS - back, 0), 0.0
                )
        main_ref[:, at] = main
        rim_ref[:, at] = rim
        lines.append(jnp.sum(grad, axis=0, keepdims=True))
        lines.append(jnp.zeros((small_ref.shape[0] - width - kernel - 1, LANES), jnp.float32))
        small_ref[width:, at] = jnp.concatenate(lines, axis=0)
    small = jnp.concatenate([first_small_ref[...], small_ref[...]], axis=0)
    count, rows = kept_ref.shape[0], small.shape[0] // PLANE
    for quarter in range(PLANE):
        quarter_ref[quarter, :rows, :] = small[quarter * rows : (quarter + 1) * rows]
        quarter_ref[quarter, rows:, :] = jnp.zeros((count - rows, total_width), jnp.float32)
    place = where_ref[0] % PLANE
    kept_ref[...] = quarter_ref[place]
    for mask, sent_ref in enumerate(sent_refs, 1):
        sent_ref[...] = quarter_ref[jnp.bitwise_xor(place, mask)].astype(jnp.bfloat16)


def run_taps(where, own, peer, conv, conv_in, ext, weight, gconv, taps, stacked, masks, first_small):
    length, width = conv.shape
    kernel = taps.shape[0]
    f32 = jnp.float32
    vmem = pl.BlockSpec(memory_space=pltpu.VMEM)
    tall = padded(weight.shape[0] + kernel + 1, 8)
    count = padded((first_small.shape[0] + tall) // PLANE, 8)
    return pl.pallas_call(
        functools.partial(taps_kernel, kernel),
        in_specs=[pl.BlockSpec(memory_space=pltpu.SMEM)] + [vmem] * 11, out_specs=[vmem] * (2 + PLANE),
        out_shape=[
            jax.ShapeDtypeStruct((length, width), f32), jax.ShapeDtypeStruct((CHUNKS, width), f32),
            jax.ShapeDtypeStruct((count, width), f32),
        ] + [jax.ShapeDtypeStruct((count, width), jnp.bfloat16)] * (PLANE - 1),
        scratch_shapes=[pltpu.VMEM((tall, width), f32), pltpu.VMEM((PLANE, count, width), f32)],
        compiler_params=params(), cost_estimate=cost(4), name="taps",
    )(where, own, peer, conv, conv_in, ext, weight, gconv, taps, stacked, masks, first_small)


def inputs_kernel(ndeps, main_ref, rim_ref, weight_ref, both_ref, gate_weight_ref, tokens_ref, *rest):
    low_ref, normed_ref = rest[ndeps:]
    length, width = main_ref.shape
    main = main_ref[...]
    low = jnp.concatenate(
        [main[: length - CHUNKS], main[length - CHUNKS :] + rim_ref[...]], axis=0
    ).astype(jnp.bfloat16)
    normed = dot(both_ref[length:, :], gate_weight_ref[...], ((1,), (1,)))
    normed = normed + dot(low, weight_ref[...], ((1,), (1,)))
    normed_ref[...] = normed
    tokens = tokens_ref[...].astype(jnp.float32)
    gain = jnp.sum(normed * tokens * inverse_rms(tokens), axis=0, keepdims=True)
    low_ref[:length, :] = low
    low_ref[length:, :] = two_rows(gain)


def run_inputs(main, rim, weight, both, gate_weight, tokens, deps):
    length, width = main.shape
    vmem = pl.BlockSpec(memory_space=pltpu.VMEM)
    return pl.pallas_call(
        functools.partial(inputs_kernel, len(deps)),
        in_specs=[vmem] * 6 + [pl.BlockSpec(memory_space=pl.ANY) for _ in deps], out_specs=[vmem] * 2,
        out_shape=[
            jax.ShapeDtypeStruct((length + 2 * CHUNKS, width), jnp.bfloat16),
            jax.ShapeDtypeStruct((length, weight.shape[0]), jnp.float32),
        ],
        compiler_params=params(), cost_estimate=cost(3), name="inputs",
    )(main, rim, weight, both, gate_weight, tokens, *deps)


def products_kernel(halves, members, ndeps, where_ref, *rest):
    early, rest = rest[:PLANE], rest[PLANE:]
    late, rest = list(rest[: 2 + len(halves) + 1]), rest[2 + len(halves) + 1 :]
    lines = members // PLANE
    share, length = early[0].shape[0] // 2, early[0].shape[1]
    rows = share // lines
    apart = late[0].shape[0] == len(halves) * length
    if apart:
        small, rest = rest[:PLANE], rest[PLANE:]
    kept_ref, small_ref, sent_ref, total_ref = rest[ndeps:]
    for number, half in enumerate(halves):
        total = None
        for mask in range(PLANE):
            if mask == 3 and len(halves) > 1:
                block = late[mask + number][...]
            else:
                block = late[mask][number * length : (number + 1) * length, :]
            part = dot(early[mask][half * share : (half + 1) * share, :], block, ((1,), (0,)))
            total = part if total is None else total + part
        for line in range(lines):
            total_ref[line, number * rows : (number + 1) * rows, :] = total[line * rows : (line + 1) * rows]
    if apart:
        line = small[0][...]
        for ref in small[1:]:
            line = line + ref[...].astype(jnp.float32)
    else:
        line = sum(
            jnp.sum(ref[len(halves) * length :, :].astype(jnp.float32), axis=0, keepdims=True) for ref in late
        )
        number = lax.broadcasted_iota(jnp.int32, small_ref.shape, 0)
        line = jnp.where(number == 0, line, 0.0)
    send(where_ref[0], 0, total_ref, line, kept_ref, small_ref, sent_ref)


def send(device, level, total_ref, line, kept_ref, small_ref, sent_ref):
    digit = device // (PLANE << level) % 2
    small_ref[...] = line
    pieces = [line]
    for block in range(total_ref.shape[0] // 2):
        kept_ref[block] = total_ref[2 * block + digit]
        pieces.append(total_ref[2 * block + 1 - digit])
    sent_ref[...] = jnp.concatenate(pieces, axis=0).astype(jnp.bfloat16)


def gather_kernel(level, count, ndeps, where_ref, kept_ref, small_ref, got_ref, *refs):
    refs = refs[ndeps:]
    total = kept_ref[...]
    got = got_ref[...].astype(jnp.float32)
    first = small_ref.shape[0]
    line = small_ref[...] + got[:first]
    left, rows, width = total.shape
    pieces = [total[index] + got[first + index * rows : first + (index + 1) * rows] for index in range(left)]
    if left > 1:
        total_ref = refs[-1]
        for index, piece in enumerate(pieces):
            total_ref[index] = piece
        send(where_ref[0], level + 1, total_ref, line, *refs[:-1])
        return
    for index in range(count):
        refs[index][...] = pieces[0][index * (rows // count) : (index + 1) * (rows // count)]
    if len(refs[count].shape) == 1:
        refs[count][...] = line[:1].reshape(width)
    else:
        refs[count][...] = line.astype(refs[count].dtype)


def multiply(halves, where, early, late, small, deps):
    members = lax.axis_size("seq")
    lines = members // PLANE
    width = late[0].shape[1]
    rows = len(halves) * (early[0].shape[0] // 2 // lines)
    vmem = pl.BlockSpec(memory_space=pltpu.VMEM)
    count = small[0].shape[0] if small else 2 * CHUNKS
    out_shape = level_shapes(lines, rows, count, width)
    return pl.pallas_call(
        functools.partial(products_kernel, halves, members, len(deps)),
        in_specs=[pl.BlockSpec(memory_space=pltpu.SMEM)] + [vmem] * (PLANE + len(late) + len(small))
        + [pl.BlockSpec(memory_space=pl.ANY) for _ in deps],
        out_specs=[vmem] * len(out_shape), out_shape=out_shape,
        scratch_shapes=[pltpu.VMEM((lines, rows, width), jnp.float32)],
        compiler_params=params(), cost_estimate=cost(4), name="products",
    )(where, *early, *late, *small, *deps)


def level_shapes(left, rows, count, width):
    return [
        jax.ShapeDtypeStruct((left // 2, rows, width), jnp.float32),
        jax.ShapeDtypeStruct((count, width), jnp.float32),
        jax.ShapeDtypeStruct((count + left // 2 * rows, width), jnp.bfloat16),
    ]


def add_line(level, where, parts, number, deps=()):
    f32 = jnp.float32
    kept, small, sent = parts
    vmem = pl.BlockSpec(memory_space=pltpu.VMEM)
    got = hop(sent, PLANE << level)
    left, rows, width = kept.shape
    count = small.shape[0]
    scratch = []
    if left > 1:
        out_shape = level_shapes(left, rows, count, width)
        scratch = [pltpu.VMEM((left, rows, width), f32)]
    else:
        out_shape = [jax.ShapeDtypeStruct((rows // number, width), f32)] * number
        single = count == 2 * CHUNKS
        out_shape.append(
            jax.ShapeDtypeStruct((width,), f32) if single else jax.ShapeDtypeStruct(small.shape, jnp.bfloat16)
        )
    return pl.pallas_call(
        functools.partial(gather_kernel, level, number, len(deps)),
        in_specs=[pl.BlockSpec(memory_space=pltpu.SMEM)] + [vmem] * 3
        + [pl.BlockSpec(memory_space=pl.ANY) for _ in deps],
        out_specs=[vmem] * len(out_shape), out_shape=out_shape, scratch_shapes=scratch,
        compiler_params=params(), cost_estimate=cost(2), name="gather",
    )(where, kept, small, got, *deps)


def branch_kernel(both_ref, weight_ref, _, branch_ref):
    branch_ref[...] = dot(both_ref[: branch_ref.shape[0], :], weight_ref[...], ((1,), (0,)))


def run_branch(both, weight, dep):
    vmem = pl.BlockSpec(memory_space=pltpu.VMEM)
    return pl.pallas_call(
        branch_kernel, in_specs=[vmem, vmem, pl.BlockSpec(memory_space=pl.ANY)], out_specs=vmem,
        out_shape=jax.ShapeDtypeStruct((both.shape[0] // 2, weight.shape[1]), jnp.float32),
        compiler_params=params(), cost_estimate=cost(5), name="branch",
    )(both, weight, dep)


def place_kernel(rows, counts, where_ref, *refs):
    quarters, outs, (table_ref,) = refs[:PLANE], refs[PLANE:-1], refs[-1:]
    place = where_ref[0] % PLANE
    for mask, ref in enumerate(quarters):
        table_ref[jnp.bitwise_xor(place, mask)] = ref[...].astype(jnp.float32)
    table = jnp.concatenate([table_ref[quarter, :rows, :] for quarter in range(PLANE)], axis=0)
    for out, (first, count) in zip(outs, counts, strict=True):
        value = table[first : first + count]
        out[...] = value.reshape(value.shape[1]) if count == 1 else value


def run_place(where, own, rows, counts):
    count, width = own.shape
    f32 = jnp.float32
    vmem = pl.BlockSpec(memory_space=pltpu.VMEM)
    shapes = [(width,) if number == 1 else (number, width) for _, number in counts]
    return pl.pallas_call(
        functools.partial(place_kernel, rows, counts),
        in_specs=[pl.BlockSpec(memory_space=pltpu.SMEM)] + [vmem] * PLANE,
        out_specs=[vmem] * len(shapes),
        out_shape=[jax.ShapeDtypeStruct(shape, f32) for shape in shapes],
        scratch_shapes=[pltpu.VMEM((PLANE, count, width), f32)],
        compiler_params=params(), cost_estimate=cost(3), name="place",
    )(where, own, hop(own, 1), hop(own, 2), hop(own, 3))


def relay_kernel(x_ref, y_ref, *rest):
    from_x_ref, from_y_ref = rest[-2:]
    length = from_x_ref.shape[0]
    from_x_ref[...] = x_ref[:length, :]
    from_y_ref[...] = y_ref[length:, :]


def run_relay(x, y, deps):
    vmem = pl.BlockSpec(memory_space=pltpu.VMEM)
    half = jax.ShapeDtypeStruct((x.shape[0] // 2, x.shape[1]), x.dtype)
    return pl.pallas_call(
        relay_kernel, in_specs=[vmem, vmem] + [pl.BlockSpec(memory_space=pl.ANY) for _ in deps],
        out_specs=[vmem] * 2,
        out_shape=[half, half], compiler_params=params(), cost_estimate=cost(1), name="relay",
    )(x, y, *deps)


def leave_kernel(tokens_ref, cot_ref, params_ref, branch_ref, branch_peer_ref, own_ref, peer_ref, mixed_ref, grad_ref):
    tokens = tokens_ref[...].astype(jnp.float32)
    mixed_ref[...] = (tokens + (branch_ref[...] + branch_peer_ref[...])).astype(jnp.bfloat16)
    scale = inverse_rms(tokens)
    scaled = (own_ref[...] + peer_ref[...]) * row(params_ref, GAIN)
    mean = jnp.mean(scaled * tokens, axis=1, keepdims=True)
    grad = cot_ref[...].astype(jnp.float32) + scale * scaled
    grad_ref[...] = grad - tokens * (scale * scale * scale * mean)


def run_leave(tokens, cot, stacked, branch, branch_peer, own, peer):
    vmem = pl.BlockSpec(memory_space=pltpu.VMEM)
    return pl.pallas_call(
        leave_kernel, in_specs=[vmem] * 7, out_specs=[vmem] * 2,
        out_shape=[
            jax.ShapeDtypeStruct(tokens.shape, jnp.bfloat16),
            jax.ShapeDtypeStruct(tokens.shape, jnp.float32),
        ],
        compiler_params=params(), cost_estimate=cost(3), name="leave",
    )(tokens, cot, stacked, branch, branch_peer, own, peer)


def from_behind(block, axis, distance):
    devices = range(lax.axis_size(axis))
    route = [(i - distance, i) for i in devices if i - distance in devices]
    return lax.ppermute(block, axis, route)


def swap(block):
    return lax.ppermute(block, "tp", [(0, 1), (1, 0)])


def hop(block, mask):
    members = lax.axis_size("seq")
    return lax.ppermute(block, "seq", [(i, i ^ mask) for i in range(members)])


def shards(
    tokens, norm_gain, in_conv_weight, in_gate_weight, conv_weight, conv_bias, scan_proj_weight,
    step_proj_weight, step_bias, decay_log, skip_gain, out_weight, segment_ids, cotangent,
):
    f32 = jnp.float32
    length, model = tokens.shape
    rank = step_proj_weight.shape[0]
    states = decay_log.shape[0]
    kernel = conv_weight.shape[0]
    width = conv_weight.shape[1]
    members = lax.axis_size("seq")
    device = lax.axis_index("seq")
    where = jnp.stack([device, lax.axis_index("tp")]).astype(jnp.int32)
    scan_width = rank + 2 * states
    padded_ids = jnp.concatenate([jnp.full((kernel,), -1, jnp.int32), segment_ids])
    near_ids = lax.dynamic_slice_in_dim(padded_ids, device * length, length + kernel)
    masks = jnp.stack(
        [near_ids[kernel:] == near_ids[tap + 1 : tap + 1 + length] for tap in range(kernel)]
    ).astype(f32)
    scan_weight = scan_proj_weight.T

    normed, rim_tokens, kept_early, *sent_early = run_early(where, tokens, cotangent, norm_gain)
    rim_tokens = from_behind(rim_tokens, "seq", 1)
    early = [kept_early] + [hop(one, mask) for mask, one in enumerate(sent_early, 1)]
    conv_in, ext, conv_out, gate_in, grad_gated, own, stacked = run_enter(
        normed, rim_tokens, cotangent, (conv_bias, step_bias, skip_gain, norm_gain), masks,
        in_conv_weight, in_gate_weight, out_weight, conv_weight, scan_weight,
    )
    peer = swap(own)
    ends, seeds, totals = run_ends(
        own, peer, step_proj_weight, stacked, decay_log, conv_out, grad_gated, gate_in, masks,
        early[1:],
    )
    near, far = exchange(where, totals, decay_log)
    both, first_small, grad_conv, low_own = run_scan(
        where, own, peer, step_proj_weight, stacked, decay_log, conv_out, grad_gated, gate_in, masks,
        ends, seeds, near, far, (),
    )
    low_peer = swap(low_own)
    main, rim, *small = run_taps(
        where, low_own, low_peer, conv_out, conv_in, ext, scan_weight, grad_conv, conv_weight, stacked,
        masks, first_small,
    )
    rim = from_behind(rim, "seq", -1)
    small = small[:1] + [hop(one, mask) for mask, one in enumerate(small[1:], 1)]
    x, y = hop(both, 1), hop(both, 2)
    from_x, from_y = run_relay(x, y, (main, rim, *small[1:3]))
    low, normed_own = run_inputs(
        main, rim, in_conv_weight, both, in_gate_weight, tokens, (from_x,)
    )
    first_late = [both, x, y, hop(from_x, 2), hop(from_y, 1)]
    second_late = [low] + [hop(low, mask) for mask in range(1, PLANE)]
    branch_own = run_branch(both, out_weight, normed_own)
    mixed_out, input_grad = run_leave(
        tokens, cotangent, stacked, branch_own, swap(branch_own), normed_own, swap(normed_own)
    )
    count = (members // PLANE).bit_length() - 1
    first = multiply((1, 0), where, early, first_late, small, (normed_own,))
    first = add_line(0, where, first, 2)
    second = multiply((0,), where, early, second_late, [], first[:1])
    for level in range(1, count):
        first = add_line(level, where, first, 2)
    out_grad, in_gate_grad, small = first
    second = add_line(0, where, second, 1, (out_grad,))
    first_row = first_small.shape[0]
    last_row = first_row + scan_width
    (
        step_proj_grad, decay_log_grad, step_bias_grad, skip_grad, scan_proj_grad, conv_weight_grad,
        conv_bias_grad,
    ) = run_place(
        where, small, (first_row + padded(scan_width + kernel + 1, 8)) // PLANE,
        (
            (0, rank), (rank, states), (rank + states, 1), (rank + states + 1, 1), (first_row, scan_width),
            (last_row, kernel), (last_row + kernel, 1),
        ),
    )
    for level in range(1, count):
        second = add_line(level, where, second, 1, (input_grad, step_proj_grad))
    in_conv_grad, gain_grad = second
    gain_grad = gain_grad + swap(gain_grad)
    return (
        mixed_out, input_grad, gain_grad, in_conv_grad, in_gate_grad, conv_weight_grad,
        conv_bias_grad, scan_proj_grad.T, step_proj_grad, step_bias_grad, decay_log_grad, skip_grad,
        out_grad.T,
    )


def solution(mesh):
    in_specs = (
        P("seq", None), P(), P(None, "tp"), P(None, "tp"), P(None, "tp"), P("tp"), P("tp", None),
        P(None, "tp"), P("tp"), P(None, "tp"), P("tp"), P("tp", None), P(), P("seq", None),
    )
    out_specs = (
        P("seq", None), P("seq", None), P(), P("seq", "tp"), P("seq", "tp"), P(None, "tp"), P("tp"),
        P("tp", None), P(None, "tp"), P("tp"), P(None, "tp"), P("tp"), P("tp", "seq"),
    )
    return jax.shard_map(shards, mesh=mesh, in_specs=in_specs, out_specs=out_specs, check_vma=False)
```

```python
import functools

import jax
import jax.numpy as jnp
from jax import lax
from jax.experimental import pallas as pl
from jax.experimental.pallas import tpu as pltpu
from jax.sharding import PartitionSpec as P

NORM_EPS = 1e-05
LANES = 128
PLANE = 4
CHUNKS = 8
LOG2E = 1.4426950408889634
LN2 = 0.6931471805599453
FAR = 1e30
MIB = 1024 * 1024
TAP_BIAS, STEP_BIAS, SKIP, GAIN = 0, 1, 2, 3


def sigmoid(value):
    return 1.0 / (1.0 + jnp.exp(-value))


def silu_grad(value):
    sigma = sigmoid(value)
    return sigma * (1.0 + value * (1.0 - sigma))


def softplus(value):
    small = jnp.exp(-jnp.abs(value))
    series = small * (1.0 - small * (0.5 - small * (1.0 / 3.0 - small * 0.25)))
    return jnp.maximum(value, 0.0) + jnp.where(small < 0.01, series, jnp.log(1.0 + small))


def dot(first, second, contract):
    return lax.dot_general(
        first, second, (contract, ((), ())), preferred_element_type=jnp.float32
    )


def strided(number, length):
    return pl.ds(number, CHUNKS, stride=length // CHUNKS)


def spread(proj_ref, first, table_ref, states, length):
    for place in range(length // CHUNKS):
        rows = proj_ref[strided(place, length), :]
        for state in range(states):
            column = rows[:, first + state : first + state + 1]
            start = (place * states + state) * CHUNKS
            table_ref[start : start + CHUNKS, :] = jnp.broadcast_to(column, (CHUNKS, LANES))


def tile(ref, place, state, states):
    start = (place * states + state) * CHUNKS
    return ref[start : start + CHUNKS, :]


def padded(number, unit):
    return -(-number // unit) * unit


def row(ref, number):
    return ref[number : number + 1, :]


def inverse_rms(tokens):
    return lax.rsqrt(jnp.mean(tokens * tokens, axis=1, keepdims=True) + NORM_EPS)


def columns(masks_ref, tap):
    return jnp.broadcast_to(row(masks_ref, tap), (LANES, masks_ref.shape[1])).T


def two_rows(line):
    high = line.astype(jnp.bfloat16).astype(jnp.float32)
    number = lax.broadcasted_iota(jnp.int32, (2 * CHUNKS, line.shape[1]), 0)
    return jnp.where(number == 0, high, jnp.where(number == 1, line - high, 0.0)).astype(jnp.bfloat16)


def group_at(group):
    return pl.ds(pl.multiple_of(group * LANES, LANES), LANES)


def params():
    return pltpu.CompilerParams(vmem_limit_bytes=64 * MIB)


def cost(us):
    return pl.CostEstimate(flops=0, bytes_accessed=int(us * 3e6), transcendentals=0)


def shifted(block, rim, back):
    if back == 0:
        return block
    moved = pltpu.roll(block, back, 0)
    near = lax.broadcasted_iota(jnp.int32, (CHUNKS, block.shape[1]), 0)
    top = jnp.where(near < back, pltpu.roll(rim, back, 0), moved[:CHUNKS])
    return jnp.concatenate([top, moved[CHUNKS:]], axis=0)


def enter_kernel(
    kernel, scan_width,
    normed_ref, rim_tokens_ref, cot_ref, tap_bias_ref, step_bias_ref, skip_ref, gain_ref, masks_ref,
    taps_ref, weight_ref, conv_w_hbm, gate_w_hbm, out_w_hbm,
    conv_ref, rim_ref, out_ref, gate_ref, gg_ref, proj_ref, stacked_ref,
    conv_w_ref, gate_w_ref, out_w_ref, sems,
):
    length, width = conv_ref.shape
    block = 3 * LANES
    blocks = [slice(first, first + block) for first in range(0, width, block)]
    copies = []
    for at in blocks:
        piece = len(copies)
        copies.append(pltpu.make_async_copy(conv_w_hbm.at[:, at], conv_w_ref.at[:, at], sems.at[piece]))
    copies.append(pltpu.make_async_copy(gate_w_hbm, gate_w_ref, sems.at[len(blocks)]))
    copies.append(pltpu.make_async_copy(out_w_hbm, out_w_ref, sems.at[len(blocks) + 1]))
    for copy in copies:
        copy.start()
    vectors = [ref[...].reshape(1, width) for ref in (tap_bias_ref, step_bias_ref, skip_ref, gain_ref)]
    stacked_ref[...] = jnp.concatenate(vectors, axis=0)
    masks = [jnp.concatenate([columns(masks_ref, tap)] * (block // LANES), axis=1) for tap in range(kernel)]
    rim = rim_tokens_ref[...].astype(jnp.float32)
    rim = (rim * inverse_rms(rim) * vectors[GAIN]).astype(jnp.bfloat16)
    normed = normed_ref[...]
    both = jnp.concatenate([normed, rim, rim], axis=0)
    proj = jnp.zeros((length, scan_width), jnp.float32)
    for piece, at in enumerate(blocks):
        copies[piece].wait()
        conv_in = dot(both, conv_w_ref[:, at], ((1,), (0,))).astype(jnp.bfloat16)
        conv_ref[:, at] = conv_in[:length]
        wide = conv_in[:length].astype(jnp.float32)
        rim = conv_in[length : length + CHUNKS].astype(jnp.float32)
        rim_ref[:, at] = rim
        total = jnp.broadcast_to(vectors[TAP_BIAS][:, at], (length, block))
        for tap in range(kernel):
            moved = shifted(wide, rim, kernel - 1 - tap)
            total = total + taps_ref[tap : tap + 1, at] * moved * masks[tap]
        out = (total * sigmoid(total)).astype(jnp.bfloat16)
        out_ref[:, at] = out
        proj = proj + dot(out, weight_ref[:, at], ((1,), (1,)))
    proj_ref[...] = jnp.concatenate([proj, jnp.zeros((length, LANES - scan_width), jnp.float32)], axis=1)
    copies[-2].wait()
    for at in blocks:
        gate_ref[:, at] = dot(normed, gate_w_ref[:, at], ((1,), (0,)))
    copies[-1].wait()
    for at in blocks:
        gg_ref[:, at] = dot(cot_ref[...], out_w_ref[at, :], ((1,), (1,)))


def run_enter(normed, rim, cot, vectors, masks, conv_w, gate_w, out_w, taps, weight):
    length, model = normed.shape
    width = conv_w.shape[1]
    f32, bf16 = jnp.float32, jnp.bfloat16
    vmem, hbm = pl.BlockSpec(memory_space=pltpu.VMEM), pl.BlockSpec(memory_space=pl.ANY)
    return pl.pallas_call(
        functools.partial(enter_kernel, taps.shape[0], weight.shape[0]),
        in_specs=[vmem] * 10 + [hbm] * 3, out_specs=[vmem] * 7,
        out_shape=[
            jax.ShapeDtypeStruct((length, width), bf16), jax.ShapeDtypeStruct((CHUNKS, width), f32),
            jax.ShapeDtypeStruct((length, width), bf16), jax.ShapeDtypeStruct((length, width), f32),
            jax.ShapeDtypeStruct((length, width), f32), jax.ShapeDtypeStruct((length, LANES), f32),
            jax.ShapeDtypeStruct((len(vectors), width), f32),
        ],
        scratch_shapes=[
            pltpu.VMEM(conv_w.shape, bf16), pltpu.VMEM(gate_w.shape, bf16), pltpu.VMEM(out_w.shape, bf16),
            pltpu.SemaphoreType.DMA((width // (3 * LANES) + 2,)),
        ],
        compiler_params=params(), cost_estimate=cost(6), name="enter",
    )(normed, rim, cot, *vectors, masks, taps, weight, conv_w, gate_w, out_w)


def early_kernel(members, kernel, tokens_ref, cot_ref, gain_ref, ids_ref, normed_ref, masks_ref, *rest):
    rim_ref, *early_refs, turned_ref, rows_ref = rest
    length, model = tokens_ref.shape
    device = lax.axis_index("seq")
    rows_ref[...] = ids_ref[...].reshape(members, length)
    ids = rows_ref[pl.ds(device, 1), :]
    before = rows_ref[pl.ds(jnp.maximum(device - 1, 0), 1), :]
    before = jnp.where(device > 0, before, -1)
    lane = lax.broadcasted_iota(jnp.int32, ids.shape, 1)
    for tap in range(kernel):
        back = kernel - 1 - tap
        seen = ids
        if back:
            seen = jnp.where(lane < back, pltpu.roll(before, back, 1), pltpu.roll(ids, back, 1))
        masks_ref[tap : tap + 1, :] = jnp.where(ids == seen, 1.0, 0.0)
    rim_ref[...] = tokens_ref[length - CHUNKS :, :]
    tokens = tokens_ref[...].astype(jnp.float32)
    gain = gain_ref[...].reshape(1, model)
    normed_ref[...] = (tokens * inverse_rms(tokens) * gain).astype(jnp.bfloat16)
    for group in range(model // LANES):
        at = slice(group * LANES, (group + 1) * LANES)
        turned_ref[at, :] = normed_ref[:, at].astype(jnp.float32).T
        turned_ref[model + group * LANES : model + (group + 1) * LANES, :] = (
            cot_ref[:, at].astype(jnp.float32).T
        )
    rows, lines = model // members, members // PLANE
    for mask, early_ref in enumerate(early_refs):
        place = jnp.bitwise_xor(device % PLANE, mask)
        for source in range(2):
            pieces = []
            for line in range(lines):
                first = source * model + (line * PLANE + place) * rows
                if rows % 8 == 0:
                    first = pl.multiple_of(first, 8)
                pieces.append(turned_ref[pl.ds(first, rows), :])
            at = slice(source * lines * rows, (source + 1) * lines * rows)
            early_ref[at, :] = jnp.concatenate(pieces, axis=0).astype(jnp.bfloat16)


def run_early(tokens, cot, gain, ids, kernel):
    length, model = tokens.shape
    members = lax.axis_size("seq")
    vmem = pl.BlockSpec(memory_space=pltpu.VMEM)
    early = jax.ShapeDtypeStruct((2 * model // PLANE, length), jnp.bfloat16)
    return pl.pallas_call(
        functools.partial(early_kernel, members, kernel),
        in_specs=[vmem] * 4, out_specs=[vmem] * (3 + PLANE),
        out_shape=[
            jax.ShapeDtypeStruct(tokens.shape, jnp.bfloat16),
            jax.ShapeDtypeStruct((kernel, length), jnp.float32),
            jax.ShapeDtypeStruct((CHUNKS, model), jnp.bfloat16),
        ] + [early] * PLANE,
        scratch_shapes=[
            pltpu.VMEM((2 * model, length), jnp.float32), pltpu.VMEM((members, length), jnp.int32),
        ],
        compiler_params=params(), cost_estimate=cost(3), name="early",
    )(tokens, cot, gain, ids)


def every(width):
    return [(group, slice(group * LANES, (group + 1) * LANES)) for group in range(width // LANES)]


def chunk_sums(long_ref, group, length):
    sums = long_ref[group, strided(0, length), :]
    for place in range(1, length // CHUNKS):
        sums = sums + long_ref[group, strided(place, length), :]
    return sums


def prepare(
    rank, states, own_ref, peer_ref, weight_ref, bias_ref, conv_ref, gg_ref, gate_ref, masks_ref,
    proj_ref, in_ref, out_ref, long_ref, drive_ref, source_ref, true_ref=None,
):
    length, width = conv_ref.shape
    proj_ref[...] = own_ref[...] + peer_ref[...]
    low = proj_ref[:, :rank].astype(jnp.bfloat16)
    step_pre = dot(low, weight_ref[...], ((1,), (0,))) + row(bias_ref, STEP_BIAS)
    spread(proj_ref, rank, in_ref, states, length)
    spread(proj_ref, rank + states, out_ref, states, length)
    same = columns(masks_ref, masks_ref.shape[0] - 2)
    for group, at in every(width):
        step = softplus(step_pre[:, at])
        if true_ref is not None:
            true_ref[group] = step
        long_ref[group] = jnp.where(same > 0.0, step, FAR)
        drive_ref[group] = step * conv_ref[:, at].astype(jnp.float32)
        gate = gate_ref[:, at]
        source_ref[group] = gg_ref[:, at] * gate * sigmoid(gate)
    return step_pre


def ends_kernel(
    rank, states, ndeps,
    own_ref, peer_ref, weight_ref, bias_ref, decay_ref, conv_ref, gg_ref, gate_ref, masks_ref, *rest,
):
    (
        ends_ref, seeds_ref, totals_ref,
        proj_ref, in_ref, out_ref, long_ref, drive_ref, source_ref, end_ref, seed_ref, dec_ref,
    ) = rest[ndeps:]
    length, width = conv_ref.shape
    places = length // CHUNKS
    prepare(
        rank, states, own_ref, peer_ref, weight_ref, bias_ref, conv_ref, gg_ref, gate_ref, masks_ref,
        proj_ref, in_ref, out_ref, long_ref, drive_ref, source_ref,
    )

    @pl.loop(0, width // LANES)
    def _(group):
        rate2 = -jnp.exp(decay_ref[:, group_at(group)]) * LOG2E
        rates = [jnp.broadcast_to(rate2[n : n + 1, :], (CHUNKS, LANES)) for n in range(states)]
        hidden = [None] * states
        for place in range(places):
            long = long_ref[group, strided(place, length), :]
            drive = drive_ref[group, strided(place, length), :]
            for n in range(states):
                term = tile(in_ref, place, n, states) * drive
                decay = jnp.exp2(long * rates[n])
                dec_ref[(place * states + n) * CHUNKS : (place * states + n + 1) * CHUNKS, :] = decay
                hidden[n] = term if place == 0 else decay * hidden[n] + term
        for n in range(states):
            end_ref[group, n * CHUNKS : (n + 1) * CHUNKS, :] = hidden[n]
        back = [None] * states
        for place in reversed(range(places)):
            long = long_ref[group, strided(place, length), :]
            source = source_ref[group, strided(place, length), :]
            for n in range(states):
                term = tile(out_ref, place, n, states) * source
                term = term if place == places - 1 else back[n] + term
                back[n] = tile(dec_ref, place, n, states) * term
        for n in range(states):
            seed_ref[group, n * CHUNKS : (n + 1) * CHUNKS, :] = back[n]

    for group, at in every(width):
        ends_ref[:, at] = end_ref[group]
        seeds_ref[:, at] = seed_ref[group]
        rate2 = -jnp.exp(decay_ref[:, at]) * LOG2E
        sums = chunk_sums(long_ref, group, length)
        decays = [jnp.exp2(rate2 * sums[c : c + 1, :]) for c in range(CHUNKS)]
        end = jnp.zeros((states, LANES), jnp.float32)
        seed = jnp.zeros((states, LANES), jnp.float32)
        for c in range(CHUNKS):
            end = decays[c] * end + end_ref[group, pl.ds(c, states, stride=CHUNKS), :]
        for c in reversed(range(CHUNKS)):
            seed = decays[c] * seed + seed_ref[group, pl.ds(c, states, stride=CHUNKS), :]
        totals_ref[:states, at] = end.astype(jnp.bfloat16)
        totals_ref[states : 2 * states, at] = seed.astype(jnp.bfloat16)
        totals_ref[2 * states :, at] = two_rows(jnp.sum(sums, axis=0, keepdims=True))


def scan_kernel(
    rank, states, members,
    where_ref, own_ref, peer_ref, weight_ref, bias_ref, decay_ref, conv_ref, gg_ref, gate_ref, masks_ref,
    ends_ref, seeds_ref, near_ref, *rest,
):
    stride, radix = levels(members)[-1]
    far_refs = rest[: radix - 1]
    both_ref, small_ref, gconv_ref, gproj_ref = rest[-21:-17]
    (
        proj_ref, in_ref, out_ref, long_ref, true_ref, drive_ref, source_ref,
        start_ref, last_ref, hidden_ref, in_acc, out_acc, scan_ref, gstep_ref, mix_ref, log_ref, dec_ref,
    ) = rest[-17:]
    length, width = conv_ref.shape
    places = length // CHUNKS
    step_pre = prepare(
        rank, states, own_ref, peer_ref, weight_ref, bias_ref, conv_ref, gg_ref, gate_ref, masks_ref,
        proj_ref, in_ref, out_ref, long_ref, drive_ref, source_ref, true_ref,
    )
    in_acc[...] = jnp.zeros_like(in_acc)
    out_acc[...] = jnp.zeros_like(out_acc)
    digit = where_ref[0] // stride % radix
    for group, at in every(width):
        start_ref[group] = ends_ref[:, at]
        last_ref[group] = seeds_ref[:, at]
        rate2 = -jnp.exp(decay_ref[:, at]) * LOG2E
        sums = chunk_sums(long_ref, group, length)
        decays = [jnp.exp2(rate2 * sums[c : c + 1, :]) for c in range(CHUNKS)]
        forward, backward = arrive(
            digit, rate2, near_ref[:, at], [ref[:, at] for ref in far_refs], states
        )
        for c in range(CHUNKS):
            rows = pl.ds(c, states, stride=CHUNKS)
            own = start_ref[group, rows, :]
            start_ref[group, rows, :] = forward
            forward = decays[c] * forward + own
        for c in reversed(range(CHUNKS)):
            rows = pl.ds(c, states, stride=CHUNKS)
            own = last_ref[group, rows, :]
            last_ref[group, rows, :] = backward
            backward = decays[c] * backward + own

    @pl.loop(0, width // LANES)
    def _(group):
        rate2 = -jnp.exp(decay_ref[:, group_at(group)]) * LOG2E
        rates = [jnp.broadcast_to(rate2[n : n + 1, :], (CHUNKS, LANES)) for n in range(states)]
        hidden = [start_ref[group, n * CHUNKS : (n + 1) * CHUNKS, :] for n in range(states)]
        for place in range(places):
            long = long_ref[group, strided(place, length), :]
            drive = drive_ref[group, strided(place, length), :]
            source = source_ref[group, strided(place, length), :]
            rows = slice(place * CHUNKS, (place + 1) * CHUNKS)
            scan = None
            for n in range(states):
                lanes = slice(n * LANES, (n + 1) * LANES)
                decay = jnp.exp2(long * rates[n])
                dec_ref[(place * states + n) * CHUNKS : (place * states + n + 1) * CHUNKS, :] = decay
                value = decay * hidden[n] + tile(in_ref, place, n, states) * drive
                hidden[n] = value
                if place < places - 1:
                    first = (place * states + n) * CHUNKS
                    hidden_ref[first : first + CHUNKS, :] = value
                part = tile(out_ref, place, n, states) * value
                scan = part if n == 0 else scan + part
                out_acc[rows, lanes] += source * value
            scan_ref[group, strided(place, length), :] = scan

        back = [last_ref[group, n * CHUNKS : (n + 1) * CHUNKS, :] for n in range(states)]
        logs = [None] * states
        for place in reversed(range(places)):
            long = long_ref[group, strided(place, length), :]
            true = true_ref[group, strided(place, length), :]
            drive = drive_ref[group, strided(place, length), :]
            source = source_ref[group, strided(place, length), :]
            rows = slice(place * CHUNKS, (place + 1) * CHUNKS)
            gstep = None
            mixed = None
            for n in range(states):
                lanes = slice(n * LANES, (n + 1) * LANES)
                grad = back[n] + tile(out_ref, place, n, states) * source
                previous = (
                    start_ref[group, n * CHUNKS : (n + 1) * CHUNKS, :] if place == 0
                    else tile(hidden_ref, place - 1, n, states)
                )
                back[n] = tile(dec_ref, place, n, states) * grad
                log = back[n] * previous
                part = log * true
                logs[n] = part if logs[n] is None else logs[n] + part
                part = log * rates[n]
                gstep = part if n == 0 else gstep + part
                part = grad * tile(in_ref, place, n, states)
                mixed = part if n == 0 else mixed + part
                in_acc[rows, lanes] += grad * drive
            gstep_ref[group, strided(place, length), :] = gstep
            mix_ref[group, strided(place, length), :] = mixed
        for n in range(states):
            log_ref[group, n * CHUNKS : (n + 1) * CHUNKS, :] = logs[n]

    low = proj_ref[...].astype(jnp.bfloat16)
    small_ref[rank + states + 2 :, :] = jnp.zeros((small_ref.shape[0] - rank - states - 2, width), jnp.float32)
    grad_low = jnp.zeros((length, rank), jnp.float32)
    for group, at in every(width):
        conv = conv_ref[:, at].astype(jnp.float32)
        gate, gg = gate_ref[:, at], gg_ref[:, at]
        source, step, mix = source_ref[group], true_ref[group], mix_ref[group]
        sigma = sigmoid(gate)
        skip = bias_ref[SKIP : SKIP + 1, at]
        scan_out = scan_ref[group] + skip * conv
        both_ref[:length, at] = (scan_out * gate * sigma).astype(jnp.bfloat16)
        ggate = gg * scan_out * sigma * (1.0 + gate * (1.0 - sigma))
        both_ref[length:, at] = ggate.astype(jnp.bfloat16)
        gconv_ref[:, at] = source * skip + mix * step
        gpre = (gstep_ref[group] * LN2 + mix * conv) * sigmoid(step_pre[:, at])
        gpre_low = gpre.astype(jnp.bfloat16)
        grad_low = grad_low + dot(gpre_low, weight_ref[:, at], ((1,), (1,)))
        small_ref[:rank, at] = dot(low, gpre_low, ((0,), (0,)))[:rank]
        decay = -jnp.exp(decay_ref[:, at])
        logs = log_ref[group, pl.ds(0, states, stride=CHUNKS), :]
        for c in range(1, CHUNKS):
            logs = logs + log_ref[group, pl.ds(c, states, stride=CHUNKS), :]
        first = rank + states
        small_ref[rank:first, at] = logs * decay
        small_ref[first : first + 1, at] = jnp.sum(gpre, axis=0, keepdims=True)
        small_ref[first + 1 : first + 2, at] = jnp.sum(source * conv, axis=0, keepdims=True)

    wide = states * LANES
    source_state = lax.broadcasted_iota(jnp.int32, (wide, LANES), 0) // LANES
    column = lax.broadcasted_iota(jnp.int32, (wide, LANES), 1)
    total = jnp.zeros((length, LANES), jnp.float32)
    for acc, first in ((in_acc, rank), (out_acc, rank + states)):
        pick = jnp.where(source_state + first == column, 1.0, 0.0).astype(jnp.bfloat16)
        value = acc[...]
        high = value.astype(jnp.bfloat16)
        rest = (value - high.astype(jnp.float32)).astype(jnp.bfloat16)
        total = total + dot(high, pick, ((1,), (0,))) + dot(rest, pick, ((1,), (0,)))
    scan_ref[0] = total
    for place in range(places):
        mix_ref[0, strided(place, length), :] = scan_ref[0, place * CHUNKS : (place + 1) * CHUNKS, :]
    gproj_ref[...] = mix_ref[0]
    gproj_ref[:, :rank] += grad_low


def column_block(rows, width=LANES):
    return pl.BlockSpec((rows, width), lambda g: (0, g))


def whole(*shape):
    return pl.BlockSpec(shape, lambda g: (0,) * len(shape))


def run_ends(own, peer, weight, stacked, decay_log, conv, gg, gate, masks, deps=()):
    length, width = conv.shape
    rank, states = weight.shape[0], decay_log.shape[0]
    tall = length // CHUNKS * states * CHUNKS
    f32 = jnp.float32
    vmem = pl.BlockSpec(memory_space=pltpu.VMEM)
    return pl.pallas_call(
        functools.partial(ends_kernel, rank, states, len(deps)),
        in_specs=[vmem] * 9 + [pl.BlockSpec(memory_space=pl.ANY) for _ in deps], out_specs=[vmem] * 3,
        out_shape=[
            jax.ShapeDtypeStruct((states * CHUNKS, width), f32),
            jax.ShapeDtypeStruct((states * CHUNKS, width), f32),
            jax.ShapeDtypeStruct((2 * states + 2 * CHUNKS, width), jnp.bfloat16),
        ],
        scratch_shapes=[pltpu.VMEM((length, LANES), f32)]
        + [pltpu.VMEM((tall, LANES), f32)] * 2 + [pltpu.VMEM((width // LANES, length, LANES), f32)] * 3
        + [pltpu.VMEM((width // LANES, states * CHUNKS, LANES), f32)] * 2
        + [pltpu.VMEM((tall, LANES), f32)],
        compiler_params=params(), cost_estimate=cost(8), name="ends",
    )(own, peer, weight, stacked, decay_log, conv, gg, gate, masks, *deps)


def run_scan(where, own, peer, weight, stacked, decay_log, conv, gg, gate, masks, ends, seeds, near, far, deps):
    length, width = conv.shape
    members = lax.axis_size("seq")
    rank, states = weight.shape[0], decay_log.shape[0]
    places = length // CHUNKS
    tall = places * states * CHUNKS
    f32, bf16 = jnp.float32, jnp.bfloat16
    groups = pltpu.VMEM((width // LANES, length, LANES), f32)
    chunks = pltpu.VMEM((width // LANES, states * CHUNKS, LANES), f32)
    table = pltpu.VMEM((tall, LANES), f32)
    vmem = pl.BlockSpec(memory_space=pltpu.VMEM)
    return pl.pallas_call(
        functools.partial(scan_kernel, rank, states, members),
        in_specs=[pl.BlockSpec(memory_space=pltpu.SMEM)] + [vmem] * (12 + len(far))
        + [pl.BlockSpec(memory_space=pl.ANY) for _ in deps],
        out_specs=[vmem] * 4,
        out_shape=[
            jax.ShapeDtypeStruct((2 * length, width), bf16),
            jax.ShapeDtypeStruct((padded(rank + states + 2, 8), width), f32),
            jax.ShapeDtypeStruct((length, width), f32),
            jax.ShapeDtypeStruct((length, LANES), f32),
        ],
        scratch_shapes=[pltpu.VMEM((length, LANES), f32), table, table] + [groups] * 4 + [chunks] * 2
        + [table] + [pltpu.VMEM((length, states * LANES), f32)] * 2 + [groups] * 3 + [chunks, table],
        compiler_params=params(), cost_estimate=cost(15), name="scan",
    )(where, own, peer, weight, stacked, decay_log, conv, gg, gate, masks, ends, seeds, near, *far, *deps)


def levels(members):
    found, stride = [], 1
    while stride < members:
        radix = 4 if members // stride % 4 == 0 else 2
        found.append((stride, radix))
        stride *= radix
    return found


def chosen(refs, own, hop):
    value = own
    for mask, ref in enumerate(refs, 1):
        value = jnp.where(hop == mask, ref.astype(jnp.float32), value)
    return value


def arrive(digit, rate2, near, far, states):
    radix = len(far) + 1
    carry = jnp.zeros_like(rate2)
    incoming = jnp.zeros_like(rate2)
    blank = jnp.zeros(far[0].shape, jnp.float32)
    for number in range(radix):
        value = chosen(far, blank, digit ^ number)
        decay = jnp.exp2(rate2 * (value[states : states + 1] + value[states + 1 : states + 2]))
        carry = jnp.where(number < digit, decay * carry + value[:states], carry)
    for number in reversed(range(radix)):
        value = chosen(far, blank, digit ^ number)
        decay = jnp.exp2(rate2 * (value[states : states + 1] + value[states + 1 : states + 2]))
        incoming = jnp.where(number > digit, decay * incoming + value[:states], incoming)
    before, behind = near[2 * states : 2 * states + 1], near[2 * states + 1 : 2 * states + 2]
    carry = near[:states] + jnp.exp2(rate2 * before) * carry
    incoming = near[states : 2 * states] + jnp.exp2(rate2 * behind) * incoming
    return carry, incoming


def fold_kernel(states, level, members, start, ndeps, where_ref, decay_ref, *refs):
    stride, radix = levels(members)[level]
    next_stride, next_radix = levels(members)[level + 1]
    last = level + 2 == len(levels(members))
    digit = where_ref[0] // stride % radix
    if not start:
        old = refs[0][...]
        refs = refs[1:]
    own = refs[0][...]
    got = [ref[...] for ref in refs[1:radix]]
    near_ref, *outs = refs[radix + ndeps :]
    rate2 = -jnp.exp(decay_ref[...]) * LOG2E
    own = own.astype(jnp.float32)
    values = [chosen(got, own, digit ^ number) for number in range(radix)]
    first = 2 * states
    sums = [value[first : first + 1] + value[first + 1 : first + 2] for value in values]
    decays = [jnp.exp2(rate2 * one) for one in sums]
    zero, line = jnp.zeros_like(rate2), jnp.zeros_like(sums[0])
    end, seed, carry, incoming, before, behind, total = zero, zero, zero, zero, line, line, line
    for number in range(radix):
        part = values[number][:states]
        end = decays[number] * end + part
        carry = jnp.where(number < digit, decays[number] * carry + part, carry)
        before = jnp.where(number < digit, before + sums[number], before)
        total = total + sums[number]
    for number in reversed(range(radix)):
        part = values[number][states : 2 * states]
        seed = decays[number] * seed + part
        incoming = jnp.where(number > digit, decays[number] * incoming + part, incoming)
        behind = jnp.where(number > digit, behind + sums[number], behind)
    if not start:
        old_before, old_behind = old[2 * states : 2 * states + 1], old[2 * states + 1 : 2 * states + 2]
        carry = old[:states] + jnp.exp2(rate2 * old_before) * carry
        incoming = old[states : 2 * states] + jnp.exp2(rate2 * old_behind) * incoming
        before, behind = before + old_before, behind + old_behind
    pad = jnp.zeros((6, line.shape[1]), jnp.float32)
    near_ref[...] = jnp.concatenate([carry, incoming, before, behind, pad], axis=0)
    tail = two_rows(total)
    if last:
        next_digit = where_ref[0] // next_stride % next_radix
        for mask, out in enumerate(outs, 1):
            value = jnp.where(next_digit < (next_digit ^ mask), end, seed)
            out[:states, :] = value.astype(jnp.bfloat16)
            out[states:, :] = tail
    else:
        outs[0][: 2 * states, :] = jnp.concatenate([end, seed], axis=0).astype(jnp.bfloat16)
        outs[0][2 * states :, :] = tail


def run_fold(level, where, decay_log, near, parts, deps):
    states, width = decay_log.shape
    members = lax.axis_size("seq")
    f32, bf16 = jnp.float32, jnp.bfloat16
    vmem = pl.BlockSpec(memory_space=pltpu.VMEM)
    tall = jax.ShapeDtypeStruct((2 * states + 8, width), f32)
    if level + 2 == len(levels(members)):
        sent = [jax.ShapeDtypeStruct((states + 2 * CHUNKS, width), bf16)] * (levels(members)[-1][1] - 1)
    else:
        sent = [jax.ShapeDtypeStruct((2 * states + 2 * CHUNKS, width), bf16)]
    extra = [] if near is None else [near]
    return pl.pallas_call(
        functools.partial(fold_kernel, states, level, members, near is None, len(deps)),
        in_specs=[pl.BlockSpec(memory_space=pltpu.SMEM)] + [vmem] * (1 + len(extra) + len(parts))
        + [pl.BlockSpec(memory_space=pl.ANY) for _ in deps],
        out_specs=[vmem] * (1 + len(sent)),
        out_shape=[tall] + sent,
        compiler_params=params(), cost_estimate=cost(2), name="fold",
    )(where, decay_log, *extra, *parts, *deps)


def exchange(where, totals, decay_log, deps):
    members = lax.axis_size("seq")
    found = levels(members)
    near = None
    for level, (stride, radix) in enumerate(found[:-1]):
        parts = [totals] + [hop(totals, mask * stride) for mask in range(1, radix)]
        near, *sent = run_fold(level, where, decay_log, near, parts, deps)
        totals = sent[0]
    stride, radix = found[-1]
    return near, [hop(one, mask * stride) for mask, one in enumerate(sent, 1)]


def taps_kernel(
    kernel,
    where_ref, own_ref, peer_ref, conv_ref, in_ref, ext_ref, weight_ref, gconv_ref, taps_ref, params_ref, masks_ref,
    first_small_ref, main_ref, rim_ref, kept_ref, *rest,
):
    *sent_refs, small_ref, quarter_ref = rest
    length, total_width = conv_ref.shape
    width = weight_ref.shape[0]
    grad_proj = (own_ref[...] + peer_ref[...]).astype(jnp.bfloat16)
    masks = [columns(masks_ref, tap) for tap in range(kernel)]
    near_row = lax.broadcasted_iota(jnp.int32, (CHUNKS, LANES), 0)
    token = lax.broadcasted_iota(jnp.int32, (length, LANES), 0)
    for group in range(total_width // LANES):
        at = slice(group * LANES, (group + 1) * LANES)
        taps = [taps_ref[tap : tap + 1, at] for tap in range(kernel)]
        conv_in = in_ref[:, at].astype(jnp.float32)
        ext = ext_ref[:, at]
        seen = [shifted(conv_in, ext, kernel - 1 - tap) * masks[tap] for tap in range(kernel)]
        pre = jnp.broadcast_to(params_ref[TAP_BIAS : TAP_BIAS + 1, at], (length, LANES))
        for tap in range(kernel):
            pre = pre + taps[tap] * seen[tap]
        small_ref[:width, at] = dot(grad_proj, conv_ref[:, at], ((0,), (0,)))[:width]
        grad = gconv_ref[:, at] + dot(grad_proj[:, :width], weight_ref[:, at], ((1,), (0,)))
        grad = grad * silu_grad(pre)
        lines = []
        main = jnp.zeros((length, LANES), jnp.float32)
        rim = jnp.zeros((CHUNKS, LANES), jnp.float32)
        for tap in range(kernel):
            back = kernel - 1 - tap
            lines.append(jnp.sum(grad * seen[tap], axis=0, keepdims=True))
            masked = grad * masks[tap] * taps[tap]
            if back == 0:
                main = main + masked
            else:
                moved = pltpu.roll(masked, length - back, 0)
                main = main + jnp.where(token < length - back, moved, 0.0)
                rim = rim + jnp.where(
                    near_row >= CHUNKS - back, pltpu.roll(masked[:CHUNKS], CHUNKS - back, 0), 0.0
                )
        main_ref[:, at] = main
        rim_ref[:, at] = rim
        lines.append(jnp.sum(grad, axis=0, keepdims=True))
        lines.append(jnp.zeros((small_ref.shape[0] - width - kernel - 1, LANES), jnp.float32))
        small_ref[width:, at] = jnp.concatenate(lines, axis=0)
    small = jnp.concatenate([first_small_ref[...], small_ref[...]], axis=0)
    count, rows = kept_ref.shape[0], small.shape[0] // PLANE
    for quarter in range(PLANE):
        quarter_ref[quarter, :rows, :] = small[quarter * rows : (quarter + 1) * rows]
        quarter_ref[quarter, rows:, :] = jnp.zeros((count - rows, total_width), jnp.float32)
    place = where_ref[0] % PLANE
    kept_ref[...] = quarter_ref[place]
    for mask, sent_ref in enumerate(sent_refs, 1):
        sent_ref[...] = quarter_ref[jnp.bitwise_xor(place, mask)].astype(jnp.bfloat16)


def run_taps(where, own, peer, conv, conv_in, ext, weight, gconv, taps, stacked, masks, first_small):
    length, width = conv.shape
    kernel = taps.shape[0]
    f32 = jnp.float32
    vmem = pl.BlockSpec(memory_space=pltpu.VMEM)
    tall = padded(weight.shape[0] + kernel + 1, 8)
    count = padded((first_small.shape[0] + tall) // PLANE, 8)
    return pl.pallas_call(
        functools.partial(taps_kernel, kernel),
        in_specs=[pl.BlockSpec(memory_space=pltpu.SMEM)] + [vmem] * 11, out_specs=[vmem] * (2 + PLANE),
        out_shape=[
            jax.ShapeDtypeStruct((length, width), f32), jax.ShapeDtypeStruct((CHUNKS, width), f32),
            jax.ShapeDtypeStruct((count, width), f32),
        ] + [jax.ShapeDtypeStruct((count, width), jnp.bfloat16)] * (PLANE - 1),
        scratch_shapes=[pltpu.VMEM((tall, width), f32), pltpu.VMEM((PLANE, count, width), f32)],
        compiler_params=params(), cost_estimate=cost(4), name="taps",
    )(where, own, peer, conv, conv_in, ext, weight, gconv, taps, stacked, masks, first_small)


def inputs_kernel(ndeps, main_ref, rim_ref, weight_ref, both_ref, gate_weight_ref, tokens_ref, *rest):
    low_ref, normed_ref = rest[ndeps:]
    length, width = main_ref.shape
    main = main_ref[...]
    low = jnp.concatenate(
        [main[: length - CHUNKS], main[length - CHUNKS :] + rim_ref[...]], axis=0
    ).astype(jnp.bfloat16)
    normed = dot(both_ref[length:, :], gate_weight_ref[...], ((1,), (1,)))
    normed = normed + dot(low, weight_ref[...], ((1,), (1,)))
    normed_ref[...] = normed
    tokens = tokens_ref[...].astype(jnp.float32)
    gain = jnp.sum(normed * tokens * inverse_rms(tokens), axis=0, keepdims=True)
    low_ref[:length, :] = low
    low_ref[length:, :] = two_rows(gain)


def run_inputs(main, rim, weight, both, gate_weight, tokens, deps):
    length, width = main.shape
    vmem = pl.BlockSpec(memory_space=pltpu.VMEM)
    return pl.pallas_call(
        functools.partial(inputs_kernel, len(deps)),
        in_specs=[vmem] * 6 + [pl.BlockSpec(memory_space=pl.ANY) for _ in deps], out_specs=[vmem] * 2,
        out_shape=[
            jax.ShapeDtypeStruct((length + 2 * CHUNKS, width), jnp.bfloat16),
            jax.ShapeDtypeStruct((length, weight.shape[0]), jnp.float32),
        ],
        compiler_params=params(), cost_estimate=cost(3), name="inputs",
    )(main, rim, weight, both, gate_weight, tokens, *deps)


def products_kernel(halves, members, ndeps, where_ref, *rest):
    early, rest = rest[:PLANE], rest[PLANE:]
    late, rest = list(rest[: 2 + len(halves) + 1]), rest[2 + len(halves) + 1 :]
    lines = members // PLANE
    share, length = early[0].shape[0] // 2, early[0].shape[1]
    rows = share // lines
    apart = late[0].shape[0] == len(halves) * length
    if apart:
        small, rest = rest[:PLANE], rest[PLANE:]
    kept_ref, small_ref, sent_ref, total_ref = rest[ndeps:]
    for number, half in enumerate(halves):
        total = None
        for mask in range(PLANE):
            if mask == 3 and len(halves) > 1:
                block = late[mask + number][...]
            else:
                block = late[mask][number * length : (number + 1) * length, :]
            part = dot(early[mask][half * share : (half + 1) * share, :], block, ((1,), (0,)))
            total = part if total is None else total + part
        for line in range(lines):
            total_ref[line, number * rows : (number + 1) * rows, :] = total[line * rows : (line + 1) * rows]
    if apart:
        line = small[0][...]
        for ref in small[1:]:
            line = line + ref[...].astype(jnp.float32)
    else:
        line = sum(
            jnp.sum(ref[len(halves) * length :, :].astype(jnp.float32), axis=0, keepdims=True) for ref in late
        )
        number = lax.broadcasted_iota(jnp.int32, small_ref.shape, 0)
        line = jnp.where(number == 0, line, 0.0)
    send(where_ref[0], 0, total_ref, line, kept_ref, small_ref, sent_ref)


def send(device, level, total_ref, line, kept_ref, small_ref, sent_ref):
    digit = device // (PLANE << level) % 2
    small_ref[...] = line
    pieces = [line]
    for block in range(total_ref.shape[0] // 2):
        kept_ref[block] = total_ref[2 * block + digit]
        pieces.append(total_ref[2 * block + 1 - digit])
    sent_ref[...] = jnp.concatenate(pieces, axis=0).astype(jnp.bfloat16)


def gather_kernel(level, count, ndeps, where_ref, kept_ref, small_ref, got_ref, *refs):
    refs = refs[ndeps:]
    total = kept_ref[...]
    got = got_ref[...].astype(jnp.float32)
    first = small_ref.shape[0]
    line = small_ref[...] + got[:first]
    left, rows, width = total.shape
    pieces = [total[index] + got[first + index * rows : first + (index + 1) * rows] for index in range(left)]
    if left > 1:
        total_ref = refs[-1]
        for index, piece in enumerate(pieces):
            total_ref[index] = piece
        send(where_ref[0], level + 1, total_ref, line, *refs[:-1])
        return
    for index in range(count):
        refs[index][...] = pieces[0][index * (rows // count) : (index + 1) * (rows // count)]
    if len(refs[count].shape) == 1:
        refs[count][...] = line[:1].reshape(width)
    else:
        refs[count][...] = line.astype(refs[count].dtype)


def multiply(halves, where, early, late, small, deps):
    members = lax.axis_size("seq")
    lines = members // PLANE
    width = late[0].shape[1]
    rows = len(halves) * (early[0].shape[0] // 2 // lines)
    vmem = pl.BlockSpec(memory_space=pltpu.VMEM)
    count = small[0].shape[0] if small else 2 * CHUNKS
    out_shape = level_shapes(lines, rows, count, width)
    return pl.pallas_call(
        functools.partial(products_kernel, halves, members, len(deps)),
        in_specs=[pl.BlockSpec(memory_space=pltpu.SMEM)] + [vmem] * (PLANE + len(late) + len(small))
        + [pl.BlockSpec(memory_space=pl.ANY) for _ in deps],
        out_specs=[vmem] * len(out_shape), out_shape=out_shape,
        scratch_shapes=[pltpu.VMEM((lines, rows, width), jnp.float32)],
        compiler_params=params(), cost_estimate=cost(4), name="products",
    )(where, *early, *late, *small, *deps)


def level_shapes(left, rows, count, width):
    return [
        jax.ShapeDtypeStruct((left // 2, rows, width), jnp.float32),
        jax.ShapeDtypeStruct((count, width), jnp.float32),
        jax.ShapeDtypeStruct((count + left // 2 * rows, width), jnp.bfloat16),
    ]


def add_line(level, where, parts, number, deps=()):
    f32 = jnp.float32
    kept, small, sent = parts
    vmem = pl.BlockSpec(memory_space=pltpu.VMEM)
    got = hop(sent, PLANE << level)
    left, rows, width = kept.shape
    count = small.shape[0]
    scratch = []
    if left > 1:
        out_shape = level_shapes(left, rows, count, width)
        scratch = [pltpu.VMEM((left, rows, width), f32)]
    else:
        out_shape = [jax.ShapeDtypeStruct((rows // number, width), f32)] * number
        single = count == 2 * CHUNKS
        out_shape.append(
            jax.ShapeDtypeStruct((width,), f32) if single else jax.ShapeDtypeStruct(small.shape, jnp.bfloat16)
        )
    return pl.pallas_call(
        functools.partial(gather_kernel, level, number, len(deps)),
        in_specs=[pl.BlockSpec(memory_space=pltpu.SMEM)] + [vmem] * 3
        + [pl.BlockSpec(memory_space=pl.ANY) for _ in deps],
        out_specs=[vmem] * len(out_shape), out_shape=out_shape, scratch_shapes=scratch,
        compiler_params=params(), cost_estimate=cost(2), name="gather",
    )(where, kept, small, got, *deps)


def branch_kernel(both_ref, weight_ref, _, branch_ref):
    branch_ref[...] = dot(both_ref[: branch_ref.shape[0], :], weight_ref[...], ((1,), (0,)))


def run_branch(both, weight, dep):
    vmem = pl.BlockSpec(memory_space=pltpu.VMEM)
    return pl.pallas_call(
        branch_kernel, in_specs=[vmem, vmem, pl.BlockSpec(memory_space=pl.ANY)], out_specs=vmem,
        out_shape=jax.ShapeDtypeStruct((both.shape[0] // 2, weight.shape[1]), jnp.float32),
        compiler_params=params(), cost_estimate=cost(5), name="branch",
    )(both, weight, dep)


def place_kernel(rows, counts, where_ref, *refs):
    quarters, outs, (table_ref,) = refs[:PLANE], refs[PLANE:-1], refs[-1:]
    place = where_ref[0] % PLANE
    for mask, ref in enumerate(quarters):
        table_ref[jnp.bitwise_xor(place, mask)] = ref[...].astype(jnp.float32)
    table = jnp.concatenate([table_ref[quarter, :rows, :] for quarter in range(PLANE)], axis=0)
    for out, (first, count) in zip(outs, counts, strict=True):
        value = table[first : first + count]
        out[...] = value.reshape(value.shape[1]) if count == 1 else value


def run_place(where, own, rows, counts):
    count, width = own.shape
    f32 = jnp.float32
    vmem = pl.BlockSpec(memory_space=pltpu.VMEM)
    shapes = [(width,) if number == 1 else (number, width) for _, number in counts]
    return pl.pallas_call(
        functools.partial(place_kernel, rows, counts),
        in_specs=[pl.BlockSpec(memory_space=pltpu.SMEM)] + [vmem] * PLANE,
        out_specs=[vmem] * len(shapes),
        out_shape=[jax.ShapeDtypeStruct(shape, f32) for shape in shapes],
        scratch_shapes=[pltpu.VMEM((PLANE, count, width), f32)],
        compiler_params=params(), cost_estimate=cost(3), name="place",
    )(where, own, hop(own, 1), hop(own, 2), hop(own, 3))


def relay_kernel(x_ref, y_ref, *rest):
    from_x_ref, from_y_ref = rest[-2:]
    length = from_x_ref.shape[0]
    from_x_ref[...] = x_ref[:length, :]
    from_y_ref[...] = y_ref[length:, :]


def run_relay(x, y, deps):
    vmem = pl.BlockSpec(memory_space=pltpu.VMEM)
    half = jax.ShapeDtypeStruct((x.shape[0] // 2, x.shape[1]), x.dtype)
    return pl.pallas_call(
        relay_kernel, in_specs=[vmem, vmem] + [pl.BlockSpec(memory_space=pl.ANY) for _ in deps],
        out_specs=[vmem] * 2,
        out_shape=[half, half], compiler_params=params(), cost_estimate=cost(1), name="relay",
    )(x, y, *deps)


def leave_kernel(tokens_ref, cot_ref, params_ref, branch_ref, branch_peer_ref, own_ref, peer_ref, mixed_ref, grad_ref):
    tokens = tokens_ref[...].astype(jnp.float32)
    mixed_ref[...] = (tokens + (branch_ref[...] + branch_peer_ref[...])).astype(jnp.bfloat16)
    scale = inverse_rms(tokens)
    scaled = (own_ref[...] + peer_ref[...]) * row(params_ref, GAIN)
    mean = jnp.mean(scaled * tokens, axis=1, keepdims=True)
    grad = cot_ref[...].astype(jnp.float32) + scale * scaled
    grad_ref[...] = grad - tokens * (scale * scale * scale * mean)


def run_leave(tokens, cot, stacked, branch, branch_peer, own, peer):
    vmem = pl.BlockSpec(memory_space=pltpu.VMEM)
    return pl.pallas_call(
        leave_kernel, in_specs=[vmem] * 7, out_specs=[vmem] * 2,
        out_shape=[
            jax.ShapeDtypeStruct(tokens.shape, jnp.bfloat16),
            jax.ShapeDtypeStruct(tokens.shape, jnp.float32),
        ],
        compiler_params=params(), cost_estimate=cost(3), name="leave",
    )(tokens, cot, stacked, branch, branch_peer, own, peer)


def from_behind(block, axis, distance):
    devices = range(lax.axis_size(axis))
    route = [(i - distance, i) for i in devices if i - distance in devices]
    return lax.ppermute(block, axis, route)


def swap(block):
    return lax.ppermute(block, "tp", [(0, 1), (1, 0)])


def hop(block, mask):
    members = lax.axis_size("seq")
    return lax.ppermute(block, "seq", [(i, i ^ mask) for i in range(members)])


def shards(
    tokens, norm_gain, in_conv_weight, in_gate_weight, conv_weight, conv_bias, scan_proj_weight,
    step_proj_weight, step_bias, decay_log, skip_gain, out_weight, segment_ids, cotangent,
):
    f32 = jnp.float32
    length, model = tokens.shape
    rank = step_proj_weight.shape[0]
    states = decay_log.shape[0]
    kernel = conv_weight.shape[0]
    width = conv_weight.shape[1]
    members = lax.axis_size("seq")
    device = lax.axis_index("seq")
    where = jnp.stack([device, lax.axis_index("tp")]).astype(jnp.int32)
    scan_width = rank + 2 * states
    scan_weight = scan_proj_weight.T

    normed, masks, rim_tokens, kept_early, *sent_early = run_early(
        tokens, cotangent, norm_gain, segment_ids, kernel
    )
    rim_tokens = from_behind(rim_tokens, "seq", 1)
    early = [kept_early] + [hop(one, mask) for mask, one in enumerate(sent_early, 1)]
    conv_in, ext, conv_out, gate_in, grad_gated, own, stacked = run_enter(
        normed, rim_tokens, cotangent, (conv_bias, step_bias, skip_gain, norm_gain), masks,
        in_conv_weight, in_gate_weight, out_weight, conv_weight, scan_weight,
    )
    peer = swap(own)
    ends, seeds, totals = run_ends(
        own, peer, step_proj_weight, stacked, decay_log, conv_out, grad_gated, gate_in, masks
    )
    near, far = exchange(where, totals, decay_log, early[1:])
    both, first_small, grad_conv, low_own = run_scan(
        where, own, peer, step_proj_weight, stacked, decay_log, conv_out, grad_gated, gate_in, masks,
        ends, seeds, near, far, (),
    )
    low_peer = swap(low_own)
    main, rim, *small = run_taps(
        where, low_own, low_peer, conv_out, conv_in, ext, scan_weight, grad_conv, conv_weight, stacked,
        masks, first_small,
    )
    rim = from_behind(rim, "seq", -1)
    small = small[:1] + [hop(one, mask) for mask, one in enumerate(small[1:], 1)]
    x, y = hop(both, 1), hop(both, 2)
    from_x, from_y = run_relay(x, y, (main, rim, *small[1:3]))
    low, normed_own = run_inputs(
        main, rim, in_conv_weight, both, in_gate_weight, tokens, (from_x,)
    )
    first_late = [both, x, y, hop(from_x, 2), hop(from_y, 1)]
    second_late = [low] + [hop(low, mask) for mask in range(1, PLANE)]
    branch_own = run_branch(both, out_weight, normed_own)
    mixed_out, input_grad = run_leave(
        tokens, cotangent, stacked, branch_own, swap(branch_own), normed_own, swap(normed_own)
    )
    count = (members // PLANE).bit_length() - 1
    first = multiply((1, 0), where, early, first_late, small, (normed_own,))
    first = add_line(0, where, first, 2)
    second = multiply((0,), where, early, second_late, [], (first[0], input_grad))
    for level in range(1, count):
        first = add_line(level, where, first, 2)
    out_grad, in_gate_grad, small = first
    second = add_line(0, where, second, 1, (out_grad,))
    first_row = first_small.shape[0]
    last_row = first_row + scan_width
    (
        step_proj_grad, decay_log_grad, step_bias_grad, skip_grad, scan_proj_grad, conv_weight_grad,
        conv_bias_grad,
    ) = run_place(
        where, small, (first_row + padded(scan_width + kernel + 1, 8)) // PLANE,
        (
            (0, rank), (rank, states), (rank + states, 1), (rank + states + 1, 1), (first_row, scan_width),
            (last_row, kernel), (last_row + kernel, 1),
        ),
    )
    for level in range(1, count):
        second = add_line(level, where, second, 1)
    in_conv_grad, gain_grad = second
    gain_grad = gain_grad + swap(gain_grad)
    return (
        mixed_out, input_grad, gain_grad, in_conv_grad, in_gate_grad, conv_weight_grad,
        conv_bias_grad, scan_proj_grad.T, step_proj_grad, step_bias_grad, decay_log_grad, skip_grad,
        out_grad.T,
    )


def solution(mesh):
    in_specs = (
        P("seq", None), P(), P(None, "tp"), P(None, "tp"), P(None, "tp"), P("tp"), P("tp", None),
        P(None, "tp"), P("tp"), P(None, "tp"), P("tp"), P("tp", None), P(), P("seq", None),
    )
    out_specs = (
        P("seq", None), P("seq", None), P(), P("seq", "tp"), P("seq", "tp"), P(None, "tp"), P("tp"),
        P("tp", None), P(None, "tp"), P("tp"), P(None, "tp"), P("tp"), P("tp", "seq"),
    )
    return jax.shard_map(shards, mesh=mesh, in_specs=in_specs, out_specs=out_specs, check_vma=False)
```
